32 devices in a mesh: dp: 8 (over y, x, core), ctx: 4 (over z).
Axes of the slice: x: 2, y: 2, z: 4, core: 2. Of those that a mesh axis runs over, the one named last changes fastest.
Arguments:
- keys_a: bfloat16 [8, 512, 2560], P('dp', 'ctx'), may hold values from -6 to 6
- values_a: bfloat16 [8, 512, 2560], P('dp', 'ctx'), may hold values from -6 to 6
- queries_b: bfloat16 [8, 512, 2560], P('dp', 'ctx'), may hold values from -6 to 6
- grad_out: bfloat16 [8, 512, 2560], P('dp', 'ctx'), may hold values from -1.5 to 1.5
- state_start: float32 [3, 20, 128, 128], P(None, None, 'ctx'), may hold values from -0.5 to 0.5
- state_next: float32 [8, 3, 20, 128, 128], P('dp', None, None, 'ctx'), may hold values from -0.5 to 0.5
Outputs:
- grad_keys: bfloat16 [8, 512, 2560], P('dp', 'ctx')
- grad_values: bfloat16 [8, 512, 2560], P('dp', 'ctx')
- grad_state: float32 [3, 20, 128, 128], P(None, None, 'ctx')
The draws below stay inside these ranges and needn't reach their ends.
All inputs are finite; a program needn't handle non-finite values.
Results may differ from the reference program's by a relative error of at most 0.033.
Values may be sent and summed in bfloat16 or wider, within the bound.
No kernel may reach another device: no remote copies, remote signals or barrier semaphores. Data moves between devices by JAX's collectives and lax.ppermute only.
A program may use at most 128 MiB of HBM per device.

```python
import jax
import jax.numpy as jnp
from jax import lax

D = 128
H = 20
F = 128
NS_STEPS = 2
TOK = 128
CLIPS = 8
GROUP = 512
N_DP = 8
N_CTX = 4


def steps_of(rng, dims, pieces, low, top_value):
    def one(axis_at, parts):
        heights = jax.random.uniform(jax.random.fold_in(jax.random.fold_in(rng, 6), axis_at), (parts,), jnp.float32, low / len(pieces), top_value / len(pieces))
        return jnp.repeat(jnp.exp(heights), dims[axis_at] // parts).reshape((-1,) + (1,) * (len(dims) - axis_at - 1))

    factor_of = one(*pieces[0])
    for cut in pieces[1:]:
        factor_of = factor_of * one(*cut)
    return factor_of


def bell_draw(rng, extent, width, limit, shards=(), held_as=jnp.bfloat16):
    drawn = width * jax.random.normal(rng, extent, jnp.float32)
    if shards:
        drawn = drawn * steps_of(rng, extent, shards, -0.22, 0.18)
    return jnp.clip(drawn, -limit, limit).astype(held_as)


def setup_inputs(seed: int = 0) -> dict:
    key_list = jax.random.split(jax.random.key(seed), 7)
    keys_a = bell_draw(key_list[0], (CLIPS, GROUP, H * D), 1.0, 6.0, ((0, 8), (1, 4)))
    values_a = bell_draw(key_list[1], (CLIPS, GROUP, H * D), 1.0, 6.0, ((0, 8), (1, 4)))
    queries_b = bell_draw(key_list[2], (CLIPS, GROUP, H * D), 1.0, 6.0, ((0, 8), (1, 4)))
    grad_out = bell_draw(key_list[3], (CLIPS, GROUP, H * D), 0.25, 1.5, ((0, 8), (1, 4)))
    state_start = bell_draw(key_list[4], (3, H, D, F), D ** -0.5, 0.5, ((2, 4),), jnp.float32)
    state_next = bell_draw(key_list[5], (CLIPS, 3, H, D, F), D ** -0.5, 0.5, ((0, 8), (3, 4)), jnp.float32)
    return {"keys_a": keys_a, "values_a": values_a, "queries_b": queries_b, "grad_out": grad_out, "state_start": state_start, "state_next": state_next}


step_rate = 4.0
coef_a = 3.4445
coef_b = -4.775
coef_c = 2.0315

def round_trip(value):
    return lax.optimization_barrier(value.astype(jnp.bfloat16)).astype(jnp.float32)

def field_grad(weights_in, inputs, targets):
    rounded = round_trip(weights_in)
    left_rows = inputs.astype(jnp.float32)
    right_rows = targets.astype(jnp.float32)
    gate_pre = jnp.einsum('thd,hdf->thf', left_rows, rounded[0])
    up_pre = jnp.einsum('thd,hdf->thf', left_rows, rounded[1])
    target_proj = jnp.einsum('thd,hdf->thf', right_rows, rounded[2])
    sigmoid_val = jax.nn.sigmoid(gate_pre)
    swish_val = gate_pre * sigmoid_val
    hidden = round_trip(swish_val * up_pre)
    d_gate = round_trip(target_proj * up_pre * sigmoid_val * (1.0 + gate_pre * (1.0 - sigmoid_val)))
    d_up = round_trip(target_proj * swish_val)
    grad_a = jnp.einsum('thd,thf->hdf', left_rows, d_gate)
    grad_b = jnp.einsum('thd,thf->hdf', left_rows, d_up)
    grad_c = jnp.einsum('thd,thf->hdf', right_rows, hidden)
    return jnp.stack([grad_a, grad_b, grad_c])

def newton(gradients):
    scale_norm = jnp.sqrt(lax.optimization_barrier(jnp.sum(gradients * gradients, axis=(1, 2), keepdims=True)) + 1e-06)
    iterate = round_trip(gradients / scale_norm)
    for repeat in range(NS_STEPS):
        gram_block = round_trip(jnp.einsum('mdf,mef->mde', iterate, iterate))
        square = jnp.einsum('mde,mek->mdk', gram_block, gram_block)
        poly_term = round_trip(coef_b * gram_block + coef_c * square)
        iterate = round_trip(coef_a * iterate + jnp.einsum('mde,mef->mdf', poly_term, iterate))
    return iterate

def reference(keys_a, values_a, queries_b, grad_out, state_start, state_next):
    block_shape = (N_CTX, TOK, H, D)
    slot_shape = (3 * H, D, F)

    def one_clip(blocks):
        key_blocks = blocks[0].reshape(block_shape)
        value_blocks = blocks[1].reshape(block_shape)
        query_blocks = blocks[2].reshape(block_shape)
        out_blocks = blocks[3].reshape(block_shape)
        clip_next = blocks[4]
        parts_g = jax.vmap(field_grad, in_axes=(None, 0, 0))(state_start, key_blocks, value_blocks)
        total_g = lax.optimization_barrier(jnp.sum(round_trip(parts_g), axis=0))
        parts_s = jax.vmap(field_grad, in_axes=(None, 0, 0))(clip_next, query_blocks, out_blocks)
        total_s = lax.optimization_barrier(jnp.sum(round_trip(parts_s), axis=0))
        d_update = round_trip(step_rate * total_s).reshape(slot_shape)
        unused, pullback = jax.vjp(newton, total_g.reshape(slot_shape))
        d_field = pullback(d_update)[0].reshape(total_g.shape)

        def backward(key_block, value_block):
            unused_out, pull_field = jax.vjp(field_grad, state_start, key_block, value_block)
            return pull_field(d_field)
        d_start, d_keys, d_values = jax.vmap(backward)(key_blocks, value_blocks)
        clip_state = lax.optimization_barrier(jnp.sum(round_trip(parts_s + d_start), axis=0))
        return (d_keys.reshape(GROUP, H * D).astype(jnp.bfloat16), d_values.reshape(GROUP, H * D).astype(jnp.bfloat16), clip_state)
    grad_keys, grad_values, clip_states = lax.map(one_clip, (keys_a, values_a, queries_b, grad_out, state_next))
    grad_state = lax.optimization_barrier(jnp.sum(clip_states, axis=0)) / N_DP
    return (grad_keys, grad_values, grad_state)
```

```python
import functools

import jax
import jax.numpy as jnp
from jax import lax
from jax.experimental import pallas as pl
from jax.experimental.pallas import tpu as pltpu
from jax.sharding import PartitionSpec as P

RATE = 4.0
CA = 3.4445
CB = -4.775
CC = 2.0315
STEPS = 2
F32 = jnp.float32
BF16 = jnp.bfloat16
VMEM_LIMIT = 48 * 1024 * 1024


def dot_nn(a, b):
    return lax.dot_general(a, b, (((1,), (0,)), ((), ())), preferred_element_type=F32)


def dot_nt(a, b):
    return lax.dot_general(a, b, (((1,), (1,)), ((), ())), preferred_element_type=F32)


def dot_tn(a, b):
    return lax.dot_general(a, b, (((0,), (0,)), ((), ())), preferred_element_type=F32)


def pack_kernel(idx, k_ref, v_ref, q_ref, o_ref, s0_ref, sn_ref, *outs, n, per, heads, chunks):
    tokens = k_ref.shape[1]
    rows = s0_ref.shape[2]
    width = s0_ref.shape[3]
    at = 0
    for first, count in chunks:
        for slot in range(n):
            for j in range(count):
                head = jnp.minimum(idx[slot] * per + first + j, heads - 1)
                cols = pl.ds(pl.multiple_of(head * width, width), width)
                for out, left, right, state in (
                    (outs[at], k_ref, v_ref, s0_ref),
                    (outs[at + 1], q_ref, o_ref, sn_ref),
                ):
                    out[j, 0:tokens, :] = left[0, :, cols]
                    out[j, tokens : 2 * tokens, :] = right[0, :, cols]
                    parts = jnp.concatenate([state[m, head] for m in range(3)], axis=0)
                    out[j, 2 * tokens : 2 * tokens + 3 * rows, :] = parts.astype(BF16)
            at += 2


def swish_terms(g):
    s = 1.0 / (1.0 + jnp.exp(-g))
    sw = g * s
    slope = s * (1.0 + g * (1.0 - s))
    return s, sw, slope


def newton_pullback(grads, updates):
    count = len(grads)
    each = range(count)
    inv = [lax.rsqrt(jnp.sum(g * g, keepdims=True) + 1e-06) for g in grads]
    xs = [[(grads[m] * inv[m]).astype(BF16) for m in each]]
    grams = []
    polys = []
    for step in range(STEPS):
        x = xs[-1]
        gram = [dot_nt(x[m], x[m]).astype(BF16) for m in each]
        poly = [(CB * gram[m].astype(F32) + CC * dot_nn(gram[m], gram[m])).astype(BF16) for m in each]
        grams.append(gram)
        polys.append(poly)
        if step + 1 < STEPS:
            xs.append([(CA * x[m].astype(F32) + dot_nn(poly[m], x[m])).astype(BF16) for m in each])
    d = updates
    for step in reversed(range(STEPS)):
        x, gram, poly = xs[step], grams[step], polys[step]
        dp = [dot_nt(d[m], x[m]) for m in each]
        sym = [dp[m] + dp[m].T for m in each]
        turned = [dot_nn(sym[m].astype(BF16), gram[m]) for m in each]
        da = [(CB * sym[m] + CC * (turned[m] + turned[m].T)).astype(BF16) for m in each]
        d = [
            (CA * d[m].astype(F32) + dot_nn(poly[m], d[m]) + dot_nn(da[m], x[m])).astype(BF16)
            for m in each
        ]
    out = []
    for m in each:
        df = d[m].astype(F32)
        along = jnp.sum(df * grads[m], keepdims=True)
        out.append(df * inv[m] - grads[m] * (along * (inv[m] * inv[m] * inv[m])))
    return out


def chunk_kernel(idx, *refs, n, count, rows):
    a_refs, b_refs = refs[:n], refs[n : 2 * n]
    d_refs, c_ref = refs[2 * n : 3 * n], refs[3 * n]
    w0, w1, gsum, ssum, acts, fields = refs[3 * n + 1 :]
    tokens = (a_refs[0].shape[1] - 3 * rows) // 2
    width = a_refs[0].shape[2]
    for slot in range(n):
        at = pl.multiple_of(idx[slot] * rows, rows)
        for j in range(count):
            for dst, src in ((w0, a_refs[slot]), (w1, b_refs[slot])):
                part = src[j, 2 * tokens : 2 * tokens + 3 * rows, :].astype(F32)
                for m in range(3):
                    dst[3 * j + m, pl.ds(at, rows), :] = part[m * rows : (m + 1) * rows]

    def forward(j, token_refs, w, keep):
        x = jnp.concatenate([r[j, 0:tokens, :] for r in token_refs], axis=0)
        y = jnp.concatenate([r[j, tokens : 2 * tokens, :] for r in token_refs], axis=0)
        wab = jnp.concatenate([w[3 * j], w[3 * j + 1]], axis=1).astype(BF16)
        gu = dot_nn(x, wab)
        g, u = gu[:, :width], gu[:, width:]
        p = dot_nn(y, w[3 * j + 2].astype(BF16))
        s, sw, slope = swish_terms(g)
        hidden = (sw * u).astype(BF16)
        dg = (p * u * slope).astype(BF16)
        du = (p * sw).astype(BF16)
        if keep:
            acts[j, 0], acts[j, 1], acts[j, 2] = g, u, p
            fields[j, 0], fields[j, 1], fields[j, 2] = dg, du, hidden
        ab = dot_tn(x, jnp.concatenate([dg, du], axis=1))
        return ab[:, :width], ab[:, width:], dot_tn(y, hidden)

    for j in range(count):
        for m, val in enumerate(forward(j, a_refs, w0, True)):
            gsum[3 * j + m] = val
        for m, val in enumerate(forward(j, b_refs, w1, False)):
            ssum[3 * j + m] = val

    slots = range(3 * count)
    grads = [gsum[m] for m in slots]
    updates = [(RATE * ssum[m]).astype(BF16) for m in slots]
    for m, val in enumerate(newton_pullback(grads, updates)):
        gsum[m] = val

    for j in range(count):
        x = jnp.concatenate([r[j, 0:tokens, :] for r in a_refs], axis=0)
        y = jnp.concatenate([r[j, tokens : 2 * tokens, :] for r in a_refs], axis=0)
        fab = jnp.concatenate([gsum[3 * j], gsum[3 * j + 1]], axis=1).astype(BF16)
        fc = gsum[3 * j + 2].astype(BF16)
        wab = jnp.concatenate([w0[3 * j], w0[3 * j + 1]], axis=1).astype(BF16)
        wc = w0[3 * j + 2].astype(BF16)
        cdgu = dot_nn(x, fab)
        cdg, cdu = cdgu[:, :width], cdgu[:, width:]
        ch = dot_nn(y, fc)
        g, u, p = acts[j, 0], acts[j, 1], acts[j, 2]
        s, sw, slope = swish_terms(g)
        curve = s * (1.0 - s) * (2.0 + g * (1.0 - 2.0 * s))
        cg = ((ch * u + cdu * p) * slope + cdg * (p * u) * curve).astype(BF16)
        cu = (ch * sw + cdg * p * slope).astype(BF16)
        cp = (cdu * sw + cdg * u * slope).astype(BF16)
        dg, du, hidden = fields[j, 0], fields[j, 1], fields[j, 2]
        dx = dot_nt(jnp.concatenate([dg, du, cg, cu], axis=1), jnp.concatenate([fab, wab], axis=1))
        dy = dot_nt(jnp.concatenate([hidden, cp], axis=1), jnp.concatenate([fc, wc], axis=1))
        for slot in range(n):
            d_refs[slot][j, 0:tokens, :] = dx[slot * tokens : (slot + 1) * tokens].astype(BF16)
            d_refs[slot][j, tokens : 2 * tokens, :] = dy[slot * tokens : (slot + 1) * tokens].astype(BF16)
        ab = dot_tn(x, jnp.concatenate([cg, cu], axis=1))
        c_ref[3 * j] = (ssum[3 * j] + ab[:, :width]).astype(BF16)
        c_ref[3 * j + 1] = (ssum[3 * j + 1] + ab[:, width:]).astype(BF16)
        c_ref[3 * j + 2] = (ssum[3 * j + 2] + dot_tn(y, cp)).astype(BF16)
    for m in range(3 * count, c_ref.shape[0]):
        c_ref[m] = jnp.zeros(c_ref.shape[1:], BF16)


def unpack_kernel(idx, *refs, n, per, heads, chunks):
    ins, (dk, dv) = refs[:-2], refs[-2:]
    tokens = dk.shape[1]
    width = dk.shape[2] // heads
    at = 0
    for first, count in chunks:
        for slot in range(n):
            for j in range(count):
                head = idx[slot] * per + first + j

                @pl.when(head < heads)
                def _(head=head, ref=ins[at], j=j):
                    cols = pl.ds(pl.multiple_of(head * width, width), width)
                    dk[0, :, cols] = ref[j, 0:tokens, :]
                    dv[0, :, cols] = ref[j, tokens : 2 * tokens, :]

            at += 1


def local(keys_a, values_a, queries_b, grad_out, state_start, state_next):
    n = lax.axis_size("ctx")
    n_dp = lax.axis_size("dp")
    tokens = keys_a.shape[1]
    _, heads, rows, width = state_start.shape
    per = -(-heads // n)
    split = max(1, per - 1)
    chunks = [c for c in ((0, split), (split, per - split)) if c[1] > 0]
    me = lax.axis_index("ctx")
    idx = jnp.bitwise_xor(me, jnp.arange(n, dtype=jnp.int32))
    smem = pl.BlockSpec(memory_space=pltpu.SMEM)
    vmem = pl.BlockSpec(memory_space=pltpu.VMEM)
    params = pltpu.CompilerParams(vmem_limit_bytes=VMEM_LIMIT)

    packed_shapes = []
    for _, count in chunks:
        one = jax.ShapeDtypeStruct((count, 2 * tokens + 3 * rows, width), BF16)
        packed_shapes += [one] * (2 * n)
    packed = pl.pallas_call(
        functools.partial(pack_kernel, n=n, per=per, heads=heads, chunks=chunks),
        out_shape=packed_shapes,
        in_specs=[smem] + [vmem] * 6,
        out_specs=[vmem] * len(packed_shapes),
        compiler_params=params,
        name="pack",
    )(idx, keys_a, values_a, queries_b, grad_out, state_start, state_next[0])

    def exchange(value, slot):
        if slot == 0:
            return value
        return lax.ppermute(value, "ctx", [(i, i ^ slot) for i in range(n)])

    back = []
    states = []
    for c, (first, count) in enumerate(chunks):
        sent = packed[2 * n * c : 2 * n * (c + 1)]
        a_in = [exchange(sent[2 * s], s) for s in range(n)]
        b_in = [exchange(sent[2 * s + 1], s) for s in range(n)]
        slots = -(-3 * count // n_dp) * n_dp
        rows_all = n * tokens
        outs = pl.pallas_call(
            functools.partial(chunk_kernel, n=n, count=count, rows=rows),
            out_shape=[jax.ShapeDtypeStruct((count, 2 * tokens, width), BF16)] * n
            + [jax.ShapeDtypeStruct((slots, width, width), BF16)],
            in_specs=[smem] + [vmem] * (2 * n),
            out_specs=[vmem] * (n + 1),
            scratch_shapes=[
                pltpu.VMEM((3 * count, width, width), F32),
                pltpu.VMEM((3 * count, width, width), F32),
                pltpu.VMEM((3 * count, width, width), F32),
                pltpu.VMEM((3 * count, width, width), F32),
                pltpu.VMEM((count, 3, rows_all, width), F32),
                pltpu.VMEM((count, 3, rows_all, width), BF16),
            ],
            compiler_params=params,
            cost_estimate=pl.CostEstimate(
                flops=count * 640 * 10**6, bytes_accessed=count * 10**6, transcendentals=0
            ),
            name=f"chunk{c}",
        )(idx, *a_in, *b_in)
        back += [exchange(outs[s], s) for s in range(n)]
        states.append((first, count, slots, outs[n]))

    grad_keys, grad_values = pl.pallas_call(
        functools.partial(unpack_kernel, n=n, per=per, heads=heads, chunks=chunks),
        out_shape=[
            jax.ShapeDtypeStruct(keys_a.shape, BF16),
            jax.ShapeDtypeStruct(values_a.shape, BF16),
        ],
        in_specs=[smem] + [vmem] * len(back),
        out_specs=[vmem] * 2,
        compiler_params=params,
        name="unpack",
    )(idx, *back)

    pieces = []
    for first, count, slots, state in states:
        own = slots // n_dp
        spread = lax.all_to_all(
            state.reshape(n_dp, own, width, width), "dp", split_axis=0, concat_axis=0, tiled=True
        )
        summed = jnp.sum(spread.astype(F32), axis=0).astype(BF16)
        by_rows = summed.reshape(own, n, rows, width).transpose(1, 0, 2, 3)
        turned = lax.all_to_all(by_rows, "ctx", split_axis=0, concat_axis=0, tiled=True)
        copies = jnp.broadcast_to(turned[None], (n_dp,) + turned.shape)
        full = lax.all_to_all(copies, "dp", split_axis=0, concat_axis=0, tiled=True)
        full = full.transpose(1, 0, 2, 3, 4).reshape(n, slots, rows, width)[:, : 3 * count]
        pieces.append(full.reshape(n, count, 3, rows, width))
    whole = jnp.concatenate(pieces, axis=1).reshape(n * per, 3, rows, width)[:heads]
    grad_state = whole.transpose(1, 0, 2, 3).astype(F32) / n_dp
    return grad_keys, grad_values, grad_state


def solution(mesh):
    placed = (
        P("dp", "ctx", None),
        P("dp", "ctx", None),
        P("dp", "ctx", None),
        P("dp", "ctx", None),
        P(None, None, "ctx", None),
        P("dp", None, None, "ctx", None),
    )
    return jax.shard_map(
        local,
        mesh=mesh,
        in_specs=placed,
        out_specs=(P("dp", "ctx", None), P("dp", "ctx", None), P(None, None, "ctx", None)),
        check_vma=False,
    )
```

```python
import functools

import jax
import jax.numpy as jnp
from jax import lax
from jax.experimental import pallas as pl
from jax.experimental.pallas import tpu as pltpu
from jax.sharding import PartitionSpec as P

RATE = 4.0
CA = 3.4445
CB = -4.775
CC = 2.0315
STEPS = 2
F32 = jnp.float32
BF16 = jnp.bfloat16
VMEM_LIMIT = 48 * 1024 * 1024
SMEM = pl.BlockSpec(memory_space=pltpu.SMEM)
VMEM = pl.BlockSpec(memory_space=pltpu.VMEM)
ANY = pl.BlockSpec(memory_space=pl.ANY)


def dot_nn(a, b):
    return lax.dot_general(a, b, (((1,), (0,)), ((), ())), preferred_element_type=F32)


def dot_nt(a, b):
    return lax.dot_general(a, b, (((1,), (1,)), ((), ())), preferred_element_type=F32)


def dot_tn(a, b):
    return lax.dot_general(a, b, (((0,), (0,)), ((), ())), preferred_element_type=F32)


def call(kernel, out_shape, args, in_specs, out_specs, name, scratch=(), flops=10**6, size=10**6):
    return pl.pallas_call(
        kernel,
        out_shape=out_shape,
        in_specs=in_specs,
        out_specs=out_specs,
        scratch_shapes=list(scratch),
        compiler_params=pltpu.CompilerParams(vmem_limit_bytes=VMEM_LIMIT),
        cost_estimate=pl.CostEstimate(flops=flops, bytes_accessed=size, transcendentals=0),
        name=name,
    )(*args)


def swish_terms(g):
    s = 1.0 / (1.0 + jnp.exp(-g))
    sw = g * s
    slope = s * (1.0 + g * (1.0 - s))
    return s, sw, slope


def newton_pullback(grads, updates):
    each = range(len(grads))
    inv = [lax.rsqrt(jnp.sum(g * g, keepdims=True) + 1e-06) for g in grads]
    xs = [[(grads[m] * inv[m]).astype(BF16) for m in each]]
    grams = []
    polys = []
    for step in range(STEPS):
        x = xs[-1]
        gram = [dot_nt(x[m], x[m]).astype(BF16) for m in each]
        poly = [(CB * gram[m].astype(F32) + CC * dot_nn(gram[m], gram[m])).astype(BF16) for m in each]
        grams.append(gram)
        polys.append(poly)
        if step + 1 < STEPS:
            xs.append([(CA * x[m].astype(F32) + dot_nn(poly[m], x[m])).astype(BF16) for m in each])
    d = updates
    for step in reversed(range(STEPS)):
        x, gram, poly = xs[step], grams[step], polys[step]
        dp = [dot_nt(d[m], x[m]) for m in each]
        sym = [dp[m] + dp[m].T for m in each]
        turned = [dot_nn(sym[m].astype(BF16), gram[m]) for m in each]
        da = [(CB * sym[m] + CC * (turned[m] + turned[m].T)).astype(BF16) for m in each]
        d = [
            (CA * d[m].astype(F32) + dot_nn(poly[m], d[m]) + dot_nn(da[m], x[m])).astype(BF16)
            for m in each
        ]
    out = []
    for m in each:
        df = d[m].astype(F32)
        along = jnp.sum(df * grads[m], keepdims=True)
        out.append(df * inv[m] - grads[m] * (along * (inv[m] * inv[m] * inv[m])))
    return out


class Plan:
    def __init__(self, n, n_dp, tokens, heads, rows, width, chunks_of):
        self.n, self.n_dp = n, n_dp
        self.tokens, self.heads, self.rows, self.width = tokens, heads, rows, width
        self.per = -(-heads // n)
        self.mats = 3 * self.per
        self.group = min(4, n_dp)
        self.share = -(-self.mats // self.group)
        self.own = -(-self.mats // n_dp)
        self.block = -(-rows // 16) * 16
        self.share_rows = -(-self.share // self.per) * self.block
        self.chunks = chunks_of(self.per)

    def first_head(self, c):
        return min(c * self.per, self.heads - self.per)


def pack_a_kernel(slot_ref, head_ref, dp_ref, k_ref, v_ref, s_ref, *refs, plan):
    n, t, w, per = plan.n, plan.tokens, plan.width, plan.per
    outs, (state, sems) = refs[:n], refs[n:]
    copies = [pltpu.make_async_copy(s_ref, state, sems.at[2 * n])]
    copies[0].start()
    for slot in range(n):
        cols = pl.ds(pl.multiple_of(head_ref[slot] * w, w), per * w)
        for part, src in enumerate((k_ref, v_ref)):
            copy = pltpu.make_async_copy(
                src.at[0, :, cols], outs[slot].at[pl.ds(part * t, t), :], sems.at[2 * slot + part]
            )
            copy.start()
            copies.append(copy)
    copies[0].wait()
    low = dp_ref[0] % plan.group
    for slot in range(n):
        for q in range(plan.share):
            mat = jnp.minimum(low * plan.share + q, plan.mats - 1)
            part = state[mat % 3, head_ref[slot] + mat // 3].astype(BF16)
            top = 2 * t + (q // per) * plan.block
            left = (q % per) * w
            outs[slot][top : top + plan.rows, left : left + w] = part
    for copy in copies[1:]:
        copy.wait()


def pack_b_kernel(slot_ref, head_ref, q_ref, o_ref, s_ref, *refs, plan):
    n, t, w = plan.n, plan.tokens, plan.width
    chunks = plan.chunks
    outs, (state, sems) = refs[: n * len(chunks)], refs[n * len(chunks) :]
    copies = [pltpu.make_async_copy(s_ref, state, sems.at[2 * n * len(chunks)])]
    copies[0].start()
    for c, (first, count) in enumerate(chunks):
        for slot in range(n):
            at = c * n + slot
            cols = pl.ds(pl.multiple_of((head_ref[slot] + first) * w, w), count * w)
            for part, src in enumerate((q_ref, o_ref)):
                copy = pltpu.make_async_copy(
                    src.at[0, :, cols], outs[at].at[pl.ds(part * t, t), :], sems.at[2 * at + part]
                )
                copy.start()
                copies.append(copy)
    copies[0].wait()
    for c, (first, count) in enumerate(chunks):
        for slot in range(n):
            for j in range(count):
                for m in range(3):
                    part = state[0, m, head_ref[slot] + first + j].astype(BF16)
                    top = 2 * t + m * plan.block
                    outs[c * n + slot][top : top + plan.rows, j * w : (j + 1) * w] = part
    for copy in copies[1:]:
        copy.wait()


def start_kernel(slot_ref, *refs, plan):
    n, w = plan.n, plan.width
    a_refs, (out, whole) = refs[:n], refs[n:]
    for slot in range(n):
        at = pl.ds(pl.multiple_of(slot_ref[slot] * plan.rows, plan.rows), plan.rows)
        for q in range(plan.share):
            top = 2 * plan.tokens + (q // plan.per) * plan.block
            left = (q % plan.per) * w
            whole[q, at, :] = a_refs[slot][top : top + plan.rows, left : left + w].astype(F32)
    out[...] = whole[...].astype(BF16)


def chunk_kernel(slot_ref, dp_ref, *refs, plan, chunk, last):
    n, t, w = plan.n, plan.tokens, plan.width
    first, count = plan.chunks[chunk]
    refs = list(refs)

    def take(k):
        got = refs[:k]
        del refs[:k]
        return got

    a_refs, b_refs, shares = take(n), take(n), take(plan.group)
    before = take(chunk) if last else []
    (d_ref,) = take(1)
    c_refs = take(plan.n_dp if last else 1)
    w0, w1, gsum, ssum, acts, fields = take(6)
    total = take(1)[0] if last else c_refs[0]
    base = 3 * first if last else 0

    low = dp_ref[0] % plan.group
    for k in range(plan.group):
        at = pl.ds(jnp.bitwise_xor(low, k) * plan.share, plan.share)
        w0[at] = shares[k][...]
    for slot in range(n):
        at = pl.ds(pl.multiple_of(slot_ref[slot] * plan.rows, plan.rows), plan.rows)
        for j in range(count):
            for m in range(3):
                top = 2 * t + m * plan.block
                part = b_refs[slot][top : top + plan.rows, j * w : (j + 1) * w]
                w1[3 * j + m, at, :] = part.astype(F32)

    def tokens_of(slots, j):
        cols = slice(j * w, (j + 1) * w)
        x = jnp.concatenate([r[0:t, cols] for r in slots], axis=0)
        y = jnp.concatenate([r[t : 2 * t, cols] for r in slots], axis=0)
        return x, y

    def forward(x, y, wa, wb, wc, keep):
        gu = dot_nn(x, jnp.concatenate([wa, wb], axis=1))
        g, u = gu[:, :w], gu[:, w:]
        p = dot_nn(y, wc)
        _, sw, slope = swish_terms(g)
        hidden = (sw * u).astype(BF16)
        dg = (p * u * slope).astype(BF16)
        du = (p * sw).astype(BF16)
        if keep is not None:
            acts[keep, 0], acts[keep, 1], acts[keep, 2] = g, u, p
            fields[keep, 0], fields[keep, 1], fields[keep, 2] = dg, du, hidden
        ab = dot_tn(x, jnp.concatenate([dg, du], axis=1))
        return ab[:, :w], ab[:, w:], dot_tn(y, hidden)

    for j in range(count):
        x, y = tokens_of(a_refs, first + j)
        at = 3 * (first + j)
        for m, val in enumerate(forward(x, y, w0[at], w0[at + 1], w0[at + 2], j)):
            gsum[3 * j + m] = val
        x, y = tokens_of(b_refs, j)
        weights = [w1[3 * j + m].astype(BF16) for m in range(3)]
        for m, val in enumerate(forward(x, y, *weights, None)):
            ssum[3 * j + m] = val

    mats = range(3 * count)
    grads = [gsum[m] for m in mats]
    updates = [(RATE * ssum[m]).astype(BF16) for m in mats]
    for m, val in enumerate(newton_pullback(grads, updates)):
        gsum[m] = val

    for j in range(count):
        x, y = tokens_of(a_refs, first + j)
        at = 3 * (first + j)
        fab = jnp.concatenate([gsum[3 * j], gsum[3 * j + 1]], axis=1).astype(BF16)
        fc = gsum[3 * j + 2].astype(BF16)
        wab = jnp.concatenate([w0[at], w0[at + 1]], axis=1)
        wc = w0[at + 2]
        cdgu = dot_nn(x, fab)
        cdg, cdu = cdgu[:, :w], cdgu[:, w:]
        ch = dot_nn(y, fc)
        g, u, p = acts[j, 0], acts[j, 1], acts[j, 2]
        s, sw, slope = swish_terms(g)
        curve = s * (1.0 - s) * (2.0 + g * (1.0 - 2.0 * s))
        cg = ((ch * u + cdu * p) * slope + cdg * (p * u) * curve).astype(BF16)
        cu = (ch * sw + cdg * p * slope).astype(BF16)
        cp = (cdu * sw + cdg * u * slope).astype(BF16)
        dg, du, hidden = fields[j, 0], fields[j, 1], fields[j, 2]
        dx = dot_nt(jnp.concatenate([dg, du, cg, cu], axis=1), jnp.concatenate([fab, wab], axis=1))
        dy = dot_nt(jnp.concatenate([hidden, cp], axis=1), jnp.concatenate([fc, wc], axis=1))
        cols = slice(j * w, (j + 1) * w)
        for slot in range(n):
            to = slot_ref[slot]
            d_ref[to, 0:t, cols] = dx[slot * t : (slot + 1) * t].astype(BF16)
            d_ref[to, t : 2 * t, cols] = dy[slot * t : (slot + 1) * t].astype(BF16)
        ab = dot_tn(x, jnp.concatenate([cg, cu], axis=1))
        grown = (ab[:, :w], ab[:, w:], dot_tn(y, cp))
        for m in range(3):
            total[base + 3 * j + m] = (ssum[3 * j + m] + grown[m]).astype(BF16)

    if last:
        for c, part in enumerate(before):
            at = 3 * plan.chunks[c][0]
            total[at : at + part.shape[0]] = part[...]
        for m in range(plan.mats, plan.n_dp * plan.own):
            total[m] = jnp.zeros((w, w), BF16)
        for k in range(plan.n_dp):
            at = jnp.bitwise_xor(dp_ref[0], k) * plan.own
            c_refs[k][...] = total[pl.ds(at, plan.own)]


def sum_kernel(slot_ref, *refs, plan):
    parts, outs, whole = refs[: plan.n_dp], refs[plan.n_dp : -1], refs[-1]
    added = parts[0][...].astype(F32)
    for part in parts[1:]:
        added = added + part[...].astype(F32)
    whole[...] = added / plan.n_dp
    for slot in range(plan.n):
        at = pl.ds(pl.multiple_of(slot_ref[slot] * plan.rows, plan.rows), plan.rows)
        outs[slot][...] = whole[:, at, :].astype(BF16)


def order_kernel(slot_ref, *refs, plan):
    for slot in range(plan.n):
        refs[-1][slot_ref[slot]] = refs[slot][...]


def state_kernel(dp_ref, *refs, plan):
    out = refs[-1]
    for k in range(plan.n_dp):
        for i in range(plan.own):
            mat = jnp.bitwise_xor(dp_ref[0], k) * plan.own + i

            @pl.when(mat < plan.mats)
            def _(mat=mat, ref=refs[k], i=i):
                for c in range(plan.n):
                    out[mat % 3, plan.first_head(c) + mat // 3] = ref[c, i].astype(F32)


def unpack_kernel(*refs, plan):
    chunks = plan.chunks
    t, w = plan.tokens, plan.width
    ins, (dk, dv, sems) = refs[: len(chunks)], refs[len(chunks) :]
    copies = []
    for c, (first, count) in enumerate(chunks):
        for owner in range(plan.n):
            cols = pl.ds((plan.first_head(owner) + first) * w, count * w)
            for part, dst in enumerate((dk, dv)):
                copy = pltpu.make_async_copy(
                    ins[c].at[owner, pl.ds(part * t, t), :],
                    dst.at[0, :, cols],
                    sems.at[(c * plan.n + owner) * 2 + part],
                )
                copy.start()
                copies.append(copy)
        if plan.n * plan.per != plan.heads:
            for copy in copies:
                copy.wait()
            copies = []
    for copy in copies:
        copy.wait()


def chunks_of(per):
    split = (per + 1) // 2
    return [c for c in ((0, split), (split, per - split)) if c[1] > 0]


def local(keys_a, values_a, queries_b, grad_out, state_start, state_next):
    n, n_dp = lax.axis_size("ctx"), lax.axis_size("dp")
    _, heads, rows, width = state_start.shape
    t = keys_a.shape[1]
    plan = Plan(n, n_dp, t, heads, rows, width, chunks_of)
    per, chunks = plan.per, plan.chunks
    bind = lambda kernel, **more: functools.partial(kernel, plan=plan, **more)

    slot_ids = jnp.bitwise_xor(lax.axis_index("ctx"), jnp.arange(n, dtype=jnp.int32))
    head_ids = jnp.minimum(slot_ids * per, heads - per)
    dp_id = lax.axis_index("dp").reshape(1)

    def swap(value, axis, size, k):
        if k == 0:
            return value
        return lax.ppermute(value, axis, [(i, i ^ k) for i in range(size)])

    def shape(*dims, dtype=BF16):
        return jax.ShapeDtypeStruct(dims, dtype)

    a_sent = call(
        bind(pack_a_kernel),
        [shape(2 * t + plan.share_rows, per * width)] * n,
        (slot_ids, head_ids, dp_id, keys_a, values_a, state_start),
        [SMEM] * 3 + [ANY] * 3,
        [VMEM] * n,
        "pack_a",
        [pltpu.VMEM(state_start.shape, F32), pltpu.SemaphoreType.DMA((2 * n + 1,))],
    )
    a_in = [swap(a_sent[s], "ctx", n, s) for s in range(n)]
    b_sent = call(
        bind(pack_b_kernel),
        [shape(2 * t + 3 * plan.block, count * width) for _, count in chunks for _ in range(n)],
        (slot_ids, head_ids, queries_b, grad_out, state_next),
        [SMEM] * 2 + [ANY] * 3,
        [VMEM] * (n * len(chunks)),
        "pack_b",
        [pltpu.VMEM(state_next.shape, F32), pltpu.SemaphoreType.DMA((2 * n * len(chunks) + 1,))],
    )
    b_in = [
        [swap(b_sent[c * n + s], "ctx", n, s) for s in range(n)] for c in range(len(chunks))
    ]
    start_own = call(
        bind(start_kernel),
        shape(plan.share, width, width),
        (slot_ids, *a_in),
        [SMEM] + [VMEM] * n,
        VMEM,
        "start_share",
        [pltpu.VMEM((plan.share, width, width), F32)],
    )
    shares = [swap(start_own, "dp", n_dp, k) for k in range(plan.group)]

    back = []
    sums = []
    for c, (first, count) in enumerate(chunks):
        last = c + 1 == len(chunks)
        before = sums if last else []
        mats = 3 * count
        if last:
            c_shapes = [shape(plan.own, width, width)] * n_dp
        else:
            c_shapes = [shape(mats, width, width)]
        scratch = [
            pltpu.VMEM((plan.group * plan.share, width, width), BF16),
            pltpu.VMEM((mats, width, width), F32),
            pltpu.VMEM((mats, width, width), F32),
            pltpu.VMEM((mats, width, width), F32),
            pltpu.VMEM((count, 3, n * t, width), F32),
            pltpu.VMEM((count, 3, n * t, width), BF16),
        ]
        if last:
            scratch.append(pltpu.VMEM((n_dp * plan.own, width, width), BF16))
        outs = call(
            bind(chunk_kernel, chunk=c, last=last),
            [shape(n, 2 * t, count * width)] + c_shapes,
            (slot_ids, dp_id, *a_in, *b_in[c], *shares, *before),
            [SMEM] * 2 + [VMEM] * (2 * n + plan.group + len(before)),
            [VMEM] * (1 + len(c_shapes)),
            f"chunk{c}",
            scratch,
            flops=count * 640 * 10**6,
            size=count * 10**6,
        )
        back.append(lax.all_to_all(outs[0], "ctx", split_axis=0, concat_axis=0, tiled=True))
        sums += outs[1:]

    parts = sums[len(chunks) - 1 :]
    parts = [swap(parts[k], "dp", n_dp, k) for k in range(n_dp)]
    by_rows = call(
        bind(sum_kernel),
        [shape(plan.own, rows, width)] * n,
        (slot_ids, *parts),
        [SMEM] + [VMEM] * n_dp,
        [VMEM] * n,
        "state_sum",
        [pltpu.VMEM((plan.own, width, width), F32)],
    )
    by_rows = [swap(by_rows[s], "ctx", n, s) for s in range(n)]
    mine = call(
        bind(order_kernel),
        shape(n, plan.own, rows, width),
        (slot_ids, *by_rows),
        [SMEM] + [VMEM] * n,
        VMEM,
        "state_order",
    )
    everyone = [swap(mine, "dp", n_dp, k) for k in range(n_dp)]
    grad_state = call(
        bind(state_kernel),
        shape(*state_start.shape, dtype=F32),
        (dp_id, *everyone),
        [SMEM] + [VMEM] * n_dp,
        VMEM,
        "state_out",
    )
    grad_keys, grad_values = call(
        bind(unpack_kernel),
        [shape(*keys_a.shape), shape(*values_a.shape)],
        back,
        [VMEM] * len(back),
        [ANY] * 2,
        "unpack",
        [pltpu.SemaphoreType.DMA((2 * n * len(chunks),))],
    )
    return grad_keys, grad_values, grad_state


def solution(mesh):
    placed = (
        P("dp", "ctx", None),
        P("dp", "ctx", None),
        P("dp", "ctx", None),
        P("dp", "ctx", None),
        P(None, None, "ctx", None),
        P("dp", None, None, "ctx", None),
    )
    return jax.shard_map(
        local,
        mesh=mesh,
        in_specs=placed,
        out_specs=(P("dp", "ctx", None), P("dp", "ctx", None), P(None, None, "ctx", None)),
        check_vma=False,
    )
```

```python
import functools

import jax
import jax.numpy as jnp
from jax import lax
from jax.experimental import pallas as pl
from jax.experimental.pallas import tpu as pltpu
from jax.sharding import PartitionSpec as P

RATE = 4.0
CA = 3.4445
CB = -4.775
CC = 2.0315
STEPS = 2
F32 = jnp.float32
BF16 = jnp.bfloat16
VMEM_LIMIT = 40 * 1024 * 1024
VMEM_WHOLE = 58 * 1024 * 1024
SMEM = pl.BlockSpec(memory_space=pltpu.SMEM)
VMEM = pl.BlockSpec(memory_space=pltpu.VMEM)
ANY = pl.BlockSpec(memory_space=pl.ANY)


def dot_nn(a, b):
    return lax.dot_general(a, b, (((1,), (0,)), ((), ())), preferred_element_type=F32)


def dot_nt(a, b):
    return lax.dot_general(a, b, (((1,), (1,)), ((), ())), preferred_element_type=F32)


def dot_tn(a, b):
    return lax.dot_general(a, b, (((0,), (0,)), ((), ())), preferred_element_type=F32)


def call(
    kernel, out_shape, args, in_specs, out_specs, name, scratch=(), flops=10**6, size=10**6, vmem=VMEM_LIMIT
):
    return pl.pallas_call(
        kernel,
        out_shape=out_shape,
        in_specs=in_specs,
        out_specs=out_specs,
        scratch_shapes=list(scratch),
        compiler_params=pltpu.CompilerParams(vmem_limit_bytes=vmem),
        cost_estimate=pl.CostEstimate(flops=flops, bytes_accessed=size, transcendentals=0),
        name=name,
    )(*args)


def swish_terms(g):
    s = 1.0 / (1.0 + jnp.exp(-g))
    sw = g * s
    slope = s * (1.0 + g * (1.0 - s))
    return s, sw, slope


def newton_forward(grads):
    each = range(len(grads))
    inv = [lax.rsqrt(jnp.sum(g * g, keepdims=True) + 1e-06) for g in grads]
    x = [(grads[m] * inv[m]).astype(BF16) for m in each]
    kept = []
    for step in range(STEPS):
        gram = [dot_nt(x[m], x[m]).astype(BF16) for m in each]
        poly = [(CB * gram[m].astype(F32) + CC * dot_nn(gram[m], gram[m])).astype(BF16) for m in each]
        kept.append((x, gram, poly))
        if step + 1 < STEPS:
            x = [(CA * x[m].astype(F32) + dot_nn(poly[m], x[m])).astype(BF16) for m in each]
    return kept


def newton_pullback(grads, kept, updates):
    each = range(len(grads))
    d = updates
    for x, gram, poly in reversed(kept):
        dp = [dot_nt(d[m], x[m]) for m in each]
        sym = [dp[m] + dp[m].T for m in each]
        turned = [dot_nn(sym[m].astype(BF16), gram[m]) for m in each]
        da = [(CB * sym[m] + CC * (turned[m] + turned[m].T)).astype(BF16) for m in each]
        d = [
            (CA * d[m].astype(F32) + dot_nn(poly[m], d[m]) + dot_nn(da[m], x[m])).astype(BF16)
            for m in each
        ]
    out = []
    for m in each:
        df = d[m].astype(F32)
        inv = lax.rsqrt(jnp.sum(grads[m] * grads[m], keepdims=True) + 1e-06)
        along = jnp.sum(df * grads[m], keepdims=True)
        out.append(df * inv - grads[m] * (along * (inv * inv * inv)))
    return out


class Plan:
    def __init__(self, n, n_dp, tokens, heads, rows, width):
        self.n, self.n_dp = n, n_dp
        self.tokens, self.heads, self.rows, self.width = tokens, heads, rows, width
        self.per = -(-heads // n)
        self.mats = 3 * self.per
        self.group = min(4, n_dp)
        self.share = -(-self.mats // self.group)
        self.pair = min(2, n_dp)
        self.rest = n_dp // self.pair
        self.own = -(-self.mats // n_dp)
        self.block = -(-rows // 16) * 16
        self.share_rows = -(-self.share // self.per) * self.block

    def first_head(self, c):
        return min(c * self.per, self.heads - self.per)


def pack_a_kernel(dp_ref, k_ref, v_ref, s_ref, out, state, stage, sems, *, plan):
    n, t, w, per = plan.n, plan.tokens, plan.width, plan.per
    load = pltpu.make_async_copy(s_ref, state, sems.at[3 * n])
    load.start()
    copies = []
    for c in range(n):
        cols = pl.ds(plan.first_head(c) * w, per * w)
        for part, src in enumerate((k_ref, v_ref)):
            copy = pltpu.make_async_copy(
                src.at[0, :, cols], out.at[c, pl.ds(part * t, t), :], sems.at[3 * c + part]
            )
            copy.start()
            copies.append(copy)
    load.wait()
    low = dp_ref[0] % plan.group
    for q in range(plan.share):
        mat = jnp.minimum(low * plan.share + q, plan.mats - 1)
        for c in range(n):
            part = state[mat % 3, plan.first_head(c) + mat // 3].astype(BF16)
            top = (q // per) * plan.block
            left = (q % per) * w
            stage[c, top : top + plan.rows, left : left + w] = part
    for c in range(n):
        copy = pltpu.make_async_copy(
            stage.at[c], out.at[c, pl.ds(2 * t, plan.share_rows), :], sems.at[3 * c + 2]
        )
        copy.start()
        copies.append(copy)
    for copy in copies:
        copy.wait()


def pack_b_kernel(head_ref, q_ref, o_ref, s_ref, *refs, plan):
    n, t, w, per = plan.n, plan.tokens, plan.width, plan.per
    outs, (state, sems) = refs[:n], refs[n:]
    copies = [pltpu.make_async_copy(s_ref, state, sems.at[2 * n])]
    copies[0].start()
    for slot in range(n):
        cols = pl.ds(pl.multiple_of(head_ref[slot] * w, w), per * w)
        for part, src in enumerate((q_ref, o_ref)):
            copy = pltpu.make_async_copy(
                src.at[0, :, cols], outs[slot].at[pl.ds(part * t, t), :], sems.at[2 * slot + part]
            )
            copy.start()
            copies.append(copy)
    copies[0].wait()
    for slot in range(n):
        for j in range(per):
            for m in range(3):
                part = state[0, m, head_ref[slot] + j].astype(BF16)
                top = 2 * t + m * plan.block
                outs[slot][top : top + plan.rows, j * w : (j + 1) * w] = part
    for copy in copies[1:]:
        copy.wait()


def start_kernel(a_ref, out, whole, *, plan):
    rows, w = plan.rows, plan.width
    for c in range(plan.n):
        for q in range(plan.share):
            top = 2 * plan.tokens + (q // plan.per) * plan.block
            left = (q % plan.per) * w
            part = a_ref[c, top : top + rows, left : left + w]
            whole[q, c * rows : (c + 1) * rows, :] = part.astype(F32)
    out[...] = whole[...].astype(BF16)


def forward(x, y, wa, wb, wc):
    w = wa.shape[1]
    gu = dot_nn(x, jnp.concatenate([wa, wb], axis=1))
    g, u = gu[:, :w], gu[:, w:]
    p = dot_nn(y, wc)
    _, sw, slope = swish_terms(g)
    hidden = (sw * u).astype(BF16)
    dg = (p * u * slope).astype(BF16)
    du = (p * sw).astype(BF16)
    ab = dot_tn(x, jnp.concatenate([dg, du], axis=1))
    return (ab[:, :w], ab[:, w:], dot_tn(y, hidden)), (g, u, p), (dg, du, hidden)


def tokens_of(ref, j, plan):
    t, w = plan.tokens, plan.width
    cols = slice(j * w, (j + 1) * w)
    x = jnp.concatenate([ref[c, 0:t, cols] for c in range(plan.n)], axis=0)
    y = jnp.concatenate([ref[c, t : 2 * t, cols] for c in range(plan.n)], axis=0)
    return x, y


def first_kernel(dp_ref, a_ref, *refs, plan):
    shares, (w0, acts, fields, gsum, *kept) = refs[: plan.group], refs[plan.group :]
    low = dp_ref[0] % plan.group
    for k in range(plan.group):
        at = pl.ds(jnp.bitwise_xor(low, k) * plan.share, plan.share)
        w0[at] = shares[k][...]
    for j in range(plan.per):
        x, y = tokens_of(a_ref, j, plan)
        sums, act, field = forward(x, y, w0[3 * j], w0[3 * j + 1], w0[3 * j + 2])
        for m in range(3):
            gsum[3 * j + m] = sums[m]
            acts[j, m] = act[m]
            fields[j, m] = field[m]
    states = newton_forward([gsum[m] for m in range(plan.mats)])
    for ref, values in zip(kept, [v for state in states for v in state]):
        for m in range(plan.mats):
            ref[m] = values[m]


def second_kernel(slot_ref, dp_ref, a_ref, w0, acts, fields, gsum, *refs, plan):
    n, t, w, per, mats = plan.n, plan.tokens, plan.width, plan.per, plan.mats
    kept, refs = refs[: 3 * STEPS], refs[3 * STEPS :]
    b_refs, (d_ref, keep_ref, send_ref, w1, ssum, total) = refs[:n], refs[n:]
    for slot in range(n):
        at = pl.ds(pl.multiple_of(slot_ref[slot] * plan.rows, plan.rows), plan.rows)
        for j in range(per):
            for m in range(3):
                top = 2 * t + m * plan.block
                part = b_refs[slot][top : top + plan.rows, j * w : (j + 1) * w]
                w1[3 * j + m, at, :] = part.astype(F32)
    for j in range(per):
        cols = slice(j * w, (j + 1) * w)
        x = jnp.concatenate([r[0:t, cols] for r in b_refs], axis=0)
        y = jnp.concatenate([r[t : 2 * t, cols] for r in b_refs], axis=0)
        sums, _, _ = forward(x, y, *[w1[3 * j + m].astype(BF16) for m in range(3)])
        for m in range(3):
            ssum[3 * j + m] = sums[m]

    states = [
        tuple([kept[3 * step + i][m] for m in range(mats)] for i in range(3)) for step in range(STEPS)
    ]
    updates = [(RATE * ssum[m]).astype(BF16) for m in range(mats)]
    field_grads = newton_pullback([gsum[m] for m in range(mats)], states, updates)
    for m in range(mats):
        w1[m] = field_grads[m]

    for j in range(per):
        x, y = tokens_of(a_ref, j, plan)
        fab = jnp.concatenate([w1[3 * j], w1[3 * j + 1]], axis=1).astype(BF16)
        fc = w1[3 * j + 2].astype(BF16)
        wab = jnp.concatenate([w0[3 * j], w0[3 * j + 1]], axis=1)
        wc = w0[3 * j + 2]
        cdgu = dot_nn(x, fab)
        cdg, cdu = cdgu[:, :w], cdgu[:, w:]
        ch = dot_nn(y, fc)
        g, u, p = acts[j, 0], acts[j, 1], acts[j, 2]
        s, sw, slope = swish_terms(g)
        curve = s * (1.0 - s) * (2.0 + g * (1.0 - 2.0 * s))
        cg = ((ch * u + cdu * p) * slope + cdg * (p * u) * curve).astype(BF16)
        cu = (ch * sw + cdg * p * slope).astype(BF16)
        cp = (cdu * sw + cdg * u * slope).astype(BF16)
        dg, du, hidden = fields[j, 0], fields[j, 1], fields[j, 2]
        dx = dot_nt(jnp.concatenate([dg, du, cg, cu], axis=1), jnp.concatenate([fab, wab], axis=1))
        dy = dot_nt(jnp.concatenate([hidden, cp], axis=1), jnp.concatenate([fc, wc], axis=1))
        cols = slice(j * w, (j + 1) * w)
        for c in range(n):
            d_ref[c, 0:t, cols] = dx[c * t : (c + 1) * t].astype(BF16)
            d_ref[c, t : 2 * t, cols] = dy[c * t : (c + 1) * t].astype(BF16)
        ab = dot_tn(x, jnp.concatenate([cg, cu], axis=1))
        grown = (ab[:, :w], ab[:, w:], dot_tn(y, cp))
        for m in range(3):
            total[3 * j + m] = (ssum[3 * j + m] + grown[m]).astype(BF16)

    for m in range(mats, plan.n_dp * plan.own):
        total[m] = jnp.zeros((w, w), BF16)
    mine = dp_ref[0] % plan.pair
    for r in range(plan.rest):
        to = slice(r * plan.own, (r + 1) * plan.own)
        keep_ref[to] = total[pl.ds((plan.pair * r + mine) * plan.own, plan.own)]
        send_ref[to] = total[pl.ds((plan.pair * r + plan.pair - 1 - mine) * plan.own, plan.own)]


def pair_kernel(dp_ref, keep_ref, got_ref, *refs, plan):
    outs, whole = refs[:-1], refs[-1]
    whole[...] = keep_ref[...].astype(F32) + got_ref[...].astype(F32)
    place = dp_ref[0] // plan.pair
    for k in range(plan.rest):
        at = pl.ds(jnp.bitwise_xor(place, k) * plan.own, plan.own)
        outs[k][...] = whole[at].astype(BF16)


def sum_kernel(slot_ref, *refs, plan):
    parts, outs, whole = refs[: plan.rest], refs[plan.rest : -1], refs[-1]
    added = parts[0][...].astype(F32)
    for part in parts[1:]:
        added = added + part[...].astype(F32)
    whole[...] = added / plan.n_dp
    for slot in range(plan.n):
        at = pl.ds(pl.multiple_of(slot_ref[slot] * plan.rows, plan.rows), plan.rows)
        outs[slot][...] = whole[:, at, :].astype(BF16)


def order_kernel(place_ref, *refs, plan):
    parts, out = refs[:-1], refs[-1]
    for k, part in enumerate(parts):
        out[place_ref[k]] = part[...]


def state_kernel(dp_ref, *refs, plan):
    out = refs[-1]
    mine = dp_ref[0] % plan.pair
    for k in range(plan.pair):
        for r in range(plan.rest):
            for i in range(plan.own):
                mat = (plan.pair * r + jnp.bitwise_xor(mine, k)) * plan.own + i

                @pl.when(mat < plan.mats)
                def _(mat=mat, ref=refs[k], r=r, i=i):
                    for c in range(plan.n):
                        out[mat % 3, plan.first_head(c) + mat // 3] = ref[r, c, i].astype(F32)


def unpack_kernel(in_ref, dk, dv, sems, *, plan):
    t, w = plan.tokens, plan.width
    copies = []
    for owner in range(plan.n):
        cols = pl.ds(plan.first_head(owner) * w, plan.per * w)
        for part, dst in enumerate((dk, dv)):
            copy = pltpu.make_async_copy(
                in_ref.at[owner, pl.ds(part * t, t), :], dst.at[0, :, cols], sems.at[owner * 2 + part]
            )
            copy.start()
            copies.append(copy)
        if plan.n * plan.per != plan.heads:
            for copy in copies:
                copy.wait()
            copies = []
    for copy in copies:
        copy.wait()


def local(keys_a, values_a, queries_b, grad_out, state_start, state_next):
    n, n_dp = lax.axis_size("ctx"), lax.axis_size("dp")
    _, heads, rows, width = state_start.shape
    t = keys_a.shape[1]
    plan = Plan(n, n_dp, t, heads, rows, width)
    per, mats, own = plan.per, plan.mats, plan.own
    bind = lambda kernel: functools.partial(kernel, plan=plan)

    slot_ids = jnp.bitwise_xor(lax.axis_index("ctx"), jnp.arange(n, dtype=jnp.int32))
    head_ids = jnp.minimum(slot_ids * per, heads - per)
    dp_id = lax.axis_index("dp").reshape(1)
    rest_ids = jnp.bitwise_xor(dp_id // plan.pair, jnp.arange(plan.rest, dtype=jnp.int32))

    def swap(value, axis, size, k):
        if k == 0:
            return value
        return lax.ppermute(value, axis, [(i, i ^ k) for i in range(size)])

    def turn(value):
        return lax.all_to_all(value, "ctx", split_axis=0, concat_axis=0, tiled=True)

    def shape(*dims, dtype=BF16):
        return jax.ShapeDtypeStruct(dims, dtype)

    a_sent = call(
        bind(pack_a_kernel),
        shape(n, 2 * t + plan.share_rows, per * width),
        (dp_id, keys_a, values_a, state_start),
        [SMEM] + [ANY] * 3,
        ANY,
        "pack_a",
        [
            pltpu.VMEM(state_start.shape, F32),
            pltpu.VMEM((n, plan.share_rows, per * width), BF16),
            pltpu.SemaphoreType.DMA((3 * n + 1,)),
        ],
        vmem=VMEM_WHOLE,
    )
    a_in = turn(a_sent)
    b_sent = call(
        bind(pack_b_kernel),
        [shape(2 * t + 3 * plan.block, per * width)] * n,
        (head_ids, queries_b, grad_out, state_next),
        [SMEM] + [ANY] * 3,
        [VMEM] * n,
        "pack_b",
        [pltpu.VMEM(state_next.shape, F32), pltpu.SemaphoreType.DMA((2 * n + 1,))],
    )
    b_in = [swap(b_sent[s], "ctx", n, s) for s in range(n)]
    start_own = call(
        bind(start_kernel),
        shape(plan.share, width, width),
        (a_in,),
        [VMEM],
        VMEM,
        "start_share",
        [pltpu.VMEM((plan.share, width, width), F32)],
    )
    shares = [swap(start_own, "dp", n_dp, k) for k in range(plan.group)]
    firsts = call(
        bind(first_kernel),
        [
            shape(plan.group * plan.share, width, width),
            shape(per, 3, n * t, width, dtype=F32),
            shape(per, 3, n * t, width),
            shape(mats, width, width, dtype=F32),
        ]
        + [shape(mats, width, width)] * (3 * STEPS),
        (dp_id, a_in, *shares),
        [SMEM] + [VMEM] * (1 + plan.group),
        [VMEM] * (4 + 3 * STEPS),
        "first",
        flops=per * 160 * 10**6,
        size=per * 10**6,
    )
    d_sent, c_keep, c_send = call(
        bind(second_kernel),
        [
            shape(n, 2 * t, per * width),
            shape(plan.rest * own, width, width),
            shape(plan.rest * own, width, width),
        ],
        (slot_ids, dp_id, a_in, *firsts, *b_in),
        [SMEM] * 2 + [VMEM] * (5 + 3 * STEPS + n),
        [VMEM] * 3,
        "second",
        [
            pltpu.VMEM((mats, width, width), F32),
            pltpu.VMEM((mats, width, width), F32),
            pltpu.VMEM((n_dp * own, width, width), BF16),
        ],
        flops=per * 400 * 10**6,
        size=per * 10**6,
    )
    back = turn(d_sent)

    halves = call(
        bind(pair_kernel),
        [shape(own, width, width)] * plan.rest,
        (dp_id, c_keep, swap(c_send, "dp", n_dp, plan.pair - 1)),
        [SMEM] + [VMEM] * 2,
        [VMEM] * plan.rest,
        "state_pair",
        [pltpu.VMEM((plan.rest * own, width, width), F32)],
    )
    halves = [swap(halves[k], "dp", n_dp, plan.pair * k) for k in range(plan.rest)]
    by_rows = call(
        bind(sum_kernel),
        [shape(own, rows, width)] * n,
        (slot_ids, *halves),
        [SMEM] + [VMEM] * plan.rest,
        [VMEM] * n,
        "state_sum",
        [pltpu.VMEM((own, width, width), F32)],
    )
    by_rows = [swap(by_rows[s], "ctx", n, s) for s in range(n)]
    mine = call(
        bind(order_kernel),
        shape(n, own, rows, width),
        (slot_ids, *by_rows),
        [SMEM] + [VMEM] * n,
        VMEM,
        "state_rows",
    )
    rest = [swap(mine, "dp", n_dp, plan.pair * k) for k in range(plan.rest)]
    half = call(
        bind(order_kernel),
        shape(plan.rest, n, own, rows, width),
        (rest_ids, *rest),
        [SMEM] + [VMEM] * plan.rest,
        VMEM,
        "state_rest",
    )
    both = [swap(half, "dp", n_dp, k) for k in range(plan.pair)]
    grad_state = call(
        bind(state_kernel),
        shape(*state_start.shape, dtype=F32),
        (dp_id, *both),
        [SMEM] + [VMEM] * plan.pair,
        VMEM,
        "state_out",
    )
    grad_keys, grad_values = call(
        bind(unpack_kernel),
        [shape(*keys_a.shape), shape(*values_a.shape)],
        (back,),
        [VMEM],
        [ANY] * 2,
        "unpack",
        [pltpu.SemaphoreType.DMA((2 * n,))],
    )
    return grad_keys, grad_values, grad_state


def solution(mesh):
    placed = (
        P("dp", "ctx", None),
        P("dp", "ctx", None),
        P("dp", "ctx", None),
        P("dp", "ctx", None),
        P(None, None, "ctx", None),
        P("dp", None, None, "ctx", None),
    )
    return jax.shard_map(
        local,
        mesh=mesh,
        in_specs=placed,
        out_specs=(P("dp", "ctx", None), P("dp", "ctx", None), P(None, None, "ctx", None)),
        check_vma=False,
    )
```

```python
import functools

import jax
import jax.numpy as jnp
from jax import lax
from jax.experimental import pallas as pl
from jax.experimental.pallas import tpu as pltpu
from jax.sharding import PartitionSpec as P

RATE = 4.0
CA = 3.4445
CB = -4.775
CC = 2.0315
STEPS = 2
F32 = jnp.float32
BF16 = jnp.bfloat16
VMEM_LIMIT = 28 * 1024 * 1024
VMEM_WHOLE = 58 * 1024 * 1024
SMEM = pl.BlockSpec(memory_space=pltpu.SMEM)
VMEM = pl.BlockSpec(memory_space=pltpu.VMEM)
ANY = pl.BlockSpec(memory_space=pl.ANY)


def dot_nn(a, b):
    return lax.dot_general(a, b, (((1,), (0,)), ((), ())), preferred_element_type=F32)


def dot_nt(a, b):
    return lax.dot_general(a, b, (((1,), (1,)), ((), ())), preferred_element_type=F32)


def dot_tn(a, b):
    return lax.dot_general(a, b, (((0,), (0,)), ((), ())), preferred_element_type=F32)


def call(
    kernel, out_shape, args, in_specs, out_specs, name, scratch=(), flops=10**6, size=10**6, vmem=VMEM_LIMIT
):
    return pl.pallas_call(
        kernel,
        out_shape=out_shape,
        in_specs=in_specs,
        out_specs=out_specs,
        scratch_shapes=list(scratch),
        compiler_params=pltpu.CompilerParams(vmem_limit_bytes=vmem),
        cost_estimate=pl.CostEstimate(flops=flops, bytes_accessed=size, transcendentals=0),
        name=name,
    )(*args)


def swish_terms(g):
    s = 1.0 / (1.0 + jnp.exp(-g))
    sw = g * s
    slope = s * (1.0 + g * (1.0 - s))
    return s, sw, slope


def newton_forward(grads):
    each = range(len(grads))
    inv = [lax.rsqrt(jnp.sum(g * g, keepdims=True) + 1e-06) for g in grads]
    x = [(grads[m] * inv[m]).astype(BF16) for m in each]
    kept = []
    for step in range(STEPS):
        gram = [dot_nt(x[m], x[m]).astype(BF16) for m in each]
        poly = [(CB * gram[m].astype(F32) + CC * dot_nn(gram[m], gram[m])).astype(BF16) for m in each]
        kept.append((x, gram, poly))
        if step + 1 < STEPS:
            x = [(CA * x[m].astype(F32) + dot_nn(poly[m], x[m])).astype(BF16) for m in each]
    return kept


def newton_pullback(grads, kept, updates):
    each = range(len(grads))
    d = updates
    for x, gram, poly in reversed(kept):
        dp = [dot_nt(d[m], x[m]) for m in each]
        sym = [dp[m] + dp[m].T for m in each]
        turned = [dot_nn(sym[m].astype(BF16), gram[m]) for m in each]
        da = [(CB * sym[m] + CC * (turned[m] + turned[m].T)).astype(BF16) for m in each]
        d = [
            (CA * d[m].astype(F32) + dot_nn(poly[m], d[m]) + dot_nn(da[m], x[m])).astype(BF16)
            for m in each
        ]
    out = []
    for m in each:
        df = d[m].astype(F32)
        inv = lax.rsqrt(jnp.sum(grads[m] * grads[m], keepdims=True) + 1e-06)
        along = jnp.sum(df * grads[m], keepdims=True)
        out.append(df * inv - grads[m] * (along * (inv * inv * inv)))
    return out


class Plan:
    def __init__(self, n, n_dp, tokens, heads, rows, width):
        self.n, self.n_dp = n, n_dp
        self.tokens, self.heads, self.rows, self.width = tokens, heads, rows, width
        self.per = -(-heads // n)
        self.mats = 3 * self.per
        early = (self.per + 1) // 2
        self.chunks = [c for c in ((0, early), (early, self.per - early)) if c[1] > 0]
        self.group = min(4, n_dp)
        self.share = -(-self.mats // self.group)
        self.pair = min(2, n_dp)
        self.rest = n_dp // self.pair
        self.own = -(-self.mats // n_dp)
        self.block = -(-rows // 16) * 16
        self.share_rows = -(-self.share // self.per) * self.block

    def first_head(self, c):
        return min(c * self.per, self.heads - self.per)


def pack_a_kernel(head_ref, dp_ref, k_ref, v_ref, s_ref, *refs, plan):
    n, t, w, per = plan.n, plan.tokens, plan.width, plan.per
    outs, (state, sems) = refs[:n], refs[n:]
    load = pltpu.make_async_copy(s_ref, state, sems.at[2 * n])
    load.start()
    copies = []
    for slot in range(n):
        cols = pl.ds(pl.multiple_of(head_ref[slot] * w, w), per * w)
        for part, src in enumerate((k_ref, v_ref)):
            copy = pltpu.make_async_copy(
                src.at[0, :, cols], outs[slot].at[pl.ds(part * t, t), :], sems.at[2 * slot + part]
            )
            copy.start()
            copies.append(copy)
    load.wait()
    low = dp_ref[0] % plan.group
    for q in range(plan.share):
        mat = jnp.minimum(low * plan.share + q, plan.mats - 1)
        for slot in range(n):
            part = state[mat % 3, head_ref[slot] + mat // 3].astype(BF16)
            top = 2 * t + (q // per) * plan.block
            left = (q % per) * w
            outs[slot][top : top + plan.rows, left : left + w] = part
    for copy in copies:
        copy.wait()


def pack_b_kernel(head_ref, q_ref, o_ref, s_ref, *refs, plan, chunk):
    n, t, w = plan.n, plan.tokens, plan.width
    first, count = plan.chunks[chunk]
    outs, (state, sems) = refs[:-2], refs[-2:]
    if len(outs) < n:
        outs = [outs[0].at[c] for c in range(n)]
        heads = [plan.first_head(c) + first for c in range(n)]
        offsets = [head * w for head in heads]
    else:
        heads = [head_ref[slot] + first for slot in range(n)]
        offsets = [pl.multiple_of(head * w, w) for head in heads]
    load = pltpu.make_async_copy(s_ref, state, sems.at[2 * n])
    load.start()
    copies = []
    for k in range(n):
        for part, src in enumerate((q_ref, o_ref)):
            copy = pltpu.make_async_copy(
                src.at[0, :, pl.ds(offsets[k], count * w)],
                outs[k].at[pl.ds(part * t, t), :],
                sems.at[2 * k + part],
            )
            copy.start()
            copies.append(copy)
    load.wait()
    for k in range(n):
        for j in range(count):
            for m in range(3):
                top = 2 * t + m * plan.block
                outs[k][top : top + plan.rows, j * w : (j + 1) * w] = state[0, m, heads[k] + j].astype(BF16)
    for copy in copies:
        copy.wait()


def start_kernel(from_ref, *refs, plan):
    rows, w = plan.rows, plan.width
    a_refs, (out, whole) = refs[: plan.n], refs[plan.n :]
    for slot in range(plan.n):
        at = pl.ds(pl.multiple_of(from_ref[slot] * rows, rows), rows)
        for q in range(plan.share):
            top = 2 * plan.tokens + (q // plan.per) * plan.block
            left = (q % plan.per) * w
            whole[q, at, :] = a_refs[slot][top : top + rows, left : left + w].astype(F32)
    out[...] = whole[...].astype(BF16)


def forward(x, y, wa, wb, wc):
    w = wa.shape[1]
    gu = dot_nn(x, jnp.concatenate([wa, wb], axis=1))
    g, u = gu[:, :w], gu[:, w:]
    p = dot_nn(y, wc)
    _, sw, slope = swish_terms(g)
    hidden = (sw * u).astype(BF16)
    dg = (p * u * slope).astype(BF16)
    du = (p * sw).astype(BF16)
    ab = dot_tn(x, jnp.concatenate([dg, du], axis=1))
    return (ab[:, :w], ab[:, w:], dot_tn(y, hidden)), (g, u, p), (dg, du, hidden)


def tokens_of(refs, j, plan):
    t, w = plan.tokens, plan.width
    cols = slice(j * w, (j + 1) * w)
    x = jnp.concatenate([r[0:t, cols] for r in refs], axis=0)
    y = jnp.concatenate([r[t : 2 * t, cols] for r in refs], axis=0)
    return x, y


def first_kernel(dp_ref, *refs, plan):
    a_refs, refs = refs[: plan.n], refs[plan.n :]
    shares, (w0, acts, fields, gsum, *kept) = refs[: plan.group], refs[plan.group :]
    low = dp_ref[0] % plan.group
    for k in range(plan.group):
        at = pl.ds(jnp.bitwise_xor(low, k) * plan.share, plan.share)
        w0[at] = shares[k][...]
    for j in range(plan.per):
        x, y = tokens_of(a_refs, j, plan)
        sums, act, field = forward(x, y, w0[3 * j], w0[3 * j + 1], w0[3 * j + 2])
        for m in range(3):
            gsum[3 * j + m] = sums[m]
            acts[j, m] = act[m]
            fields[j, m] = field[m]
    states = newton_forward([gsum[m] for m in range(plan.mats)])
    for ref, values in zip(kept, [v for state in states for v in state]):
        for m in range(plan.mats):
            ref[m] = values[m]


def second_kernel(from_ref, dp_ref, *refs, plan, chunk):
    n, t, w = plan.n, plan.tokens, plan.width
    first, count = plan.chunks[chunk]
    last = chunk + 1 == len(plan.chunks)
    mats = 3 * count
    refs = list(refs)

    def take(k):
        got = refs[:k]
        del refs[:k]
        return got

    a_refs, (w0, acts, fields, gsum), kept = take(n), take(4), take(3 * STEPS)
    joined = len(refs[0].shape) == 3
    b_refs = take(1 if joined else n)
    if joined:
        b_refs = [b_refs[0].at[c] for c in range(n)]
        sources = list(range(n))
    else:
        sources = [from_ref[slot] for slot in range(n)]
    before = take(chunk) if last else []
    (d_ref,) = take(1)
    c_refs = take(2 if last else 1)
    w1, ssum = take(2)
    total = take(1)[0] if last else c_refs[0]
    base = 3 * first if last else 0

    for slot in range(n):
        row = sources[slot] * plan.rows
        at = pl.ds(row if joined else pl.multiple_of(row, plan.rows), plan.rows)
        for j in range(count):
            for m in range(3):
                top = 2 * t + m * plan.block
                part = b_refs[slot][top : top + plan.rows, j * w : (j + 1) * w]
                w1[3 * j + m, at, :] = part.astype(F32)
    for j in range(count):
        x, y = tokens_of(b_refs, j, plan)
        sums, _, _ = forward(x, y, *[w1[3 * j + m].astype(BF16) for m in range(3)])
        for m in range(3):
            ssum[3 * j + m] = sums[m]

    span = range(3 * first, 3 * (first + count))
    states = [
        tuple([kept[3 * step + i][m] for m in span] for i in range(3)) for step in range(STEPS)
    ]
    updates = [(RATE * ssum[m]).astype(BF16) for m in range(mats)]
    field_grads = newton_pullback([gsum[m] for m in span], states, updates)
    for m in range(mats):
        w1[m] = field_grads[m]

    for j in range(count):
        head = first + j
        x, y = tokens_of(a_refs, head, plan)
        fab = jnp.concatenate([w1[3 * j], w1[3 * j + 1]], axis=1).astype(BF16)
        fc = w1[3 * j + 2].astype(BF16)
        wab = jnp.concatenate([w0[3 * head], w0[3 * head + 1]], axis=1)
        wc = w0[3 * head + 2]
        cdgu = dot_nn(x, fab)
        cdg, cdu = cdgu[:, :w], cdgu[:, w:]
        ch = dot_nn(y, fc)
        g, u, p = acts[head, 0], acts[head, 1], acts[head, 2]
        s, sw, slope = swish_terms(g)
        curve = s * (1.0 - s) * (2.0 + g * (1.0 - 2.0 * s))
        cg = ((ch * u + cdu * p) * slope + cdg * (p * u) * curve).astype(BF16)
        cu = (ch * sw + cdg * p * slope).astype(BF16)
        cp = (cdu * sw + cdg * u * slope).astype(BF16)
        dg, du, hidden = fields[head, 0], fields[head, 1], fields[head, 2]
        dx = dot_nt(jnp.concatenate([dg, du, cg, cu], axis=1), jnp.concatenate([fab, wab], axis=1))
        dy = dot_nt(jnp.concatenate([hidden, cp], axis=1), jnp.concatenate([fc, wc], axis=1))
        cols = slice(j * w, (j + 1) * w)
        for slot in range(n):
            to = from_ref[slot]
            d_ref[to, 0:t, cols] = dx[slot * t : (slot + 1) * t].astype(BF16)
            d_ref[to, t : 2 * t, cols] = dy[slot * t : (slot + 1) * t].astype(BF16)
        ab = dot_tn(x, jnp.concatenate([cg, cu], axis=1))
        grown = (ab[:, :w], ab[:, w:], dot_tn(y, cp))
        for m in range(3):
            total[base + 3 * j + m] = (ssum[3 * j + m] + grown[m]).astype(BF16)

    if last:
        for c, part in enumerate(before):
            at = 3 * plan.chunks[c][0]
            total[at : at + part.shape[0]] = part[...]
        for m in range(plan.mats, plan.n_dp * plan.own):
            total[m] = jnp.zeros((w, w), BF16)
        mine = dp_ref[0] % plan.pair
        for r in range(plan.rest):
            to = slice(r * plan.own, (r + 1) * plan.own)
            for ref, which in zip(c_refs, (mine, plan.pair - 1 - mine)):
                ref[to] = total[pl.ds((plan.pair * r + which) * plan.own, plan.own)]


def pair_kernel(dp_ref, keep_ref, got_ref, *refs, plan):
    outs, whole = refs[:-1], refs[-1]
    whole[...] = keep_ref[...].astype(F32) + got_ref[...].astype(F32)
    place = dp_ref[0] // plan.pair
    for k in range(plan.rest):
        at = pl.ds(jnp.bitwise_xor(place, k) * plan.own, plan.own)
        outs[k][...] = whole[at].astype(BF16)


def sum_kernel(to_ref, *refs, plan):
    parts, outs, whole = refs[: plan.rest], refs[plan.rest : -1], refs[-1]
    added = parts[0][...].astype(F32)
    for part in parts[1:]:
        added = added + part[...].astype(F32)
    whole[...] = added / plan.n_dp
    for slot in range(plan.n):
        at = pl.ds(pl.multiple_of(to_ref[slot] * plan.rows, plan.rows), plan.rows)
        outs[slot][...] = whole[:, at, :].astype(BF16)


def order_kernel(place_ref, *refs, plan):
    parts, out = refs[:-1], refs[-1]
    for k, part in enumerate(parts):
        out[place_ref[k]] = part[...]


def state_kernel(dp_ref, *refs, plan):
    out = refs[-1]
    mine = dp_ref[0] % plan.pair
    for k in range(plan.pair):
        for r in range(plan.rest):
            for i in range(plan.own):
                mat = (plan.pair * r + jnp.bitwise_xor(mine, k)) * plan.own + i

                @pl.when(mat < plan.mats)
                def _(mat=mat, ref=refs[k], r=r, i=i):
                    for c in range(plan.n):
                        out[mat % 3, plan.first_head(c) + mat // 3] = ref[r, c, i].astype(F32)


def unpack_kernel(*refs, plan):
    t, w = plan.tokens, plan.width
    ins, (dk, dv, sems) = refs[:-3], refs[-3:]
    copies = []
    for c, (first, count) in enumerate(plan.chunks):
        for owner in range(plan.n):
            cols = pl.ds((plan.first_head(owner) + first) * w, count * w)
            for part, dst in enumerate((dk, dv)):
                copy = pltpu.make_async_copy(
                    ins[c].at[owner, pl.ds(part * t, t), :],
                    dst.at[0, :, cols],
                    sems.at[(c * plan.n + owner) * 2 + part],
                )
                copy.start()
                copies.append(copy)
            if plan.n * plan.per != plan.heads:
                for copy in copies:
                    copy.wait()
                copies = []
    for copy in copies:
        copy.wait()


def local(keys_a, values_a, queries_b, grad_out, state_start, state_next):
    n, n_dp = lax.axis_size("ctx"), lax.axis_size("dp")
    _, heads, rows, width = state_start.shape
    t = keys_a.shape[1]
    plan = Plan(n, n_dp, t, heads, rows, width)
    per, mats, own, chunks = plan.per, plan.mats, plan.own, plan.chunks
    bind = lambda kernel, **more: functools.partial(kernel, plan=plan, **more)

    me = lax.axis_index("ctx")
    places = jnp.arange(n, dtype=jnp.int32)
    to_ids = lax.rem(me + places, n)
    from_ids = lax.rem(me + n - places, n)
    head_ids = jnp.minimum(to_ids * per, heads - per)
    dp_id = lax.axis_index("dp").reshape(1)
    rest_ids = jnp.bitwise_xor(lax.div(dp_id, plan.pair), jnp.arange(plan.rest, dtype=jnp.int32))

    def swap(value, k):
        if k == 0:
            return value
        return lax.ppermute(value, "dp", [(i, i ^ k) for i in range(n_dp)])

    def shift(values):
        return [
            lax.ppermute(v, "ctx", [(i, (i + s) % n) for i in range(n)]) if s else v
            for s, v in enumerate(values)
        ]

    def turn(value):
        return lax.all_to_all(value, "ctx", split_axis=0, concat_axis=0, tiled=True)

    def shape(*dims, dtype=BF16):
        return jax.ShapeDtypeStruct(dims, dtype)

    a_in = shift(
        call(
            bind(pack_a_kernel),
            [shape(2 * t + plan.share_rows, per * width)] * n,
            (head_ids, dp_id, keys_a, values_a, state_start),
            [SMEM] * 2 + [ANY] * 3,
            [VMEM] * n,
            "pack_a",
            [pltpu.VMEM(state_start.shape, F32), pltpu.SemaphoreType.DMA((2 * n + 1,))],
            vmem=VMEM_WHOLE,
        )
    )
    b_in = []
    for c, (_, count) in enumerate(chunks):
        joined = c == 0
        dims = (2 * t + 3 * plan.block, count * width)
        sent = call(
            bind(pack_b_kernel, chunk=c),
            [shape(n, *dims)] if joined else [shape(*dims)] * n,
            (head_ids, queries_b, grad_out, state_next),
            [SMEM] + [ANY] * 3,
            [VMEM] * (1 if joined else n),
            f"pack_b{c}",
            [pltpu.VMEM(state_next.shape, F32), pltpu.SemaphoreType.DMA((2 * n + 1,))],
        )
        b_in.append([turn(sent[0])] if joined else shift(sent))
    start_own = call(
        bind(start_kernel),
        shape(plan.share, width, width),
        (from_ids, *a_in),
        [SMEM] + [VMEM] * n,
        VMEM,
        "start_share",
        [pltpu.VMEM((plan.share, width, width), F32)],
    )
    shares = [swap(start_own, k) for k in range(plan.group)]
    firsts = call(
        bind(first_kernel),
        [
            shape(plan.group * plan.share, width, width),
            shape(per, 3, n * t, width, dtype=F32),
            shape(per, 3, n * t, width),
            shape(mats, width, width, dtype=F32),
        ]
        + [shape(mats, width, width)] * (3 * STEPS),
        (dp_id, *a_in, *shares),
        [SMEM] + [VMEM] * (n + plan.group),
        [VMEM] * (4 + 3 * STEPS),
        "first",
        flops=per * 160 * 10**6,
        size=per * 10**6,
    )
    d_sent = []
    sums = []
    for c, (_, count) in enumerate(chunks):
        last = c + 1 == len(chunks)
        if last:
            c_shapes = [shape(plan.rest * own, width, width)] * 2
            scratch = [pltpu.VMEM((n_dp * own, width, width), BF16)]
        else:
            c_shapes = [shape(3 * count, width, width)]
            scratch = []
        before = sums if last else []
        outs = call(
            bind(second_kernel, chunk=c),
            [shape(n, 2 * t, count * width)] + c_shapes,
            (from_ids, dp_id, *a_in, *firsts, *b_in[c], *before),
            [SMEM] * 2 + [VMEM] * (n + 4 + 3 * STEPS + len(b_in[c]) + len(before)),
            [VMEM] * (1 + len(c_shapes)),
            f"second{c}",
            [pltpu.VMEM((3 * count, width, width), F32)] * 2 + scratch,
            flops=count * 400 * 10**6,
            size=count * 10**6,
        )
        d_sent.append(outs[0])
        sums = outs[1:]
    c_keep, c_send = sums

    halves = call(
        bind(pair_kernel),
        [shape(own, width, width)] * plan.rest,
        (dp_id, c_keep, swap(c_send, plan.pair - 1)),
        [SMEM] + [VMEM] * 2,
        [VMEM] * plan.rest,
        "state_pair",
        [pltpu.VMEM((plan.rest * own, width, width), F32)],
    )
    halves = [swap(halves[k], plan.pair * k) for k in range(plan.rest)]
    by_rows = call(
        bind(sum_kernel),
        [shape(own, rows, width)] * n,
        (to_ids, *halves),
        [SMEM] + [VMEM] * plan.rest,
        [VMEM] * n,
        "state_sum",
        [pltpu.VMEM((own, width, width), F32)],
    )
    mine = call(
        bind(order_kernel),
        shape(n, own, rows, width),
        (from_ids, *shift(by_rows)),
        [SMEM] + [VMEM] * n,
        VMEM,
        "state_rows",
    )
    back = [turn(d) for d in d_sent[:-1]]
    mine, late = lax.optimization_barrier((mine, d_sent[-1]))
    back.append(turn(late))
    rest = [swap(mine, plan.pair * k) for k in range(plan.rest)]
    half = call(
        bind(order_kernel),
        shape(plan.rest, n, own, rows, width),
        (rest_ids, *rest),
        [SMEM] + [VMEM] * plan.rest,
        VMEM,
        "state_rest",
    )
    both = [swap(half, k) for k in range(plan.pair)]
    grad_state = call(
        bind(state_kernel),
        shape(*state_start.shape, dtype=F32),
        (dp_id, *both),
        [SMEM] + [VMEM] * plan.pair,
        VMEM,
        "state_out",
    )
    grad_keys, grad_values = call(
        bind(unpack_kernel),
        [shape(*keys_a.shape), shape(*values_a.shape)],
        back,
        [VMEM] * len(back),
        [ANY] * 2,
        "unpack",
        [pltpu.SemaphoreType.DMA((2 * n * len(chunks),))],
    )
    return grad_keys, grad_values, grad_state


def solution(mesh):
    placed = (
        P("dp", "ctx", None),
        P("dp", "ctx", None),
        P("dp", "ctx", None),
        P("dp", "ctx", None),
        P(None, None, "ctx", None),
        P("dp", None, None, "ctx", None),
    )
    return jax.shard_map(
        local,
        mesh=mesh,
        in_specs=placed,
        out_specs=(P("dp", "ctx", None), P("dp", "ctx", None), P(None, None, "ctx", None)),
        check_vma=False,
    )
```

```python
import functools

import jax
import jax.numpy as jnp
from jax import lax
from jax.experimental import pallas as pl
from jax.experimental.pallas import tpu as pltpu
from jax.sharding import PartitionSpec as P

RATE = 4.0
CA = 3.4445
CB = -4.775
CC = 2.0315
STEPS = 2
F32 = jnp.float32
BF16 = jnp.bfloat16
VMEM_SMALL = 8 * 1024 * 1024
VMEM_LARGE = 28 * 1024 * 1024
SMEM = pl.BlockSpec(memory_space=pltpu.SMEM)
VMEM = pl.BlockSpec(memory_space=pltpu.VMEM)
ANY = pl.BlockSpec(memory_space=pl.ANY)
HBM = pl.BlockSpec(memory_space=pltpu.HBM)


def dot_nn(a, b):
    return lax.dot_general(a, b, (((1,), (0,)), ((), ())), preferred_element_type=F32)


def dot_nt(a, b):
    return lax.dot_general(a, b, (((1,), (1,)), ((), ())), preferred_element_type=F32)


def dot_tn(a, b):
    return lax.dot_general(a, b, (((0,), (0,)), ((), ())), preferred_element_type=F32)


def call(
    kernel, out_shape, args, in_specs, out_specs, name, scratch=(), flops=10**6, size=10**6, vmem=VMEM_SMALL
):
    return pl.pallas_call(
        kernel,
        out_shape=out_shape,
        in_specs=in_specs,
        out_specs=out_specs,
        scratch_shapes=list(scratch),
        compiler_params=pltpu.CompilerParams(vmem_limit_bytes=vmem),
        cost_estimate=pl.CostEstimate(flops=flops, bytes_accessed=size, transcendentals=0),
        name=name,
    )(*args)


def swish_terms(g):
    s = 1.0 / (1.0 + jnp.exp(-g))
    sw = g * s
    slope = s * (1.0 + g * (1.0 - s))
    return s, sw, slope


def newton_pullback(grads, updates):
    each = range(len(grads))
    inv = [lax.rsqrt(jnp.sum(g * g, keepdims=True) + 1e-06) for g in grads]
    xs = [[(grads[m] * inv[m]).astype(BF16) for m in each]]
    grams = []
    polys = []
    for step in range(STEPS):
        x = xs[-1]
        gram = [dot_nt(x[m], x[m]).astype(BF16) for m in each]
        poly = [(CB * gram[m].astype(F32) + CC * dot_nn(gram[m], gram[m])).astype(BF16) for m in each]
        grams.append(gram)
        polys.append(poly)
        if step + 1 < STEPS:
            xs.append([(CA * x[m].astype(F32) + dot_nn(poly[m], x[m])).astype(BF16) for m in each])
    d = updates
    for step in reversed(range(STEPS)):
        x, gram, poly = xs[step], grams[step], polys[step]
        dp = [dot_nt(d[m], x[m]) for m in each]
        sym = [dp[m] + dp[m].T for m in each]
        turned = [dot_nn(sym[m].astype(BF16), gram[m]) for m in each]
        da = [(CB * sym[m] + CC * (turned[m] + turned[m].T)).astype(BF16) for m in each]
        d = [
            (CA * d[m].astype(F32) + dot_nn(poly[m], d[m]) + dot_nn(da[m], x[m])).astype(BF16)
            for m in each
        ]
    out = []
    for m in each:
        df = d[m].astype(F32)
        along = jnp.sum(df * grads[m], keepdims=True)
        out.append(df * inv[m] - grads[m] * (along * (inv[m] * inv[m] * inv[m])))
    return out


class Plan:
    def __init__(self, n, n_dp, tokens, heads, rows, width):
        self.n, self.n_dp = n, n_dp
        self.tokens, self.heads, self.rows, self.width = tokens, heads, rows, width
        self.per = -(-heads // n)
        self.mats = 3 * self.per
        early = (self.per + 1) // 2
        self.chunks = [c for c in ((0, early), (early, self.per - early)) if c[1] > 0]
        self.group = min(4, n_dp)
        self.share = -(-self.mats // self.group)
        self.pair = min(2, n_dp)
        self.rest = n_dp // self.pair
        self.own = -(-self.mats // n_dp)
        self.block = -(-rows // 16) * 16
        self.share_rows = -(-self.share // self.per) * self.block

    def first_head(self, c):
        return min(c * self.per, self.heads - self.per)


def pack_a_kernel(head_ref, dp_ref, k_ref, v_ref, s_ref, out, state, sems, *, plan, slot):
    t, w, per = plan.tokens, plan.width, plan.per
    low = lax.rem(dp_ref[0], plan.group)
    head = head_ref[slot]
    loads = []
    for q in range(plan.share):
        mat = jnp.minimum(low * plan.share + q, plan.mats - 1)
        load = pltpu.make_async_copy(
            s_ref.at[lax.rem(mat, 3), head + lax.div(mat, 3)], state.at[q], sems.at[2 + q]
        )
        load.start()
        loads.append(load)
    cols = pl.ds(pl.multiple_of(head * w, w), per * w)
    copies = []
    for part, src in enumerate((k_ref, v_ref)):
        copy = pltpu.make_async_copy(src.at[0, :, cols], out.at[pl.ds(part * t, t), :], sems.at[part])
        copy.start()
        copies.append(copy)
    for load in loads:
        load.wait()
    for q in range(plan.share):
        top = 2 * t + (q // per) * plan.block
        left = (q % per) * w
        out[top : top + plan.rows, left : left + w] = state[q].astype(BF16)
    for copy in copies:
        copy.wait()


def pack_b_kernel(head_ref, q_ref, o_ref, s_ref, *refs, plan, chunk):
    n, t, w = plan.n, plan.tokens, plan.width
    first, count = plan.chunks[chunk]
    outs, (state, sems) = refs[:-2], refs[-2:]
    if len(outs) < n:
        outs = [outs[0].at[c] for c in range(n)]
        heads = [plan.first_head(c) + first for c in range(n)]
        offsets = [head * w for head in heads]
    else:
        heads = [head_ref[slot] + first for slot in range(n)]
        offsets = [pl.multiple_of(head * w, w) for head in heads]
    loads = []
    copies = []
    for k in range(n):
        load = pltpu.make_async_copy(
            s_ref.at[0, :, pl.ds(heads[k], count)], state.at[k], sems.at[3 * k + 2]
        )
        load.start()
        loads.append(load)
        for part, src in enumerate((q_ref, o_ref)):
            copy = pltpu.make_async_copy(
                src.at[0, :, pl.ds(offsets[k], count * w)],
                outs[k].at[pl.ds(part * t, t), :],
                sems.at[3 * k + part],
            )
            copy.start()
            copies.append(copy)
    for k in range(n):
        loads[k].wait()
        for j in range(count):
            for m in range(3):
                top = 2 * t + m * plan.block
                outs[k][top : top + plan.rows, j * w : (j + 1) * w] = state[k, m, j].astype(BF16)
    for copy in copies:
        copy.wait()


def start_kernel(from_ref, *refs, plan):
    rows, w = plan.rows, plan.width
    a_refs, (out, whole) = refs[: plan.n], refs[plan.n :]
    for slot in range(plan.n):
        at = pl.ds(pl.multiple_of(from_ref[slot] * rows, rows), rows)
        for q in range(plan.share):
            top = 2 * plan.tokens + (q // plan.per) * plan.block
            left = (q % plan.per) * w
            whole[q, at, :] = a_refs[slot][top : top + rows, left : left + w].astype(F32)
    out[...] = whole[...].astype(BF16)


def tokens_of(refs, j, plan):
    t, w = plan.tokens, plan.width
    cols = slice(j * w, (j + 1) * w)
    x = jnp.concatenate([r[0:t, cols] for r in refs], axis=0)
    y = jnp.concatenate([r[t : 2 * t, cols] for r in refs], axis=0)
    return x, y


def forward(x, y, wa, wb, wc):
    w = wa.shape[1]
    gu = dot_nn(x, jnp.concatenate([wa, wb], axis=1))
    g, u = gu[:, :w], gu[:, w:]
    p = dot_nn(y, wc)
    _, sw, slope = swish_terms(g)
    hidden = (sw * u).astype(BF16)
    dg = (p * u * slope).astype(BF16)
    du = (p * sw).astype(BF16)
    ab = dot_tn(x, jnp.concatenate([dg, du], axis=1))
    return (ab[:, :w], ab[:, w:], dot_tn(y, hidden)), (g, u, p), (dg, du, hidden)


def chunk_kernel(from_ref, dp_ref, *refs, plan, chunk):
    n, t, w = plan.n, plan.tokens, plan.width
    first, count = plan.chunks[chunk]
    last = chunk + 1 == len(plan.chunks)
    mats = 3 * count
    refs = list(refs)

    def take(k):
        got = refs[:k]
        del refs[:k]
        return got

    a_refs, shares = take(n), take(plan.group)
    joined = len(refs[0].shape) == 3
    b_refs = take(1 if joined else n)
    if joined:
        b_refs = [b_refs[0].at[c] for c in range(n)]
        sources = list(range(n))
    else:
        sources = [from_ref[slot] for slot in range(n)]
    before = take(chunk) if last else []
    (d_ref,) = take(1)
    c_refs = take(2 if last else 1)
    w0, w1, gsum, ssum, acts, fields = take(6)
    total = take(1)[0] if last else c_refs[0]
    base = 3 * first if last else 0

    low = lax.rem(dp_ref[0], plan.group)
    for k in range(plan.group):
        at = pl.ds(jnp.bitwise_xor(low, k) * plan.share, plan.share)
        w0[at] = shares[k][...]
    for slot in range(n):
        row = sources[slot] * plan.rows
        at = pl.ds(row if joined else pl.multiple_of(row, plan.rows), plan.rows)
        for j in range(count):
            for m in range(3):
                top = 2 * t + m * plan.block
                part = b_refs[slot][top : top + plan.rows, j * w : (j + 1) * w]
                w1[3 * j + m, at, :] = part.astype(F32)

    for j in range(count):
        at = 3 * (first + j)
        x, y = tokens_of(a_refs, first + j, plan)
        sums, act, field = forward(x, y, w0[at], w0[at + 1], w0[at + 2])
        for m in range(3):
            gsum[3 * j + m] = sums[m]
            acts[j, m] = act[m]
            fields[j, m] = field[m]
        x, y = tokens_of(b_refs, j, plan)
        sums, _, _ = forward(x, y, *[w1[3 * j + m].astype(BF16) for m in range(3)])
        for m in range(3):
            ssum[3 * j + m] = sums[m]

    grads = [gsum[m] for m in range(mats)]
    updates = [(RATE * ssum[m]).astype(BF16) for m in range(mats)]
    for m, val in enumerate(newton_pullback(grads, updates)):
        gsum[m] = val

    for j in range(count):
        at = 3 * (first + j)
        x, y = tokens_of(a_refs, first + j, plan)
        fab = jnp.concatenate([gsum[3 * j], gsum[3 * j + 1]], axis=1).astype(BF16)
        fc = gsum[3 * j + 2].astype(BF16)
        wab = jnp.concatenate([w0[at], w0[at + 1]], axis=1)
        wc = w0[at + 2]
        cdgu = dot_nn(x, fab)
        cdg, cdu = cdgu[:, :w], cdgu[:, w:]
        ch = dot_nn(y, fc)
        g, u, p = acts[j, 0], acts[j, 1], acts[j, 2]
        s, sw, slope = swish_terms(g)
        curve = s * (1.0 - s) * (2.0 + g * (1.0 - 2.0 * s))
        cg = ((ch * u + cdu * p) * slope + cdg * (p * u) * curve).astype(BF16)
        cu = (ch * sw + cdg * p * slope).astype(BF16)
        cp = (cdu * sw + cdg * u * slope).astype(BF16)
        dg, du, hidden = fields[j, 0], fields[j, 1], fields[j, 2]
        dx = dot_nt(jnp.concatenate([dg, du, cg, cu], axis=1), jnp.concatenate([fab, wab], axis=1))
        dy = dot_nt(jnp.concatenate([hidden, cp], axis=1), jnp.concatenate([fc, wc], axis=1))
        cols = slice(j * w, (j + 1) * w)
        for slot in range(n):
            to = from_ref[slot]
            d_ref[to, 0:t, cols] = dx[slot * t : (slot + 1) * t].astype(BF16)
            d_ref[to, t : 2 * t, cols] = dy[slot * t : (slot + 1) * t].astype(BF16)
        ab = dot_tn(x, jnp.concatenate([cg, cu], axis=1))
        grown = (ab[:, :w], ab[:, w:], dot_tn(y, cp))
        for m in range(3):
            total[base + 3 * j + m] = (ssum[3 * j + m] + grown[m]).astype(BF16)

    if last:
        for c, part in enumerate(before):
            at = 3 * plan.chunks[c][0]
            total[at : at + part.shape[0]] = part[...]
        for m in range(plan.mats, plan.n_dp * plan.own):
            total[m] = jnp.zeros((w, w), BF16)
        mine = lax.rem(dp_ref[0], plan.pair)
        for r in range(plan.rest):
            to = slice(r * plan.own, (r + 1) * plan.own)
            for ref, which in zip(c_refs, (mine, plan.pair - 1 - mine)):
                ref[to] = total[pl.ds((plan.pair * r + which) * plan.own, plan.own)]


def pair_kernel(dp_ref, keep_ref, got_ref, *refs, plan):
    outs, whole = refs[:-1], refs[-1]
    whole[...] = keep_ref[...].astype(F32) + got_ref[...].astype(F32)
    place = lax.div(dp_ref[0], plan.pair)
    for k in range(plan.rest):
        at = pl.ds(jnp.bitwise_xor(place, k) * plan.own, plan.own)
        outs[k][...] = whole[at].astype(BF16)


def sum_kernel(to_ref, *refs, plan):
    parts, outs, whole = refs[: plan.rest], refs[plan.rest : -1], refs[-1]
    added = parts[0][...].astype(F32)
    for part in parts[1:]:
        added = added + part[...].astype(F32)
    whole[...] = added / plan.n_dp
    for slot in range(plan.n):
        at = pl.ds(pl.multiple_of(to_ref[slot] * plan.rows, plan.rows), plan.rows)
        outs[slot][...] = whole[:, at, :].astype(BF16)


def order_kernel(place_ref, *refs, plan):
    parts, out = refs[:-1], refs[-1]
    for k, part in enumerate(parts):
        out[place_ref[k]] = part[...]


def state_kernel(dp_ref, *refs, plan):
    out = refs[-1]
    mine = lax.rem(dp_ref[0], plan.pair)
    for k in range(plan.pair):
        for r in range(plan.rest):
            for i in range(plan.own):
                mat = (plan.pair * r + jnp.bitwise_xor(mine, k)) * plan.own + i

                @pl.when(mat < plan.mats)
                def _(mat=mat, ref=refs[k], r=r, i=i):
                    for c in range(plan.n):
                        out[lax.rem(mat, 3), plan.first_head(c) + lax.div(mat, 3)] = ref[r, c, i].astype(F32)


def unpack_kernel(*refs, plan):
    t, w = plan.tokens, plan.width
    ins, (dk, dv, sems) = refs[:-3], refs[-3:]
    copies = []
    for c, (first, count) in enumerate(plan.chunks):
        for owner in range(plan.n):
            cols = pl.ds((plan.first_head(owner) + first) * w, count * w)
            for part, dst in enumerate((dk, dv)):
                copy = pltpu.make_async_copy(
                    ins[c].at[owner, pl.ds(part * t, t), :],
                    dst.at[0, :, cols],
                    sems.at[(c * plan.n + owner) * 2 + part],
                )
                copy.start()
                copies.append(copy)
            if plan.n * plan.per != plan.heads:
                for copy in copies:
                    copy.wait()
                copies = []
    for copy in copies:
        copy.wait()


def local(keys_a, values_a, queries_b, grad_out, state_start, state_next):
    n, n_dp = lax.axis_size("ctx"), lax.axis_size("dp")
    _, heads, rows, width = state_start.shape
    t = keys_a.shape[1]
    plan = Plan(n, n_dp, t, heads, rows, width)
    per, mats, own, chunks = plan.per, plan.mats, plan.own, plan.chunks
    bind = lambda kernel, **more: functools.partial(kernel, plan=plan, **more)

    keys_a, values_a, grad_out, state_start, state_next = (
        pltpu.with_memory_space_constraint(arg, pltpu.HBM)
        for arg in (keys_a, values_a, grad_out, state_start, state_next)
    )
    me = lax.axis_index("ctx")
    places = jnp.arange(n, dtype=jnp.int32)
    to_ids = lax.rem(me + places, n)
    from_ids = lax.rem(me + n - places, n)
    head_ids = jnp.minimum(to_ids * per, heads - per)
    dp_id = lax.axis_index("dp").reshape(1)
    rest_ids = jnp.bitwise_xor(lax.div(dp_id, plan.pair), jnp.arange(plan.rest, dtype=jnp.int32))

    def swap(value, k):
        if k == 0:
            return value
        return lax.ppermute(value, "dp", [(i, i ^ k) for i in range(n_dp)])

    def shift(values):
        return [
            lax.ppermute(v, "ctx", [(i, (i + s) % n) for i in range(n)]) if s else v
            for s, v in enumerate(values)
        ]

    def turn(value):
        return lax.all_to_all(value, "ctx", split_axis=0, concat_axis=0, tiled=True)

    def shape(*dims, dtype=BF16):
        return jax.ShapeDtypeStruct(dims, dtype)

    def pack_a(slot):
        return call(
            bind(pack_a_kernel, slot=slot),
            shape(2 * t + plan.share_rows, per * width),
            (head_ids, dp_id, keys_a, values_a, state_start),
            [SMEM] * 2 + [HBM] * 3,
            VMEM,
            f"pack_a{slot}",
            [
                pltpu.VMEM((plan.share, rows, width), F32),
                pltpu.SemaphoreType.DMA((2 + plan.share,)),
            ],
        )

    def pack_b(c, queries):
        dims = (2 * t + 3 * plan.block, chunks[c][1] * width)
        joined = c > 0
        return call(
            bind(pack_b_kernel, chunk=c),
            [shape(n, *dims)] if joined else [shape(*dims)] * n,
            (head_ids, pltpu.with_memory_space_constraint(queries, pltpu.HBM), grad_out, state_next),
            [SMEM] + [HBM] * 3,
            [VMEM] * (1 if joined else n),
            f"pack_b{c}",
            [
                pltpu.VMEM((n, 3, chunks[c][1], rows, width), F32),
                pltpu.SemaphoreType.DMA((3 * n,)),
            ],
        )

    a_sent = [pack_a(s) for s in [*range(1, n), 0]]
    a_sent = [a_sent[-1]] + a_sent[:-1]
    queries, a_sent[-1] = lax.optimization_barrier((queries_b, a_sent[-1]))
    a_in = shift(a_sent)
    b_in = [shift(pack_b(0, queries))]
    if len(chunks) > 1:
        queries, a_in[1 % n] = lax.optimization_barrier((queries_b, a_in[1 % n]))
        b_in.append([turn(pack_b(1, queries)[0])])
    start_own = call(
        bind(start_kernel),
        shape(plan.share, width, width),
        (from_ids, *a_in),
        [SMEM] + [VMEM] * n,
        VMEM,
        "start_share",
        [pltpu.VMEM((plan.share, width, width), F32)],
    )
    shares = [swap(start_own, k) for k in range(plan.group)]
    d_sent = []
    sums = []
    for c, (_, count) in enumerate(chunks):
        last = c + 1 == len(chunks)
        if last:
            c_shapes = [shape(plan.rest * own, width, width)] * 2
        else:
            c_shapes = [shape(3 * count, width, width)]
        scratch = [
            pltpu.VMEM((plan.group * plan.share, width, width), BF16),
            pltpu.VMEM((3 * count, width, width), F32),
            pltpu.VMEM((3 * count, width, width), F32),
            pltpu.VMEM((3 * count, width, width), F32),
            pltpu.VMEM((count, 3, n * t, width), F32),
            pltpu.VMEM((count, 3, n * t, width), BF16),
        ]
        if last:
            scratch.append(pltpu.VMEM((n_dp * own, width, width), BF16))
        before = sums if last else []
        outs = call(
            bind(chunk_kernel, chunk=c),
            [shape(n, 2 * t, count * width)] + c_shapes,
            (from_ids, dp_id, *a_in, *shares, *b_in[c], *before),
            [SMEM] * 2 + [VMEM] * (n + plan.group + len(b_in[c]) + len(before)),
            [VMEM] * (1 + len(c_shapes)),
            f"chunk{c}",
            scratch,
            flops=count * 640 * 10**6,
            size=count * 10**6,
            vmem=VMEM_LARGE,
        )
        d_sent.append(outs[0])
        sums = outs[1:]
    c_keep, c_send = sums

    halves = call(
        bind(pair_kernel),
        [shape(own, width, width)] * plan.rest,
        (dp_id, c_keep, swap(c_send, plan.pair - 1)),
        [SMEM] + [VMEM] * 2,
        [VMEM] * plan.rest,
        "state_pair",
        [pltpu.VMEM((plan.rest * own, width, width), F32)],
    )
    halves = [swap(halves[k], plan.pair * k) for k in range(plan.rest)]
    by_rows = call(
        bind(sum_kernel),
        [shape(own, rows, width)] * n,
        (to_ids, *halves),
        [SMEM] + [VMEM] * plan.rest,
        [VMEM] * n,
        "state_sum",
        [pltpu.VMEM((own, width, width), F32)],
    )
    by_rows = list(by_rows)
    back = [turn(d) for d in d_sent[:-1]]
    if back:
        back[0], by_rows[-1] = lax.optimization_barrier((back[0], by_rows[-1]))
    mine = call(
        bind(order_kernel),
        shape(n, own, rows, width),
        (from_ids, *shift(by_rows)),
        [SMEM] + [VMEM] * n,
        VMEM,
        "state_rows",
    )
    mine, late = lax.optimization_barrier((mine, d_sent[-1]))
    back.append(turn(late))
    rest = [swap(mine, plan.pair * k) for k in range(plan.rest)]
    half = call(
        bind(order_kernel),
        shape(plan.rest, n, own, rows, width),
        (rest_ids, *rest),
        [SMEM] + [VMEM] * plan.rest,
        VMEM,
        "state_rest",
    )
    both = [swap(half, k) for k in range(plan.pair)]
    grad_state = call(
        bind(state_kernel),
        shape(*state_start.shape, dtype=F32),
        (dp_id, *both),
        [SMEM] + [VMEM] * plan.pair,
        VMEM,
        "state_out",
    )
    grad_keys, grad_values = call(
        bind(unpack_kernel),
        [shape(*keys_a.shape), shape(*values_a.shape)],
        back,
        [VMEM] * len(back),
        [ANY] * 2,
        "unpack",
        [pltpu.SemaphoreType.DMA((2 * n * len(chunks),))],
    )
    return grad_keys, grad_values, grad_state


def solution(mesh):
    placed = (
        P("dp", "ctx", None),
        P("dp", "ctx", None),
        P("dp", "ctx", None),
        P("dp", "ctx", None),
        P(None, None, "ctx", None),
        P("dp", None, None, "ctx", None),
    )
    return jax.shard_map(
        local,
        mesh=mesh,
        in_specs=placed,
        out_specs=(P("dp", "ctx", None), P("dp", "ctx", None), P(None, None, "ctx", None)),
        check_vma=False,
    )
```

```python
import functools

import jax
import jax.numpy as jnp
from jax import lax
from jax.experimental import pallas as pl
from jax.experimental.pallas import tpu as pltpu
from jax.sharding import PartitionSpec as P

RATE = 4.0
CA = 3.4445
CB = -4.775
CC = 2.0315
STEPS = 2
F32 = jnp.float32
BF16 = jnp.bfloat16
VMEM_SMALL = 8 * 1024 * 1024
VMEM_LARGE = 28 * 1024 * 1024
SMEM = pl.BlockSpec(memory_space=pltpu.SMEM)
VMEM = pl.BlockSpec(memory_space=pltpu.VMEM)
ANY = pl.BlockSpec(memory_space=pl.ANY)
HBM = pl.BlockSpec(memory_space=pltpu.HBM)


def dot_nn(a, b):
    return lax.dot_general(a, b, (((1,), (0,)), ((), ())), preferred_element_type=F32)


def dot_nt(a, b):
    return lax.dot_general(a, b, (((1,), (1,)), ((), ())), preferred_element_type=F32)


def dot_tn(a, b):
    return lax.dot_general(a, b, (((0,), (0,)), ((), ())), preferred_element_type=F32)


def call(
    kernel, out_shape, args, in_specs, out_specs, name, scratch=(), flops=10**6, size=10**6, vmem=VMEM_SMALL
):
    return pl.pallas_call(
        kernel,
        out_shape=out_shape,
        in_specs=in_specs,
        out_specs=out_specs,
        scratch_shapes=list(scratch),
        compiler_params=pltpu.CompilerParams(vmem_limit_bytes=vmem),
        cost_estimate=pl.CostEstimate(flops=flops, bytes_accessed=size, transcendentals=0),
        name=name,
    )(*args)


def swish_terms(g):
    s = 1.0 / (1.0 + jnp.exp(-g))
    sw = g * s
    slope = s * (1.0 + g * (1.0 - s))
    return s, sw, slope


def newton_pullback(grads, updates):
    each = range(len(grads))
    inv = [lax.rsqrt(jnp.sum(g * g, keepdims=True) + 1e-06) for g in grads]
    xs = [[(grads[m] * inv[m]).astype(BF16) for m in each]]
    grams = []
    polys = []
    for step in range(STEPS):
        x = xs[-1]
        gram = [dot_nt(x[m], x[m]).astype(BF16) for m in each]
        poly = [(CB * gram[m].astype(F32) + CC * dot_nn(gram[m], gram[m])).astype(BF16) for m in each]
        grams.append(gram)
        polys.append(poly)
        if step + 1 < STEPS:
            xs.append([(CA * x[m].astype(F32) + dot_nn(poly[m], x[m])).astype(BF16) for m in each])
    d = updates
    for step in reversed(range(STEPS)):
        x, gram, poly = xs[step], grams[step], polys[step]
        dp = [dot_nt(d[m], x[m]) for m in each]
        sym = [dp[m] + dp[m].T for m in each]
        turned = [dot_nn(sym[m].astype(BF16), gram[m]) for m in each]
        da = [(CB * sym[m] + CC * (turned[m] + turned[m].T)).astype(BF16) for m in each]
        d = [
            (CA * d[m].astype(F32) + dot_nn(poly[m], d[m]) + dot_nn(da[m], x[m])).astype(BF16)
            for m in each
        ]
    out = []
    for m in each:
        df = d[m].astype(F32)
        along = jnp.sum(df * grads[m], keepdims=True)
        out.append(df * inv[m] - grads[m] * (along * (inv[m] * inv[m] * inv[m])))
    return out


class Plan:
    def __init__(self, n, n_dp, tokens, heads, rows, width):
        self.n, self.n_dp = n, n_dp
        self.tokens, self.heads, self.rows, self.width = tokens, heads, rows, width
        self.per = -(-heads // n)
        self.mats = 3 * self.per
        early = (self.per + 1) // 2
        self.chunks = [c for c in ((0, early), (early, self.per - early)) if c[1] > 0]
        self.group = min(4, n_dp)
        self.share = -(-self.mats // self.group)
        self.pair = min(2, n_dp)
        self.rest = n_dp // self.pair
        self.own = -(-self.mats // n_dp)
        self.block = -(-rows // 16) * 16
        self.share_rows = -(-self.share // self.per) * self.block

    def first_head(self, c):
        return min(c * self.per, self.heads - self.per)


def pack_a_kernel(head_ref, dp_ref, k_ref, v_ref, s_ref, out, state, sems, *, plan, slot):
    t, w, per = plan.tokens, plan.width, plan.per
    low = lax.rem(dp_ref[0], plan.group)
    head = head_ref[slot]
    loads = []
    for q in range(plan.share):
        mat = jnp.minimum(low * plan.share + q, plan.mats - 1)
        load = pltpu.make_async_copy(
            s_ref.at[lax.rem(mat, 3), head + lax.div(mat, 3)], state.at[q], sems.at[2 + q]
        )
        load.start()
        loads.append(load)
    cols = pl.ds(pl.multiple_of(head * w, w), per * w)
    copies = []
    for part, src in enumerate((k_ref, v_ref)):
        copy = pltpu.make_async_copy(src.at[0, :, cols], out.at[pl.ds(part * t, t), :], sems.at[part])
        copy.start()
        copies.append(copy)
    for load in loads:
        load.wait()
    for q in range(plan.share):
        top = 2 * t + (q // per) * plan.block
        left = (q % per) * w
        out[top : top + plan.rows, left : left + w] = state[q].astype(BF16)
    for copy in copies:
        copy.wait()


def pack_b_kernel(head_ref, q_ref, o_ref, s_ref, *refs, plan, chunk):
    n, t, w = plan.n, plan.tokens, plan.width
    first, count = plan.chunks[chunk]
    outs, (state, sems) = refs[:-2], refs[-2:]
    if len(outs) < n:
        outs = [outs[0].at[c] for c in range(n)]
        heads = [plan.first_head(c) + first for c in range(n)]
        offsets = [head * w for head in heads]
    else:
        heads = [head_ref[slot] + first for slot in range(n)]
        offsets = [pl.multiple_of(head * w, w) for head in heads]
    loads = []
    copies = []
    for k in range(n):
        load = pltpu.make_async_copy(
            s_ref.at[0, :, pl.ds(heads[k], count)], state.at[k], sems.at[3 * k + 2]
        )
        load.start()
        loads.append(load)
        for part, src in enumerate((q_ref, o_ref)):
            copy = pltpu.make_async_copy(
                src.at[0, :, pl.ds(offsets[k], count * w)],
                outs[k].at[pl.ds(part * t, t), :],
                sems.at[3 * k + part],
            )
            copy.start()
            copies.append(copy)
    for k in range(n):
        loads[k].wait()
        for j in range(count):
            for m in range(3):
                top = 2 * t + m * plan.block
                outs[k][top : top + plan.rows, j * w : (j + 1) * w] = state[k, m, j].astype(BF16)
    for copy in copies:
        copy.wait()


def start_kernel(from_ref, *refs, plan):
    rows, w = plan.rows, plan.width
    a_refs, (out, whole) = refs[: plan.n], refs[plan.n :]
    for slot in range(plan.n):
        at = pl.ds(pl.multiple_of(from_ref[slot] * rows, rows), rows)
        for q in range(plan.share):
            top = 2 * plan.tokens + (q // plan.per) * plan.block
            left = (q % plan.per) * w
            whole[q, at, :] = a_refs[slot][top : top + rows, left : left + w].astype(F32)
    out[...] = whole[...].astype(BF16)


def tokens_of(refs, j, plan):
    t, w = plan.tokens, plan.width
    cols = slice(j * w, (j + 1) * w)
    x = jnp.concatenate([r[0:t, cols] for r in refs], axis=0)
    y = jnp.concatenate([r[t : 2 * t, cols] for r in refs], axis=0)
    return x, y


def forward(x, y, wa, wb, wc):
    w = wa.shape[1]
    gu = dot_nn(x, jnp.concatenate([wa, wb], axis=1))
    g, u = gu[:, :w], gu[:, w:]
    p = dot_nn(y, wc)
    _, sw, slope = swish_terms(g)
    hidden = (sw * u).astype(BF16)
    dg = (p * u * slope).astype(BF16)
    du = (p * sw).astype(BF16)
    ab = dot_tn(x, jnp.concatenate([dg, du], axis=1))
    return (ab[:, :w], ab[:, w:], dot_tn(y, hidden)), (g, u, p), (dg, du, hidden)


def chunk_kernel(from_ref, dp_ref, *refs, plan, chunk):
    n, t, w = plan.n, plan.tokens, plan.width
    first, count = plan.chunks[chunk]
    last = chunk + 1 == len(plan.chunks)
    mats = 3 * count
    refs = list(refs)

    def take(k):
        got = refs[:k]
        del refs[:k]
        return got

    a_refs, shares = take(n), take(plan.group)
    joined = len(refs[0].shape) == 3
    b_refs = take(1 if joined else n)
    if joined:
        b_refs = [b_refs[0].at[c] for c in range(n)]
        sources = list(range(n))
    else:
        sources = [from_ref[slot] for slot in range(n)]
    before = take(chunk) if last else []
    (d_ref,) = take(1)
    c_refs = take(2 if last else 1)
    w0, w1, gsum, ssum, acts, fields = take(6)
    total = take(1)[0] if last else c_refs[0]
    base = 3 * first if last else 0

    low = lax.rem(dp_ref[0], plan.group)
    for k in range(plan.group):
        at = pl.ds(jnp.bitwise_xor(low, k) * plan.share, plan.share)
        w0[at] = shares[k][...]
    for slot in range(n):
        row = sources[slot] * plan.rows
        at = pl.ds(row if joined else pl.multiple_of(row, plan.rows), plan.rows)
        for j in range(count):
            for m in range(3):
                top = 2 * t + m * plan.block
                part = b_refs[slot][top : top + plan.rows, j * w : (j + 1) * w]
                w1[3 * j + m, at, :] = part.astype(F32)

    for j in range(count):
        at = 3 * (first + j)
        x, y = tokens_of(a_refs, first + j, plan)
        sums, act, field = forward(x, y, w0[at], w0[at + 1], w0[at + 2])
        for m in range(3):
            gsum[3 * j + m] = sums[m]
            acts[j, m] = act[m]
            fields[j, m] = field[m]
        x, y = tokens_of(b_refs, j, plan)
        sums, _, _ = forward(x, y, *[w1[3 * j + m].astype(BF16) for m in range(3)])
        for m in range(3):
            ssum[3 * j + m] = sums[m]

    grads = [gsum[m] for m in range(mats)]
    updates = [(RATE * ssum[m]).astype(BF16) for m in range(mats)]
    for m, val in enumerate(newton_pullback(grads, updates)):
        gsum[m] = val

    for j in range(count):
        at = 3 * (first + j)
        x, y = tokens_of(a_refs, first + j, plan)
        fab = jnp.concatenate([gsum[3 * j], gsum[3 * j + 1]], axis=1).astype(BF16)
        fc = gsum[3 * j + 2].astype(BF16)
        wab = jnp.concatenate([w0[at], w0[at + 1]], axis=1)
        wc = w0[at + 2]
        cdgu = dot_nn(x, fab)
        cdg, cdu = cdgu[:, :w], cdgu[:, w:]
        ch = dot_nn(y, fc)
        g, u, p = acts[j, 0], acts[j, 1], acts[j, 2]
        s, sw, slope = swish_terms(g)
        curve = s * (1.0 - s) * (2.0 + g * (1.0 - 2.0 * s))
        cg = ((ch * u + cdu * p) * slope + cdg * (p * u) * curve).astype(BF16)
        cu = (ch * sw + cdg * p * slope).astype(BF16)
        cp = (cdu * sw + cdg * u * slope).astype(BF16)
        dg, du, hidden = fields[j, 0], fields[j, 1], fields[j, 2]
        dx = dot_nt(jnp.concatenate([dg, du, cg, cu], axis=1), jnp.concatenate([fab, wab], axis=1))
        dy = dot_nt(jnp.concatenate([hidden, cp], axis=1), jnp.concatenate([fc, wc], axis=1))
        cols = slice(j * w, (j + 1) * w)
        for slot in range(n):
            to = from_ref[slot]
            d_ref[to, 0:t, cols] = dx[slot * t : (slot + 1) * t].astype(BF16)
            d_ref[to, t : 2 * t, cols] = dy[slot * t : (slot + 1) * t].astype(BF16)
        ab = dot_tn(x, jnp.concatenate([cg, cu], axis=1))
        grown = (ab[:, :w], ab[:, w:], dot_tn(y, cp))
        for m in range(3):
            total[base + 3 * j + m] = (ssum[3 * j + m] + grown[m]).astype(BF16)

    if last:
        for c, part in enumerate(before):
            at = 3 * plan.chunks[c][0]
            total[at : at + part.shape[0]] = part[...]
        for m in range(plan.mats, plan.n_dp * plan.own):
            total[m] = jnp.zeros((w, w), BF16)
        mine = lax.rem(dp_ref[0], plan.pair)
        for r in range(plan.rest):
            to = slice(r * plan.own, (r + 1) * plan.own)
            for ref, which in zip(c_refs, (mine, plan.pair - 1 - mine)):
                ref[to] = total[pl.ds((plan.pair * r + which) * plan.own, plan.own)]


def pair_kernel(dp_ref, keep_ref, got_ref, *refs, plan):
    outs, whole = refs[:-1], refs[-1]
    whole[...] = keep_ref[...].astype(F32) + got_ref[...].astype(F32)
    place = lax.div(dp_ref[0], plan.pair)
    for k in range(plan.rest):
        at = pl.ds(jnp.bitwise_xor(place, k) * plan.own, plan.own)
        outs[k][...] = whole[at].astype(BF16)


def sum_kernel(to_ref, *refs, plan):
    parts, outs, whole = refs[: plan.rest], refs[plan.rest : -1], refs[-1]
    added = parts[0][...].astype(F32)
    for part in parts[1:]:
        added = added + part[...].astype(F32)
    whole[...] = added / plan.n_dp
    for slot in range(plan.n):
        at = pl.ds(pl.multiple_of(to_ref[slot] * plan.rows, plan.rows), plan.rows)
        outs[slot][...] = whole[:, at, :].astype(BF16)


def order_kernel(place_ref, *refs, plan):
    parts, out = refs[:-1], refs[-1]
    for k, part in enumerate(parts):
        out[place_ref[k]] = part[...]


def state_kernel(dp_ref, *refs, plan):
    out = refs[-1]
    mine = lax.rem(dp_ref[0], plan.pair)
    for k in range(plan.pair):
        for r in range(plan.rest):
            for i in range(plan.own):
                mat = (plan.pair * r + jnp.bitwise_xor(mine, k)) * plan.own + i

                @pl.when(mat < plan.mats)
                def _(mat=mat, ref=refs[k], r=r, i=i):
                    for c in range(plan.n):
                        out[lax.rem(mat, 3), plan.first_head(c) + lax.div(mat, 3)] = ref[r, c, i].astype(F32)


def unpack_kernel(*refs, plan):
    t, w = plan.tokens, plan.width
    ins, (dk, dv, sems) = refs[:-3], refs[-3:]
    copies = []
    for c, (first, count) in enumerate(plan.chunks):
        for owner in range(plan.n):
            cols = pl.ds((plan.first_head(owner) + first) * w, count * w)
            for part, dst in enumerate((dk, dv)):
                copy = pltpu.make_async_copy(
                    ins[c].at[owner, pl.ds(part * t, t), :],
                    dst.at[0, :, cols],
                    sems.at[(c * plan.n + owner) * 2 + part],
                )
                copy.start()
                copies.append(copy)
            if plan.n * plan.per != plan.heads:
                for copy in copies:
                    copy.wait()
                copies = []
    for copy in copies:
        copy.wait()


def local(keys_a, values_a, queries_b, grad_out, state_start, state_next):
    n, n_dp = lax.axis_size("ctx"), lax.axis_size("dp")
    _, heads, rows, width = state_start.shape
    t = keys_a.shape[1]
    plan = Plan(n, n_dp, t, heads, rows, width)
    per, mats, own, chunks = plan.per, plan.mats, plan.own, plan.chunks
    bind = lambda kernel, **more: functools.partial(kernel, plan=plan, **more)

    keys_a, values_a, grad_out, state_start, state_next = (
        pltpu.with_memory_space_constraint(arg, pltpu.HBM)
        for arg in (keys_a, values_a, grad_out, state_start, state_next)
    )
    me = lax.axis_index("ctx")
    places = jnp.arange(n, dtype=jnp.int32)
    to_ids = lax.rem(me + places, n)
    from_ids = lax.rem(me + n - places, n)
    head_ids = jnp.minimum(to_ids * per, heads - per)
    dp_id = lax.axis_index("dp").reshape(1)
    rest_ids = jnp.bitwise_xor(lax.div(dp_id, plan.pair), jnp.arange(plan.rest, dtype=jnp.int32))

    def swap(value, k):
        if k == 0:
            return value
        return lax.ppermute(value, "dp", [(i, i ^ k) for i in range(n_dp)])

    def shift(values):
        return [
            lax.ppermute(v, "ctx", [(i, (i + s) % n) for i in range(n)]) if s else v
            for s, v in enumerate(values)
        ]

    def turn(value):
        return lax.all_to_all(value, "ctx", split_axis=0, concat_axis=0, tiled=True)

    def shape(*dims, dtype=BF16):
        return jax.ShapeDtypeStruct(dims, dtype)

    def pack_a(slot):
        return call(
            bind(pack_a_kernel, slot=slot),
            shape(2 * t + plan.share_rows, per * width),
            (head_ids, dp_id, keys_a, values_a, state_start),
            [SMEM] * 2 + [HBM] * 3,
            VMEM,
            f"pack_a{slot}",
            [
                pltpu.VMEM((plan.share, rows, width), F32),
                pltpu.SemaphoreType.DMA((2 + plan.share,)),
            ],
        )

    def pack_b(c, queries):
        dims = (2 * t + 3 * plan.block, chunks[c][1] * width)
        joined = c == 0
        outs = call(
            bind(pack_b_kernel, chunk=c),
            [shape(n, *dims)] if joined else [shape(*dims)] * n,
            (head_ids, pltpu.with_memory_space_constraint(queries, pltpu.HBM), grad_out, state_next),
            [SMEM] + [HBM] * 3,
            [VMEM] * (1 if joined else n),
            f"pack_b{c}",
            [
                pltpu.VMEM((n, 3, chunks[c][1], rows, width), F32),
                pltpu.SemaphoreType.DMA((3 * n,)),
            ],
        )
        return list(outs)

    a_sent = [pack_a(s) for s in [*range(1, n), 0]]
    a_sent = [a_sent[-1]] + a_sent[:-1]
    queries, a_sent[-1] = lax.optimization_barrier((queries_b, a_sent[-1]))
    a_in = shift(a_sent)
    b_sent = pack_b(0, queries)
    queries, b_sent[0] = lax.optimization_barrier((queries_b, b_sent[0]))
    b_in = [[turn(b_sent[0])]]
    b_sent = pack_b(1, queries)
    start_own = call(
        bind(start_kernel),
        shape(plan.share, width, width),
        (from_ids, *a_in),
        [SMEM] + [VMEM] * n,
        VMEM,
        "start_share",
        [pltpu.VMEM((plan.share, width, width), F32)],
    )
    shares = [swap(start_own, k) for k in range(plan.group)]
    b_sent[-1], shares[-1] = lax.optimization_barrier((b_sent[-1], shares[-1]))
    b_in.append(shift(b_sent))
    d_sent = []
    sums = []
    for c, (_, count) in enumerate(chunks):
        last = c + 1 == len(chunks)
        if last:
            c_shapes = [shape(plan.rest * own, width, width)] * 2
        else:
            c_shapes = [shape(3 * count, width, width)]
        scratch = [
            pltpu.VMEM((plan.group * plan.share, width, width), BF16),
            pltpu.VMEM((3 * count, width, width), F32),
            pltpu.VMEM((3 * count, width, width), F32),
            pltpu.VMEM((3 * count, width, width), F32),
            pltpu.VMEM((count, 3, n * t, width), F32),
            pltpu.VMEM((count, 3, n * t, width), BF16),
        ]
        if last:
            scratch.append(pltpu.VMEM((n_dp * own, width, width), BF16))
        before = sums if last else []
        outs = call(
            bind(chunk_kernel, chunk=c),
            [shape(n, 2 * t, count * width)] + c_shapes,
            (from_ids, dp_id, *a_in, *shares, *b_in[c], *before),
            [SMEM] * 2 + [VMEM] * (n + plan.group + len(b_in[c]) + len(before)),
            [VMEM] * (1 + len(c_shapes)),
            f"chunk{c}",
            scratch,
            flops=count * 640 * 10**6,
            size=count * 10**6,
            vmem=VMEM_LARGE,
        )
        d_sent.append(outs[0])
        sums = outs[1:]
    c_keep, c_send = sums

    halves = call(
        bind(pair_kernel),
        [shape(own, width, width)] * plan.rest,
        (dp_id, c_keep, swap(c_send, plan.pair - 1)),
        [SMEM] + [VMEM] * 2,
        [VMEM] * plan.rest,
        "state_pair",
        [pltpu.VMEM((plan.rest * own, width, width), F32)],
    )
    halves = [swap(halves[k], plan.pair * k) for k in range(plan.rest)]
    by_rows = call(
        bind(sum_kernel),
        [shape(own, rows, width)] * n,
        (to_ids, *halves),
        [SMEM] + [VMEM] * plan.rest,
        [VMEM] * n,
        "state_sum",
        [pltpu.VMEM((own, width, width), F32)],
    )
    back = [turn(d_sent[0])]
    by_rows = shift(by_rows)
    by_rows[0], back[0] = lax.optimization_barrier((by_rows[0], back[0]))
    mine = call(
        bind(order_kernel),
        shape(n, own, rows, width),
        (from_ids, *by_rows),
        [SMEM] + [VMEM] * n,
        VMEM,
        "state_rows",
    )
    mine, late = lax.optimization_barrier((mine, d_sent[1]))
    back.append(turn(late))
    rest = [swap(mine, plan.pair * k) for k in range(plan.rest)]
    half = call(
        bind(order_kernel),
        shape(plan.rest, n, own, rows, width),
        (rest_ids, *rest),
        [SMEM] + [VMEM] * plan.rest,
        VMEM,
        "state_rest",
    )
    both = [swap(half, k) for k in range(plan.pair)]
    grad_state = call(
        bind(state_kernel),
        shape(*state_start.shape, dtype=F32),
        (dp_id, *both),
        [SMEM] + [VMEM] * plan.pair,
        VMEM,
        "state_out",
    )
    grad_keys, grad_values = call(
        bind(unpack_kernel),
        [shape(*keys_a.shape), shape(*values_a.shape)],
        back,
        [VMEM] * len(back),
        [ANY] * 2,
        "unpack",
        [pltpu.SemaphoreType.DMA((2 * n * len(chunks),))],
    )
    return grad_keys, grad_values, grad_state


def solution(mesh):
    placed = (
        P("dp", "ctx", None),
        P("dp", "ctx", None),
        P("dp", "ctx", None),
        P("dp", "ctx", None),
        P(None, None, "ctx", None),
        P("dp", None, None, "ctx", None),
    )
    return jax.shard_map(
        local,
        mesh=mesh,
        in_specs=placed,
        out_specs=(P("dp", "ctx", None), P("dp", "ctx", None), P(None, None, "ctx", None)),
        check_vma=False,
    )
```

```python
import functools

import jax
import jax.numpy as jnp
from jax import lax
from jax.experimental import pallas as pl
from jax.experimental.pallas import tpu as pltpu
from jax.sharding import PartitionSpec as P

RATE = 4.0
CA = 3.4445
CB = -4.775
CC = 2.0315
STEPS = 2
F32 = jnp.float32
BF16 = jnp.bfloat16
VMEM_SMALL = 8 * 1024 * 1024
VMEM_LARGE = 28 * 1024 * 1024
SMEM = pl.BlockSpec(memory_space=pltpu.SMEM)
VMEM = pl.BlockSpec(memory_space=pltpu.VMEM)
ANY = pl.BlockSpec(memory_space=pl.ANY)
HBM = pl.BlockSpec(memory_space=pltpu.HBM)


def dot_nn(a, b):
    return lax.dot_general(a, b, (((1,), (0,)), ((), ())), preferred_element_type=F32)


def dot_nt(a, b):
    return lax.dot_general(a, b, (((1,), (1,)), ((), ())), preferred_element_type=F32)


def dot_tn(a, b):
    return lax.dot_general(a, b, (((0,), (0,)), ((), ())), preferred_element_type=F32)


def call(
    kernel, out_shape, args, in_specs, out_specs, name, scratch=(), flops=10**6, size=10**6, vmem=VMEM_SMALL
):
    return pl.pallas_call(
        kernel,
        out_shape=out_shape,
        in_specs=in_specs,
        out_specs=out_specs,
        scratch_shapes=list(scratch),
        compiler_params=pltpu.CompilerParams(vmem_limit_bytes=vmem),
        cost_estimate=pl.CostEstimate(flops=flops, bytes_accessed=size, transcendentals=0),
        name=name,
    )(*args)


def swish_terms(g):
    s = 1.0 / (1.0 + jnp.exp(-g))
    sw = g * s
    slope = s * (1.0 + g * (1.0 - s))
    return s, sw, slope


def newton_pullback(grads, updates):
    each = range(len(grads))
    inv = [lax.rsqrt(jnp.sum(g * g, keepdims=True) + 1e-06) for g in grads]
    xs = [[(grads[m] * inv[m]).astype(BF16) for m in each]]
    grams = []
    polys = []
    for step in range(STEPS):
        x = xs[-1]
        gram = [dot_nt(x[m], x[m]).astype(BF16) for m in each]
        poly = [(CB * gram[m].astype(F32) + CC * dot_nn(gram[m], gram[m])).astype(BF16) for m in each]
        grams.append(gram)
        polys.append(poly)
        if step + 1 < STEPS:
            xs.append([(CA * x[m].astype(F32) + dot_nn(poly[m], x[m])).astype(BF16) for m in each])
    d = updates
    for step in reversed(range(STEPS)):
        x, gram, poly = xs[step], grams[step], polys[step]
        dp = [dot_nt(d[m], x[m]) for m in each]
        sym = [dp[m] + dp[m].T for m in each]
        turned = [dot_nn(sym[m].astype(BF16), gram[m]) for m in each]
        da = [(CB * sym[m] + CC * (turned[m] + turned[m].T)).astype(BF16) for m in each]
        d = [
            (CA * d[m].astype(F32) + dot_nn(poly[m], d[m]) + dot_nn(da[m], x[m])).astype(BF16)
            for m in each
        ]
    out = []
    for m in each:
        df = d[m].astype(F32)
        along = jnp.sum(df * grads[m], keepdims=True)
        out.append(df * inv[m] - grads[m] * (along * (inv[m] * inv[m] * inv[m])))
    return out


class Plan:
    def __init__(self, n, n_dp, tokens, heads, rows, width):
        self.n, self.n_dp = n, n_dp
        self.tokens, self.heads, self.rows, self.width = tokens, heads, rows, width
        self.per = -(-heads // n)
        self.mats = 3 * self.per
        early = (self.per + 1) // 2
        self.chunks = [c for c in ((0, early), (early, self.per - early)) if c[1] > 0]
        self.group = min(4, n_dp)
        self.share = -(-self.mats // self.group)
        self.pair = min(2, n_dp)
        self.rest = n_dp // self.pair
        self.own = -(-self.mats // n_dp)
        self.block = -(-rows // 16) * 16
        self.share_rows = -(-self.share // self.per) * self.block

    def first_head(self, c):
        return min(c * self.per, self.heads - self.per)


def pack_a_kernel(head_ref, dp_ref, k_ref, v_ref, s_ref, out, state, sems, *, plan, slot):
    t, w, per = plan.tokens, plan.width, plan.per
    low = lax.rem(dp_ref[0], plan.group)
    head = head_ref[slot]
    loads = []
    for q in range(plan.share):
        mat = jnp.minimum(low * plan.share + q, plan.mats - 1)
        load = pltpu.make_async_copy(
            s_ref.at[lax.rem(mat, 3), head + lax.div(mat, 3)], state.at[q], sems.at[2 + q]
        )
        load.start()
        loads.append(load)
    cols = pl.ds(pl.multiple_of(head * w, w), per * w)
    copies = []
    for part, src in enumerate((k_ref, v_ref)):
        copy = pltpu.make_async_copy(src.at[0, :, cols], out.at[pl.ds(part * t, t), :], sems.at[part])
        copy.start()
        copies.append(copy)
    for load in loads:
        load.wait()
    for q in range(plan.share):
        top = 2 * t + (q // per) * plan.block
        left = (q % per) * w
        out[top : top + plan.rows, left : left + w] = state[q].astype(BF16)
    for copy in copies:
        copy.wait()


def pack_b_kernel(head_ref, q_ref, o_ref, s_ref, *refs, plan, chunk):
    n, t, w = plan.n, plan.tokens, plan.width
    first, count = plan.chunks[chunk]
    outs, (state, sems) = refs[:-2], refs[-2:]
    if len(outs) < n:
        outs = [outs[0].at[c] for c in range(n)]
        heads = [plan.first_head(c) + first for c in range(n)]
        offsets = [head * w for head in heads]
    else:
        heads = [head_ref[slot] + first for slot in range(n)]
        offsets = [pl.multiple_of(head * w, w) for head in heads]
    loads = []
    copies = []
    for k in range(n):
        load = pltpu.make_async_copy(
            s_ref.at[0, :, pl.ds(heads[k], count)], state.at[k], sems.at[3 * k + 2]
        )
        load.start()
        loads.append(load)
        for part, src in enumerate((q_ref, o_ref)):
            copy = pltpu.make_async_copy(
                src.at[0, :, pl.ds(offsets[k], count * w)],
                outs[k].at[pl.ds(part * t, t), :],
                sems.at[3 * k + part],
            )
            copy.start()
            copies.append(copy)
    for k in range(n):
        loads[k].wait()
        for j in range(count):
            for m in range(3):
                top = 2 * t + m * plan.block
                outs[k][top : top + plan.rows, j * w : (j + 1) * w] = state[k, m, j].astype(BF16)
    for copy in copies:
        copy.wait()


def start_kernel(from_ref, *refs, plan):
    rows, w = plan.rows, plan.width
    a_refs, (out, whole) = refs[: plan.n], refs[plan.n :]
    for slot in range(plan.n):
        at = pl.ds(pl.multiple_of(from_ref[slot] * rows, rows), rows)
        for q in range(plan.share):
            top = 2 * plan.tokens + (q // plan.per) * plan.block
            left = (q % plan.per) * w
            whole[q, at, :] = a_refs[slot][top : top + rows, left : left + w].astype(F32)
    out[...] = whole[...].astype(BF16)


def tokens_of(refs, j, plan):
    t, w = plan.tokens, plan.width
    cols = slice(j * w, (j + 1) * w)
    x = jnp.concatenate([r[0:t, cols] for r in refs], axis=0)
    y = jnp.concatenate([r[t : 2 * t, cols] for r in refs], axis=0)
    return x, y


def forward(x, y, wa, wb, wc):
    w = wa.shape[1]
    gu = dot_nn(x, jnp.concatenate([wa, wb], axis=1))
    g, u = gu[:, :w], gu[:, w:]
    p = dot_nn(y, wc)
    _, sw, slope = swish_terms(g)
    hidden = (sw * u).astype(BF16)
    dg = (p * u * slope).astype(BF16)
    du = (p * sw).astype(BF16)
    ab = dot_tn(x, jnp.concatenate([dg, du], axis=1))
    return (ab[:, :w], ab[:, w:], dot_tn(y, hidden)), (g, u, p), (dg, du, hidden)


def chunk_kernel(from_ref, dp_ref, *refs, plan, chunk):
    n, t, w = plan.n, plan.tokens, plan.width
    first, count = plan.chunks[chunk]
    last = chunk + 1 == len(plan.chunks)
    mats = 3 * count
    refs = list(refs)

    def take(k):
        got = refs[:k]
        del refs[:k]
        return got

    a_refs, shares = take(n), take(plan.group)
    joined = len(refs[0].shape) == 3
    b_refs = take(1 if joined else n)
    if joined:
        b_refs = [b_refs[0].at[c] for c in range(n)]
        sources = list(range(n))
    else:
        sources = [from_ref[slot] for slot in range(n)]
    before = take(chunk) if last else []
    (d_ref,) = take(1)
    c_refs = take(2 if last else 1)
    w0, w1, gsum, ssum, acts, fields = take(6)
    total = take(1)[0] if last else c_refs[0]
    base = 3 * first if last else 0

    low = lax.rem(dp_ref[0], plan.group)
    for k in range(plan.group):
        at = pl.ds(jnp.bitwise_xor(low, k) * plan.share, plan.share)
        w0[at] = shares[k][...]
    for slot in range(n):
        row = sources[slot] * plan.rows
        at = pl.ds(row if joined else pl.multiple_of(row, plan.rows), plan.rows)
        for j in range(count):
            for m in range(3):
                top = 2 * t + m * plan.block
                part = b_refs[slot][top : top + plan.rows, j * w : (j + 1) * w]
                w1[3 * j + m, at, :] = part.astype(F32)

    for j in range(count):
        at = 3 * (first + j)
        x, y = tokens_of(a_refs, first + j, plan)
        sums, act, field = forward(x, y, w0[at], w0[at + 1], w0[at + 2])
        for m in range(3):
            gsum[3 * j + m] = sums[m]
            acts[j, m] = act[m]
            fields[j, m] = field[m]
        x, y = tokens_of(b_refs, j, plan)
        sums, _, _ = forward(x, y, *[w1[3 * j + m].astype(BF16) for m in range(3)])
        for m in range(3):
            ssum[3 * j + m] = sums[m]

    grads = [gsum[m] for m in range(mats)]
    updates = [(RATE * ssum[m]).astype(BF16) for m in range(mats)]
    for m, val in enumerate(newton_pullback(grads, updates)):
        gsum[m] = val

    for j in range(count):
        at = 3 * (first + j)
        x, y = tokens_of(a_refs, first + j, plan)
        fab = jnp.concatenate([gsum[3 * j], gsum[3 * j + 1]], axis=1).astype(BF16)
        fc = gsum[3 * j + 2].astype(BF16)
        wab = jnp.concatenate([w0[at], w0[at + 1]], axis=1)
        wc = w0[at + 2]
        cdgu = dot_nn(x, fab)
        cdg, cdu = cdgu[:, :w], cdgu[:, w:]
        ch = dot_nn(y, fc)
        g, u, p = acts[j, 0], acts[j, 1], acts[j, 2]
        s, sw, slope = swish_terms(g)
        curve = s * (1.0 - s) * (2.0 + g * (1.0 - 2.0 * s))
        cg = ((ch * u + cdu * p) * slope + cdg * (p * u) * curve).astype(BF16)
        cu = (ch * sw + cdg * p * slope).astype(BF16)
        cp = (cdu * sw + cdg * u * slope).astype(BF16)
        dg, du, hidden = fields[j, 0], fields[j, 1], fields[j, 2]
        dx = dot_nt(jnp.concatenate([dg, du, cg, cu], axis=1), jnp.concatenate([fab, wab], axis=1))
        dy = dot_nt(jnp.concatenate([hidden, cp], axis=1), jnp.concatenate([fc, wc], axis=1))
        cols = slice(j * w, (j + 1) * w)
        for slot in range(n):
            to = from_ref[slot]
            d_ref[to, 0:t, cols] = dx[slot * t : (slot + 1) * t].astype(BF16)
            d_ref[to, t : 2 * t, cols] = dy[slot * t : (slot + 1) * t].astype(BF16)
        ab = dot_tn(x, jnp.concatenate([cg, cu], axis=1))
        grown = (ab[:, :w], ab[:, w:], dot_tn(y, cp))
        for m in range(3):
            total[base + 3 * j + m] = (ssum[3 * j + m] + grown[m]).astype(BF16)

    if last:
        for c, part in enumerate(before):
            at = 3 * plan.chunks[c][0]
            total[at : at + part.shape[0]] = part[...]
        for m in range(plan.mats, plan.n_dp * plan.own):
            total[m] = jnp.zeros((w, w), BF16)
        mine = lax.rem(dp_ref[0], plan.pair)
        for r in range(plan.rest):
            to = slice(r * plan.own, (r + 1) * plan.own)
            for ref, which in zip(c_refs, (mine, plan.pair - 1 - mine)):
                ref[to] = total[pl.ds((plan.pair * r + which) * plan.own, plan.own)]


def pair_kernel(dp_ref, keep_ref, got_ref, *refs, plan):
    outs, whole = refs[:-1], refs[-1]
    whole[...] = keep_ref[...].astype(F32) + got_ref[...].astype(F32)
    place = lax.div(dp_ref[0], plan.pair)
    for k in range(plan.rest):
        at = pl.ds(jnp.bitwise_xor(place, k) * plan.own, plan.own)
        outs[k][...] = whole[at].astype(BF16)


def sum_kernel(to_ref, *refs, plan):
    parts, outs, whole = refs[: plan.rest], refs[plan.rest : -1], refs[-1]
    added = parts[0][...].astype(F32)
    for part in parts[1:]:
        added = added + part[...].astype(F32)
    whole[...] = added / plan.n_dp
    for slot in range(plan.n):
        at = pl.ds(pl.multiple_of(to_ref[slot] * plan.rows, plan.rows), plan.rows)
        outs[slot][...] = whole[:, at, :].astype(BF16)


def order_kernel(place_ref, *refs, plan):
    parts, out = refs[:-1], refs[-1]
    for k, part in enumerate(parts):
        out[place_ref[k]] = part[...]


def state_kernel(dp_ref, *refs, plan):
    out = refs[-1]
    mine = lax.rem(dp_ref[0], plan.pair)
    for k in range(plan.pair):
        for r in range(plan.rest):
            for i in range(plan.own):
                mat = (plan.pair * r + jnp.bitwise_xor(mine, k)) * plan.own + i

                @pl.when(mat < plan.mats)
                def _(mat=mat, ref=refs[k], r=r, i=i):
                    for c in range(plan.n):
                        out[lax.rem(mat, 3), plan.first_head(c) + lax.div(mat, 3)] = ref[r, c, i].astype(F32)


def unpack_kernel(*refs, plan):
    t, w = plan.tokens, plan.width
    ins, (dk, dv, sems) = refs[:-3], refs[-3:]
    copies = []
    for c, (first, count) in enumerate(plan.chunks):
        for owner in range(plan.n):
            cols = pl.ds((plan.first_head(owner) + first) * w, count * w)
            for part, dst in enumerate((dk, dv)):
                copy = pltpu.make_async_copy(
                    ins[c].at[owner, pl.ds(part * t, t), :],
                    dst.at[0, :, cols],
                    sems.at[(c * plan.n + owner) * 2 + part],
                )
                copy.start()
                copies.append(copy)
            if plan.n * plan.per != plan.heads:
                for copy in copies:
                    copy.wait()
                copies = []
    for copy in copies:
        copy.wait()


def local(keys_a, values_a, queries_b, grad_out, state_start, state_next):
    n, n_dp = lax.axis_size("ctx"), lax.axis_size("dp")
    _, heads, rows, width = state_start.shape
    t = keys_a.shape[1]
    plan = Plan(n, n_dp, t, heads, rows, width)
    per, mats, own, chunks = plan.per, plan.mats, plan.own, plan.chunks
    bind = lambda kernel, **more: functools.partial(kernel, plan=plan, **more)

    keys_a, values_a, grad_out, state_start, state_next = (
        pltpu.with_memory_space_constraint(arg, pltpu.HBM)
        for arg in (keys_a, values_a, grad_out, state_start, state_next)
    )
    me = lax.axis_index("ctx")
    places = jnp.arange(n, dtype=jnp.int32)
    to_ids = lax.rem(me + places, n)
    from_ids = lax.rem(me + n - places, n)
    head_ids = jnp.minimum(to_ids * per, heads - per)
    dp_id = lax.axis_index("dp").reshape(1)
    rest_ids = jnp.bitwise_xor(lax.div(dp_id, plan.pair), jnp.arange(plan.rest, dtype=jnp.int32))

    def swap(value, k):
        if k == 0:
            return value
        return lax.ppermute(value, "dp", [(i, i ^ k) for i in range(n_dp)])

    def shift(values):
        return [
            lax.ppermute(v, "ctx", [(i, (i + s) % n) for i in range(n)]) if s else v
            for s, v in enumerate(values)
        ]

    def turn(value):
        return lax.all_to_all(value, "ctx", split_axis=0, concat_axis=0, tiled=True)

    def shape(*dims, dtype=BF16):
        return jax.ShapeDtypeStruct(dims, dtype)

    def pack_a(slot):
        return call(
            bind(pack_a_kernel, slot=slot),
            shape(2 * t + plan.share_rows, per * width),
            (head_ids, dp_id, keys_a, values_a, state_start),
            [SMEM] * 2 + [HBM] * 3,
            VMEM,
            f"pack_a{slot}",
            [
                pltpu.VMEM((plan.share, rows, width), F32),
                pltpu.SemaphoreType.DMA((2 + plan.share,)),
            ],
        )

    def pack_b(c, queries):
        dims = (2 * t + 3 * plan.block, chunks[c][1] * width)
        joined = c > 0
        outs = call(
            bind(pack_b_kernel, chunk=c),
            [shape(n, *dims)] if joined else [shape(*dims)] * n,
            (head_ids, pltpu.with_memory_space_constraint(queries, pltpu.HBM), grad_out, state_next),
            [SMEM] + [HBM] * 3,
            [VMEM] * (1 if joined else n),
            f"pack_b{c}",
            [
                pltpu.VMEM((n, 3, chunks[c][1], rows, width), F32),
                pltpu.SemaphoreType.DMA((3 * n,)),
            ],
        )
        return list(outs)

    a_sent = [pack_a(s) for s in [*range(1, n), 0]]
    a_sent = [a_sent[-1]] + a_sent[:-1]
    queries, a_sent[-1] = lax.optimization_barrier((queries_b, a_sent[-1]))
    a_in = shift(a_sent)
    b_in = [shift(pack_b(0, queries))]
    queries, a_in = lax.optimization_barrier((queries_b, a_in))
    b_in.append([turn(pack_b(1, queries)[0])])
    start_own = call(
        bind(start_kernel),
        shape(plan.share, width, width),
        (from_ids, *a_in),
        [SMEM] + [VMEM] * n,
        VMEM,
        "start_share",
        [pltpu.VMEM((plan.share, width, width), F32)],
    )
    shares = [swap(start_own, k) for k in range(plan.group)]
    d_sent = []
    sums = []
    for c, (_, count) in enumerate(chunks):
        last = c + 1 == len(chunks)
        if last:
            c_shapes = [shape(plan.rest * own, width, width)] * 2
        else:
            c_shapes = [shape(3 * count, width, width)]
        scratch = [
            pltpu.VMEM((plan.group * plan.share, width, width), BF16),
            pltpu.VMEM((3 * count, width, width), F32),
            pltpu.VMEM((3 * count, width, width), F32),
            pltpu.VMEM((3 * count, width, width), F32),
            pltpu.VMEM((count, 3, n * t, width), F32),
            pltpu.VMEM((count, 3, n * t, width), BF16),
        ]
        if last:
            scratch.append(pltpu.VMEM((n_dp * own, width, width), BF16))
        before = sums if last else []
        outs = call(
            bind(chunk_kernel, chunk=c),
            [shape(n, 2 * t, count * width)] + c_shapes,
            (from_ids, dp_id, *a_in, *shares, *b_in[c], *before),
            [SMEM] * 2 + [VMEM] * (n + plan.group + len(b_in[c]) + len(before)),
            [VMEM] * (1 + len(c_shapes)),
            f"chunk{c}",
            scratch,
            flops=count * 640 * 10**6,
            size=count * 10**6,
            vmem=VMEM_LARGE,
        )
        d_sent.append(outs[0])
        sums = outs[1:]
    c_keep, c_send = sums

    halves = call(
        bind(pair_kernel),
        [shape(own, width, width)] * plan.rest,
        (dp_id, c_keep, swap(c_send, plan.pair - 1)),
        [SMEM] + [VMEM] * 2,
        [VMEM] * plan.rest,
        "state_pair",
        [pltpu.VMEM((plan.rest * own, width, width), F32)],
    )
    halves = [swap(halves[k], plan.pair * k) for k in range(plan.rest)]
    by_rows = call(
        bind(sum_kernel),
        [shape(own, rows, width)] * n,
        (to_ids, *halves),
        [SMEM] + [VMEM] * plan.rest,
        [VMEM] * n,
        "state_sum",
        [pltpu.VMEM((own, width, width), F32)],
    )
    back = [turn(d_sent[0])]
    by_rows = shift(by_rows)
    by_rows[0], back[0] = lax.optimization_barrier((by_rows[0], back[0]))
    mine = call(
        bind(order_kernel),
        shape(n, own, rows, width),
        (from_ids, *by_rows),
        [SMEM] + [VMEM] * n,
        VMEM,
        "state_rows",
    )
    mine, late = lax.optimization_barrier((mine, d_sent[1]))
    back.append(turn(late))
    rest = [swap(mine, plan.pair * k) for k in range(plan.rest)]
    half = call(
        bind(order_kernel),
        shape(plan.rest, n, own, rows, width),
        (rest_ids, *rest),
        [SMEM] + [VMEM] * plan.rest,
        VMEM,
        "state_rest",
    )
    both = [swap(half, k) for k in range(plan.pair)]
    grad_state = call(
        bind(state_kernel),
        shape(*state_start.shape, dtype=F32),
        (dp_id, *both),
        [SMEM] + [VMEM] * plan.pair,
        VMEM,
        "state_out",
    )
    grad_keys, grad_values = call(
        bind(unpack_kernel),
        [shape(*keys_a.shape), shape(*values_a.shape)],
        back,
        [VMEM] * len(back),
        [ANY] * 2,
        "unpack",
        [pltpu.SemaphoreType.DMA((2 * n * len(chunks),))],
    )
    return grad_keys, grad_values, grad_state


def solution(mesh):
    placed = (
        P("dp", "ctx", None),
        P("dp", "ctx", None),
        P("dp", "ctx", None),
        P("dp", "ctx", None),
        P(None, None, "ctx", None),
        P("dp", None, None, "ctx", None),
    )
    return jax.shard_map(
        local,
        mesh=mesh,
        in_specs=placed,
        out_specs=(P("dp", "ctx", None), P("dp", "ctx", None), P(None, None, "ctx", None)),
        check_vma=False,
    )
```

```python
import functools

import jax
import jax.numpy as jnp
from jax import lax
from jax.experimental import pallas as pl
from jax.experimental.pallas import tpu as pltpu
from jax.sharding import PartitionSpec as P

RATE = 4.0
CA = 3.4445
CB = -4.775
CC = 2.0315
STEPS = 2
F32 = jnp.float32
BF16 = jnp.bfloat16
VMEM_SMALL = 8 * 1024 * 1024
VMEM_LARGE = 28 * 1024 * 1024
SMEM = pl.BlockSpec(memory_space=pltpu.SMEM)
VMEM = pl.BlockSpec(memory_space=pltpu.VMEM)
ANY = pl.BlockSpec(memory_space=pl.ANY)
HBM = pl.BlockSpec(memory_space=pltpu.HBM)


def dot_nn(a, b):
    return lax.dot_general(a, b, (((1,), (0,)), ((), ())), preferred_element_type=F32)


def dot_nt(a, b):
    return lax.dot_general(a, b, (((1,), (1,)), ((), ())), preferred_element_type=F32)


def dot_tn(a, b):
    return lax.dot_general(a, b, (((0,), (0,)), ((), ())), preferred_element_type=F32)


def call(
    kernel, out_shape, args, in_specs, out_specs, name, scratch=(), flops=10**6, size=10**6, vmem=VMEM_SMALL
):
    return pl.pallas_call(
        kernel,
        out_shape=out_shape,
        in_specs=in_specs,
        out_specs=out_specs,
        scratch_shapes=list(scratch),
        compiler_params=pltpu.CompilerParams(vmem_limit_bytes=vmem),
        cost_estimate=pl.CostEstimate(flops=flops, bytes_accessed=size, transcendentals=0),
        name=name,
    )(*args)


def swish_terms(g):
    s = 1.0 / (1.0 + jnp.exp(-g))
    sw = g * s
    slope = s * (1.0 + g * (1.0 - s))
    return s, sw, slope


def newton_pullback(grads, updates):
    each = range(len(grads))
    inv = [lax.rsqrt(jnp.sum(g * g, keepdims=True) + 1e-06) for g in grads]
    xs = [[(grads[m] * inv[m]).astype(BF16) for m in each]]
    grams = []
    polys = []
    for step in range(STEPS):
        x = xs[-1]
        gram = [dot_nt(x[m], x[m]).astype(BF16) for m in each]
        poly = [(CB * gram[m].astype(F32) + CC * dot_nn(gram[m], gram[m])).astype(BF16) for m in each]
        grams.append(gram)
        polys.append(poly)
        if step + 1 < STEPS:
            xs.append([(CA * x[m].astype(F32) + dot_nn(poly[m], x[m])).astype(BF16) for m in each])
    d = updates
    for step in reversed(range(STEPS)):
        x, gram, poly = xs[step], grams[step], polys[step]
        dp = [dot_nt(d[m], x[m]) for m in each]
        sym = [dp[m] + dp[m].T for m in each]
        turned = [dot_nn(sym[m].astype(BF16), gram[m]) for m in each]
        da = [(CB * sym[m] + CC * (turned[m] + turned[m].T)).astype(BF16) for m in each]
        d = [
            (CA * d[m].astype(F32) + dot_nn(poly[m], d[m]) + dot_nn(da[m], x[m])).astype(BF16)
            for m in each
        ]
    out = []
    for m in each:
        df = d[m].astype(F32)
        along = jnp.sum(df * grads[m], keepdims=True)
        out.append(df * inv[m] - grads[m] * (along * (inv[m] * inv[m] * inv[m])))
    return out


class Plan:
    def __init__(self, n, n_dp, tokens, heads, rows, width):
        self.n, self.n_dp = n, n_dp
        self.tokens, self.heads, self.rows, self.width = tokens, heads, rows, width
        self.per = -(-heads // n)
        self.mats = 3 * self.per
        early = max(1, self.per - 1)
        self.chunks = [c for c in ((0, early), (early, self.per - early)) if c[1] > 0]
        self.group = min(4, n_dp)
        self.share = -(-self.mats // self.group)
        self.pair = min(2, n_dp)
        self.rest = n_dp // self.pair
        self.own = -(-self.mats // n_dp)
        self.block = -(-rows // 16) * 16
        self.share_rows = -(-self.share // self.per) * self.block

    def first_head(self, c):
        return min(c * self.per, self.heads - self.per)


def pack_a_kernel(dp_ref, k_ref, v_ref, s_ref, out, state, sems, *, plan):
    n, t, w, per = plan.n, plan.tokens, plan.width, plan.per
    low = lax.rem(dp_ref[0], plan.group)
    loads = []
    copies = []
    for c in range(n):
        for q in range(plan.share):
            mat = jnp.minimum(low * plan.share + q, plan.mats - 1)
            load = pltpu.make_async_copy(
                s_ref.at[lax.rem(mat, 3), plan.first_head(c) + lax.div(mat, 3)],
                state.at[c, q],
                sems.at[c, 2 + q],
            )
            load.start()
            loads.append(load)
        cols = pl.ds(plan.first_head(c) * w, per * w)
        for part, src in enumerate((k_ref, v_ref)):
            copy = pltpu.make_async_copy(
                src.at[0, :, cols], out.at[c, pl.ds(part * t, t), :], sems.at[c, part]
            )
            copy.start()
            copies.append(copy)
    for load in loads:
        load.wait()
    for c in range(n):
        for q in range(plan.share):
            top = 2 * t + (q // per) * plan.block
            left = (q % per) * w
            out[c, top : top + plan.rows, left : left + w] = state[c, q].astype(BF16)
    for copy in copies:
        copy.wait()


def pack_b_kernel(head_ref, q_ref, o_ref, s_ref, *refs, plan, chunk):
    n, t, w = plan.n, plan.tokens, plan.width
    first, count = plan.chunks[chunk]
    outs, (state, sems) = refs[:-2], refs[-2:]
    if len(outs) < n:
        outs = [outs[0].at[c] for c in range(n)]
        heads = [plan.first_head(c) + first for c in range(n)]
        offsets = [head * w for head in heads]
    else:
        heads = [head_ref[slot] + first for slot in range(n)]
        offsets = [pl.multiple_of(head * w, w) for head in heads]
    loads = []
    copies = []
    for k in range(n):
        load = pltpu.make_async_copy(
            s_ref.at[0, :, pl.ds(heads[k], count)], state.at[k], sems.at[3 * k + 2]
        )
        load.start()
        loads.append(load)
        for part, src in enumerate((q_ref, o_ref)):
            copy = pltpu.make_async_copy(
                src.at[0, :, pl.ds(offsets[k], count * w)],
                outs[k].at[pl.ds(part * t, t), :],
                sems.at[3 * k + part],
            )
            copy.start()
            copies.append(copy)
    for k in range(n):
        loads[k].wait()
        for j in range(count):
            for m in range(3):
                top = 2 * t + m * plan.block
                outs[k][top : top + plan.rows, j * w : (j + 1) * w] = state[k, m, j].astype(BF16)
    for copy in copies:
        copy.wait()


def start_kernel(a_ref, out, whole, *, plan):
    rows, w = plan.rows, plan.width
    for c in range(plan.n):
        for q in range(plan.share):
            top = 2 * plan.tokens + (q // plan.per) * plan.block
            left = (q % plan.per) * w
            part = a_ref[c, top : top + rows, left : left + w]
            whole[q, c * rows : (c + 1) * rows, :] = part.astype(F32)
    out[...] = whole[...].astype(BF16)


def tokens_of(refs, j, plan):
    t, w = plan.tokens, plan.width
    cols = slice(j * w, (j + 1) * w)
    x = jnp.concatenate([r[0:t, cols] for r in refs], axis=0)
    y = jnp.concatenate([r[t : 2 * t, cols] for r in refs], axis=0)
    return x, y


def forward(x, y, wa, wb, wc):
    w = wa.shape[1]
    gu = dot_nn(x, jnp.concatenate([wa, wb], axis=1))
    g, u = gu[:, :w], gu[:, w:]
    p = dot_nn(y, wc)
    _, sw, slope = swish_terms(g)
    hidden = (sw * u).astype(BF16)
    dg = (p * u * slope).astype(BF16)
    du = (p * sw).astype(BF16)
    ab = dot_tn(x, jnp.concatenate([dg, du], axis=1))
    return (ab[:, :w], ab[:, w:], dot_tn(y, hidden)), (g, u, p), (dg, du, hidden)


def chunk_kernel(from_ref, dp_ref, *refs, plan, chunk):
    n, t, w = plan.n, plan.tokens, plan.width
    first, count = plan.chunks[chunk]
    last = chunk + 1 == len(plan.chunks)
    mats = 3 * count
    refs = list(refs)

    def take(k):
        got = refs[:k]
        del refs[:k]
        return got

    (a_ref,), shares = take(1), take(plan.group)
    a_refs = [a_ref.at[c] for c in range(n)]
    joined = len(refs[0].shape) == 3
    b_refs = take(1 if joined else n)
    if joined:
        b_refs = [b_refs[0].at[c] for c in range(n)]
        sources = list(range(n))
    else:
        sources = [from_ref[slot] for slot in range(n)]
    before = take(chunk) if last else []
    (d_ref,) = take(1)
    c_refs = take(2 if last else 1)
    w0, w1, gsum, ssum, acts, fields = take(6)
    total = take(1)[0] if last else c_refs[0]
    base = 3 * first if last else 0

    low = lax.rem(dp_ref[0], plan.group)
    for k in range(plan.group):
        at = pl.ds(jnp.bitwise_xor(low, k) * plan.share, plan.share)
        w0[at] = shares[k][...]
    for slot in range(n):
        row = sources[slot] * plan.rows
        at = pl.ds(row if joined else pl.multiple_of(row, plan.rows), plan.rows)
        for j in range(count):
            for m in range(3):
                top = 2 * t + m * plan.block
                part = b_refs[slot][top : top + plan.rows, j * w : (j + 1) * w]
                w1[3 * j + m, at, :] = part.astype(F32)

    for j in range(count):
        at = 3 * (first + j)
        x, y = tokens_of(a_refs, first + j, plan)
        sums, act, field = forward(x, y, w0[at], w0[at + 1], w0[at + 2])
        for m in range(3):
            gsum[3 * j + m] = sums[m]
            acts[j, m] = act[m]
            fields[j, m] = field[m]
        x, y = tokens_of(b_refs, j, plan)
        sums, _, _ = forward(x, y, *[w1[3 * j + m].astype(BF16) for m in range(3)])
        for m in range(3):
            ssum[3 * j + m] = sums[m]

    grads = [gsum[m] for m in range(mats)]
    updates = [(RATE * ssum[m]).astype(BF16) for m in range(mats)]
    for m, val in enumerate(newton_pullback(grads, updates)):
        gsum[m] = val

    for j in range(count):
        at = 3 * (first + j)
        x, y = tokens_of(a_refs, first + j, plan)
        fab = jnp.concatenate([gsum[3 * j], gsum[3 * j + 1]], axis=1).astype(BF16)
        fc = gsum[3 * j + 2].astype(BF16)
        wab = jnp.concatenate([w0[at], w0[at + 1]], axis=1)
        wc = w0[at + 2]
        cdgu = dot_nn(x, fab)
        cdg, cdu = cdgu[:, :w], cdgu[:, w:]
        ch = dot_nn(y, fc)
        g, u, p = acts[j, 0], acts[j, 1], acts[j, 2]
        s, sw, slope = swish_terms(g)
        curve = s * (1.0 - s) * (2.0 + g * (1.0 - 2.0 * s))
        cg = ((ch * u + cdu * p) * slope + cdg * (p * u) * curve).astype(BF16)
        cu = (ch * sw + cdg * p * slope).astype(BF16)
        cp = (cdu * sw + cdg * u * slope).astype(BF16)
        dg, du, hidden = fields[j, 0], fields[j, 1], fields[j, 2]
        dx = dot_nt(jnp.concatenate([dg, du, cg, cu], axis=1), jnp.concatenate([fab, wab], axis=1))
        dy = dot_nt(jnp.concatenate([hidden, cp], axis=1), jnp.concatenate([fc, wc], axis=1))
        cols = slice(j * w, (j + 1) * w)
        for c in range(n):
            d_ref[c, 0:t, cols] = dx[c * t : (c + 1) * t].astype(BF16)
            d_ref[c, t : 2 * t, cols] = dy[c * t : (c + 1) * t].astype(BF16)
        ab = dot_tn(x, jnp.concatenate([cg, cu], axis=1))
        grown = (ab[:, :w], ab[:, w:], dot_tn(y, cp))
        for m in range(3):
            total[base + 3 * j + m] = (ssum[3 * j + m] + grown[m]).astype(BF16)

    if last:
        for c, part in enumerate(before):
            at = 3 * plan.chunks[c][0]
            total[at : at + part.shape[0]] = part[...]
        for m in range(plan.mats, plan.n_dp * plan.own):
            total[m] = jnp.zeros((w, w), BF16)
        mine = lax.rem(dp_ref[0], plan.pair)
        for r in range(plan.rest):
            to = slice(r * plan.own, (r + 1) * plan.own)
            for ref, which in zip(c_refs, (mine, plan.pair - 1 - mine)):
                ref[to] = total[pl.ds((plan.pair * r + which) * plan.own, plan.own)]


def pair_kernel(dp_ref, keep_ref, got_ref, *refs, plan):
    outs, whole = refs[:-1], refs[-1]
    whole[...] = keep_ref[...].astype(F32) + got_ref[...].astype(F32)
    place = lax.div(dp_ref[0], plan.pair)
    for k in range(plan.rest):
        at = pl.ds(jnp.bitwise_xor(place, k) * plan.own, plan.own)
        outs[k][...] = whole[at].astype(BF16)


def sum_kernel(to_ref, *refs, plan):
    parts, outs, whole = refs[: plan.rest], refs[plan.rest : -1], refs[-1]
    added = parts[0][...].astype(F32)
    for part in parts[1:]:
        added = added + part[...].astype(F32)
    whole[...] = added / plan.n_dp
    for slot in range(plan.n):
        at = pl.ds(pl.multiple_of(to_ref[slot] * plan.rows, plan.rows), plan.rows)
        outs[slot][...] = whole[:, at, :].astype(BF16)


def order_kernel(place_ref, *refs, plan):
    parts, out = refs[:-1], refs[-1]
    for k, part in enumerate(parts):
        out[place_ref[k]] = part[...]


def state_kernel(dp_ref, *refs, plan):
    out = refs[-1]
    mine = lax.rem(dp_ref[0], plan.pair)
    for k in range(plan.pair):
        for r in range(plan.rest):
            for i in range(plan.own):
                mat = (plan.pair * r + jnp.bitwise_xor(mine, k)) * plan.own + i

                @pl.when(mat < plan.mats)
                def _(mat=mat, ref=refs[k], r=r, i=i):
                    for c in range(plan.n):
                        out[lax.rem(mat, 3), plan.first_head(c) + lax.div(mat, 3)] = ref[r, c, i].astype(F32)


def unpack_kernel(*refs, plan):
    t, w = plan.tokens, plan.width
    ins, (dk, dv, sems) = refs[:-3], refs[-3:]
    copies = []
    for c, (first, count) in enumerate(plan.chunks):
        for owner in range(plan.n):
            cols = pl.ds((plan.first_head(owner) + first) * w, count * w)
            for part, dst in enumerate((dk, dv)):
                copy = pltpu.make_async_copy(
                    ins[c].at[owner, pl.ds(part * t, t), :],
                    dst.at[0, :, cols],
                    sems.at[(c * plan.n + owner) * 2 + part],
                )
                copy.start()
                copies.append(copy)
            if plan.n * plan.per != plan.heads:
                for copy in copies:
                    copy.wait()
                copies = []
    for copy in copies:
        copy.wait()


def local(keys_a, values_a, queries_b, grad_out, state_start, state_next):
    n, n_dp = lax.axis_size("ctx"), lax.axis_size("dp")
    _, heads, rows, width = state_start.shape
    t = keys_a.shape[1]
    plan = Plan(n, n_dp, t, heads, rows, width)
    per, mats, own, chunks = plan.per, plan.mats, plan.own, plan.chunks
    bind = lambda kernel, **more: functools.partial(kernel, plan=plan, **more)

    keys_a, values_a, grad_out, state_start, state_next = (
        pltpu.with_memory_space_constraint(arg, pltpu.HBM)
        for arg in (keys_a, values_a, grad_out, state_start, state_next)
    )
    me = lax.axis_index("ctx")
    places = jnp.arange(n, dtype=jnp.int32)
    to_ids = lax.rem(me + places, n)
    from_ids = lax.rem(me + n - places, n)
    head_ids = jnp.minimum(to_ids * per, heads - per)
    dp_id = lax.axis_index("dp").reshape(1)
    rest_ids = jnp.bitwise_xor(lax.div(dp_id, plan.pair), jnp.arange(plan.rest, dtype=jnp.int32))

    def swap(value, k):
        if k == 0:
            return value
        return lax.ppermute(value, "dp", [(i, i ^ k) for i in range(n_dp)])

    def shift(values):
        return [
            lax.ppermute(v, "ctx", [(i, (i + s) % n) for i in range(n)]) if s else v
            for s, v in enumerate(values)
        ]

    def turn(value):
        return lax.all_to_all(value, "ctx", split_axis=0, concat_axis=0, tiled=True)

    def shape(*dims, dtype=BF16):
        return jax.ShapeDtypeStruct(dims, dtype)

    def pack_b(c, queries):
        dims = (2 * t + 3 * plan.block, chunks[c][1] * width)
        joined = c > 0
        outs = call(
            bind(pack_b_kernel, chunk=c),
            [shape(n, *dims)] if joined else [shape(*dims)] * n,
            (head_ids, pltpu.with_memory_space_constraint(queries, pltpu.HBM), grad_out, state_next),
            [SMEM] + [HBM] * 3,
            [VMEM] * (1 if joined else n),
            f"pack_b{c}",
            [
                pltpu.VMEM((n, 3, chunks[c][1], rows, width), F32),
                pltpu.SemaphoreType.DMA((3 * n,)),
            ],
        )
        return list(outs)

    a_sent = call(
        bind(pack_a_kernel),
        shape(n, 2 * t + plan.share_rows, per * width),
        (dp_id, keys_a, values_a, state_start),
        [SMEM] + [HBM] * 3,
        VMEM,
        "pack_a",
        [
            pltpu.VMEM((n, plan.share, rows, width), F32),
            pltpu.SemaphoreType.DMA((n, 2 + plan.share)),
        ],
    )
    queries, a_sent = lax.optimization_barrier((queries_b, a_sent))
    a_in = turn(a_sent)
    b_in = [shift(pack_b(0, queries))]
    queries, a_in = lax.optimization_barrier((queries_b, a_in))
    b_in.append([turn(pack_b(1, queries)[0])])
    start_own = call(
        bind(start_kernel),
        shape(plan.share, width, width),
        (a_in,),
        [VMEM],
        VMEM,
        "start_share",
        [pltpu.VMEM((plan.share, width, width), F32)],
    )
    shares = [swap(start_own, k) for k in range(plan.group)]
    d_sent = []
    sums = []
    for c, (_, count) in enumerate(chunks):
        last = c + 1 == len(chunks)
        if last:
            c_shapes = [shape(plan.rest * own, width, width)] * 2
        else:
            c_shapes = [shape(3 * count, width, width)]
        scratch = [
            pltpu.VMEM((plan.group * plan.share, width, width), BF16),
            pltpu.VMEM((3 * count, width, width), F32),
            pltpu.VMEM((3 * count, width, width), F32),
            pltpu.VMEM((3 * count, width, width), F32),
            pltpu.VMEM((count, 3, n * t, width), F32),
            pltpu.VMEM((count, 3, n * t, width), BF16),
        ]
        if last:
            scratch.append(pltpu.VMEM((n_dp * own, width, width), BF16))
        before = sums if last else []
        outs = call(
            bind(chunk_kernel, chunk=c),
            [shape(n, 2 * t, count * width)] + c_shapes,
            (from_ids, dp_id, a_in, *shares, *b_in[c], *before),
            [SMEM] * 2 + [VMEM] * (1 + plan.group + len(b_in[c]) + len(before)),
            [VMEM] * (1 + len(c_shapes)),
            f"chunk{c}",
            scratch,
            flops=count * 640 * 10**6,
            size=count * 10**6,
            vmem=VMEM_LARGE,
        )
        d_sent.append(outs[0])
        sums = outs[1:]
    c_keep, c_send = sums

    halves = call(
        bind(pair_kernel),
        [shape(own, width, width)] * plan.rest,
        (dp_id, c_keep, swap(c_send, plan.pair - 1)),
        [SMEM] + [VMEM] * 2,
        [VMEM] * plan.rest,
        "state_pair",
        [pltpu.VMEM((plan.rest * own, width, width), F32)],
    )
    halves = [swap(halves[k], plan.pair * k) for k in range(plan.rest)]
    by_rows = call(
        bind(sum_kernel),
        [shape(own, rows, width)] * n,
        (to_ids, *halves),
        [SMEM] + [VMEM] * plan.rest,
        [VMEM] * n,
        "state_sum",
        [pltpu.VMEM((own, width, width), F32)],
    )
    back = [turn(d_sent[0])]
    by_rows = shift(by_rows)
    by_rows[0], back[0] = lax.optimization_barrier((by_rows[0], back[0]))
    mine = call(
        bind(order_kernel),
        shape(n, own, rows, width),
        (from_ids, *by_rows),
        [SMEM] + [VMEM] * n,
        VMEM,
        "state_rows",
    )
    mine, late = lax.optimization_barrier((mine, d_sent[1]))
    back.append(turn(late))
    rest = [swap(mine, plan.pair * k) for k in range(plan.rest)]
    half = call(
        bind(order_kernel),
        shape(plan.rest, n, own, rows, width),
        (rest_ids, *rest),
        [SMEM] + [VMEM] * plan.rest,
        VMEM,
        "state_rest",
    )
    both = [swap(half, k) for k in range(plan.pair)]
    grad_state = call(
        bind(state_kernel),
        shape(*state_start.shape, dtype=F32),
        (dp_id, *both),
        [SMEM] + [VMEM] * plan.pair,
        VMEM,
        "state_out",
    )
    grad_keys, grad_values = call(
        bind(unpack_kernel),
        [shape(*keys_a.shape), shape(*values_a.shape)],
        back,
        [VMEM] * len(back),
        [ANY] * 2,
        "unpack",
        [pltpu.SemaphoreType.DMA((2 * n * len(chunks),))],
    )
    return grad_keys, grad_values, grad_state


def solution(mesh):
    placed = (
        P("dp", "ctx", None),
        P("dp", "ctx", None),
        P("dp", "ctx", None),
        P("dp", "ctx", None),
        P(None, None, "ctx", None),
        P("dp", None, None, "ctx", None),
    )
    return jax.shard_map(
        local,
        mesh=mesh,
        in_specs=placed,
        out_specs=(P("dp", "ctx", None), P("dp", "ctx", None), P(None, None, "ctx", None)),
        check_vma=False,
    )
```

```python
import functools

import jax
import jax.numpy as jnp
from jax import lax
from jax.experimental import pallas as pl
from jax.experimental.pallas import tpu as pltpu
from jax.sharding import PartitionSpec as P

RATE = 4.0
CA = 3.4445
CB = -4.775
CC = 2.0315
STEPS = 2
F32 = jnp.float32
BF16 = jnp.bfloat16
VMEM_SMALL = 8 * 1024 * 1024
VMEM_LARGE = 28 * 1024 * 1024
SMEM = pl.BlockSpec(memory_space=pltpu.SMEM)
VMEM = pl.BlockSpec(memory_space=pltpu.VMEM)
ANY = pl.BlockSpec(memory_space=pl.ANY)
HBM = pl.BlockSpec(memory_space=pltpu.HBM)


def dot_nn(a, b):
    return lax.dot_general(a, b, (((1,), (0,)), ((), ())), preferred_element_type=F32)


def dot_nt(a, b):
    return lax.dot_general(a, b, (((1,), (1,)), ((), ())), preferred_element_type=F32)


def dot_tn(a, b):
    return lax.dot_general(a, b, (((0,), (0,)), ((), ())), preferred_element_type=F32)


def call(
    kernel, out_shape, args, in_specs, out_specs, name, scratch=(), flops=10**6, size=10**6, vmem=VMEM_SMALL
):
    return pl.pallas_call(
        kernel,
        out_shape=out_shape,
        in_specs=in_specs,
        out_specs=out_specs,
        scratch_shapes=list(scratch),
        compiler_params=pltpu.CompilerParams(vmem_limit_bytes=vmem),
        cost_estimate=pl.CostEstimate(flops=flops, bytes_accessed=size, transcendentals=0),
        name=name,
    )(*args)


def swish_terms(g):
    s = 1.0 / (1.0 + jnp.exp(-g))
    sw = g * s
    slope = s * (1.0 + g * (1.0 - s))
    return s, sw, slope


def newton_pullback(grads, updates):
    each = range(len(grads))
    inv = [lax.rsqrt(jnp.sum(g * g, keepdims=True) + 1e-06) for g in grads]
    xs = [[(grads[m] * inv[m]).astype(BF16) for m in each]]
    grams = []
    polys = []
    for step in range(STEPS):
        x = xs[-1]
        gram = [dot_nt(x[m], x[m]).astype(BF16) for m in each]
        poly = [(CB * gram[m].astype(F32) + CC * dot_nn(gram[m], gram[m])).astype(BF16) for m in each]
        grams.append(gram)
        polys.append(poly)
        if step + 1 < STEPS:
            xs.append([(CA * x[m].astype(F32) + dot_nn(poly[m], x[m])).astype(BF16) for m in each])
    d = updates
    for step in reversed(range(STEPS)):
        x, gram, poly = xs[step], grams[step], polys[step]
        dp = [dot_nt(d[m], x[m]) for m in each]
        sym = [dp[m] + dp[m].T for m in each]
        turned = [dot_nn(sym[m].astype(BF16), gram[m]) for m in each]
        da = [(CB * sym[m] + CC * (turned[m] + turned[m].T)).astype(BF16) for m in each]
        d = [
            (CA * d[m].astype(F32) + dot_nn(poly[m], d[m]) + dot_nn(da[m], x[m])).astype(BF16)
            for m in each
        ]
    out = []
    for m in each:
        df = d[m].astype(F32)
        along = jnp.sum(df * grads[m], keepdims=True)
        out.append(df * inv[m] - grads[m] * (along * (inv[m] * inv[m] * inv[m])))
    return out


class Plan:
    def __init__(self, n, n_dp, tokens, heads, rows, width):
        self.n, self.n_dp = n, n_dp
        self.tokens, self.heads, self.rows, self.width = tokens, heads, rows, width
        self.per = -(-heads // n)
        self.mats = 3 * self.per
        most = max(1, self.per - 1)
        self.chunks = [(0, most), (most, self.per - most)]
        self.early = (most + 2) // 2
        self.pair = min(2, n_dp)
        self.rest = n_dp // self.pair
        self.own = -(-self.mats // n_dp)
        self.block = -(-rows // 16) * 16
        self.packed_rows = 4 * tokens + 6 * self.block
        self.ids = {}
        at = 0
        for name, size in (("to", n), ("from", n), ("head", n), ("rest", self.rest), ("mine", 1), ("place", 1)):
            self.ids[name] = at
            at += size

    def first_head(self, c):
        return min(c * self.per, self.heads - self.per)


def pack_kernel(ids, k_ref, v_ref, q_ref, o_ref, s_ref, t_ref, *refs, plan, slots, chunk):
    t, w = plan.tokens, plan.width
    first, count = plan.chunks[chunk]
    outs, (state, sems) = refs[:-2], refs[-2:]
    loads = []
    copies = []
    for k, slot in enumerate(slots):
        head = ids[plan.ids["head"] + slot] + first
        for i, src in enumerate((s_ref, t_ref.at[0])):
            loads.append(
                pltpu.make_async_copy(src.at[:, pl.ds(head, count)], state.at[k, i], sems.at[k, 4 + i])
            )
            loads[-1].start()
        cols = pl.ds(pl.multiple_of(head * w, w), count * w)
        for i, src in enumerate((k_ref, v_ref, q_ref, o_ref)):
            copies.append(
                pltpu.make_async_copy(src.at[0, :, cols], outs[k].at[pl.ds(i * t, t), :], sems.at[k, i])
            )
            copies[-1].start()
    for k in range(len(slots)):
        for i in range(2):
            loads[2 * k + i].wait()
            for j in range(count):
                for m in range(3):
                    top = 4 * t + (3 * i + m) * plan.block
                    outs[k][top : top + plan.rows, j * w : (j + 1) * w] = state[k, i, m, j].astype(BF16)
    for copy in copies:
        copy.wait()


def tokens_of(refs, j, group, plan):
    t, w = plan.tokens, plan.width
    cols = slice(j * w, (j + 1) * w)
    top = 2 * group * t
    x = jnp.concatenate([r[top : top + t, cols] for r in refs], axis=0)
    y = jnp.concatenate([r[top + t : top + 2 * t, cols] for r in refs], axis=0)
    return x, y


def forward(x, y, wa, wb, wc):
    w = wa.shape[1]
    gu = dot_nn(x, jnp.concatenate([wa, wb], axis=1))
    g, u = gu[:, :w], gu[:, w:]
    p = dot_nn(y, wc)
    _, sw, slope = swish_terms(g)
    hidden = (sw * u).astype(BF16)
    dg = (p * u * slope).astype(BF16)
    du = (p * sw).astype(BF16)
    ab = dot_tn(x, jnp.concatenate([dg, du], axis=1))
    return (ab[:, :w], ab[:, w:], dot_tn(y, hidden)), (g, u, p), (dg, du, hidden)


def chunk_kernel(ids, *refs, plan, chunk):
    n, t, w = plan.n, plan.tokens, plan.width
    first, count = plan.chunks[chunk]
    last = chunk + 1 == len(plan.chunks)
    mats = 3 * count
    refs = list(refs)

    def take(k):
        got = refs[:k]
        del refs[:k]
        return got

    in_refs = take(n)
    before, held = take(2) if last else (None, None)
    d_refs = take(1 if last else 2)
    c_refs = take(2 if last else 1)
    w0, w1, gsum, ssum, acts, fields = take(6)
    total = take(1)[0] if last else c_refs[0]
    base = 3 * first if last else 0

    for slot in range(n):
        at = pl.ds(pl.multiple_of(ids[plan.ids["from"] + slot] * plan.rows, plan.rows), plan.rows)
        for j in range(count):
            for m in range(3):
                for i, dst in enumerate((w0, w1)):
                    top = 4 * t + (3 * i + m) * plan.block
                    part = in_refs[slot][top : top + plan.rows, j * w : (j + 1) * w]
                    dst[3 * j + m, at, :] = part.astype(F32)

    for j in range(count):
        x, y = tokens_of(in_refs, j, 0, plan)
        sums, act, field = forward(x, y, *[w0[3 * j + m].astype(BF16) for m in range(3)])
        for m in range(3):
            gsum[3 * j + m] = sums[m]
            acts[j, m] = act[m]
            fields[j, m] = field[m]
        x, y = tokens_of(in_refs, j, 1, plan)
        sums, _, _ = forward(x, y, *[w1[3 * j + m].astype(BF16) for m in range(3)])
        for m in range(3):
            ssum[3 * j + m] = sums[m]

    grads = [gsum[m] for m in range(mats)]
    updates = [(RATE * ssum[m]).astype(BF16) for m in range(mats)]
    for m, val in enumerate(newton_pullback(grads, updates)):
        gsum[m] = val

    for j in range(count):
        x, y = tokens_of(in_refs, j, 0, plan)
        fab = jnp.concatenate([gsum[3 * j], gsum[3 * j + 1]], axis=1).astype(BF16)
        fc = gsum[3 * j + 2].astype(BF16)
        wab = jnp.concatenate([w0[3 * j], w0[3 * j + 1]], axis=1).astype(BF16)
        wc = w0[3 * j + 2].astype(BF16)
        cdgu = dot_nn(x, fab)
        cdg, cdu = cdgu[:, :w], cdgu[:, w:]
        ch = dot_nn(y, fc)
        g, u, p = acts[j, 0], acts[j, 1], acts[j, 2]
        s, sw, slope = swish_terms(g)
        curve = s * (1.0 - s) * (2.0 + g * (1.0 - 2.0 * s))
        cg = ((ch * u + cdu * p) * slope + cdg * (p * u) * curve).astype(BF16)
        cu = (ch * sw + cdg * p * slope).astype(BF16)
        cp = (cdu * sw + cdg * u * slope).astype(BF16)
        dg, du, hidden = fields[j, 0], fields[j, 1], fields[j, 2]
        dx = dot_nt(jnp.concatenate([dg, du, cg, cu], axis=1), jnp.concatenate([fab, wab], axis=1))
        dy = dot_nt(jnp.concatenate([hidden, cp], axis=1), jnp.concatenate([fc, wc], axis=1))
        if last:
            d_ref, at = d_refs[0], first - plan.early + j
        elif j < plan.early:
            d_ref, at = d_refs[0], j
        else:
            d_ref, at = d_refs[1], j - plan.early
        cols = slice(at * w, (at + 1) * w)
        for slot in range(n):
            to = ids[plan.ids["from"] + slot]
            d_ref[to, 0:t, cols] = dx[slot * t : (slot + 1) * t].astype(BF16)
            d_ref[to, t : 2 * t, cols] = dy[slot * t : (slot + 1) * t].astype(BF16)
        ab = dot_tn(x, jnp.concatenate([cg, cu], axis=1))
        grown = (ab[:, :w], ab[:, w:], dot_tn(y, cp))
        for m in range(3):
            total[base + 3 * j + m] = (ssum[3 * j + m] + grown[m]).astype(BF16)

    if last:
        total[0 : before.shape[0]] = before[...]
        if first > plan.early:
            d_refs[0][:, :, 0 : held.shape[2]] = held[...]
        for m in range(plan.mats, plan.n_dp * plan.own):
            total[m] = jnp.zeros((w, w), BF16)
        mine = ids[plan.ids["mine"]]
        for r in range(plan.rest):
            to = slice(r * plan.own, (r + 1) * plan.own)
            for ref, which in zip(c_refs, (mine, plan.pair - 1 - mine)):
                ref[to] = total[pl.ds((plan.pair * r + which) * plan.own, plan.own)]


def pair_kernel(ids, keep_ref, got_ref, *refs, plan):
    outs, whole = refs[:-1], refs[-1]
    whole[...] = keep_ref[...].astype(F32) + got_ref[...].astype(F32)
    for k in range(plan.rest):
        outs[k][...] = whole[pl.ds(ids[plan.ids["rest"] + k] * plan.own, plan.own)].astype(BF16)


def sum_kernel(ids, *refs, plan):
    parts, outs, whole = refs[: plan.rest], refs[plan.rest : -1], refs[-1]
    added = parts[0][...].astype(F32)
    for part in parts[1:]:
        added = added + part[...].astype(F32)
    whole[...] = added / plan.n_dp
    for slot in range(plan.n):
        at = pl.ds(pl.multiple_of(ids[plan.ids["to"] + slot] * plan.rows, plan.rows), plan.rows)
        outs[slot][...] = whole[:, at, :].astype(BF16)


def order_kernel(ids, *refs, plan, name):
    parts, out = refs[:-1], refs[-1]
    for k, part in enumerate(parts):
        out[ids[plan.ids[name] + k]] = part[...]


def state_kernel(ids, *refs, plan):
    out = refs[-1]
    for k in range(plan.pair):
        for r in range(plan.rest):
            for i in range(plan.own):
                mat = (plan.pair * r + jnp.bitwise_xor(ids[plan.ids["mine"]], k)) * plan.own + i

                @pl.when(mat < plan.mats)
                def _(mat=mat, ref=refs[k], r=r, i=i):
                    for c in range(plan.n):
                        head = plan.first_head(c) + lax.div(mat, 3)
                        out[lax.rem(mat, 3), head] = ref[r, c, i].astype(F32)


def unpack_kernel(*refs, plan):
    t, w = plan.tokens, plan.width
    ins, (dk, dv, sems) = refs[:-3], refs[-3:]
    copies = []
    parts = [(0, plan.early), (plan.early, plan.per - plan.early)]
    for c, (first, count) in enumerate(parts):
        for owner in range(plan.n):
            cols = pl.ds((plan.first_head(owner) + first) * w, count * w)
            for part, dst in enumerate((dk, dv)):
                copy = pltpu.make_async_copy(
                    ins[c].at[owner, pl.ds(part * t, t), :],
                    dst.at[0, :, cols],
                    sems.at[(c * plan.n + owner) * 2 + part],
                )
                copy.start()
                copies.append(copy)
            if plan.n * plan.per != plan.heads:
                for copy in copies:
                    copy.wait()
                copies = []
    for copy in copies:
        copy.wait()


def local(keys_a, values_a, queries_b, grad_out, state_start, state_next):
    n, n_dp = lax.axis_size("ctx"), lax.axis_size("dp")
    _, heads, rows, width = state_start.shape
    t = keys_a.shape[1]
    plan = Plan(n, n_dp, t, heads, rows, width)
    per, own, chunks = plan.per, plan.own, plan.chunks
    bind = lambda kernel, **more: functools.partial(kernel, plan=plan, **more)

    me, dp = lax.axis_index("ctx"), lax.axis_index("dp")
    places = jnp.arange(n, dtype=jnp.int32)
    to_ids = lax.rem(me + places, n)
    place = lax.div(dp, plan.pair)
    ids = jnp.concatenate(
        [
            to_ids,
            lax.rem(me + n - places, n),
            jnp.minimum(to_ids * per, heads - per),
            jnp.bitwise_xor(place, jnp.arange(plan.rest, dtype=jnp.int32)),
            lax.rem(dp, plan.pair).reshape(1),
            place.reshape(1),
        ]
    )

    def swap(value, k):
        if k == 0:
            return value
        return lax.ppermute(value, "dp", [(i, i ^ k) for i in range(n_dp)])

    def shift(value, s):
        if s == 0:
            return value
        return lax.ppermute(value, "ctx", [(i, (i + s) % n) for i in range(n)])

    def turn(value):
        return lax.all_to_all(value, "ctx", split_axis=0, concat_axis=0, tiled=True)

    def shape(*dims, dtype=BF16):
        return jax.ShapeDtypeStruct(dims, dtype)

    def pack(c, slots, keys):
        args = (keys, values_a, queries_b, grad_out, state_start, state_next)
        outs = call(
            bind(pack_kernel, slots=slots, chunk=c),
            [shape(plan.packed_rows, chunks[c][1] * width)] * len(slots),
            (ids, *[pltpu.with_memory_space_constraint(arg, pltpu.HBM) for arg in args]),
            [SMEM] + [HBM] * 6,
            [VMEM] * len(slots),
            f"pack{c}_{slots[0]}",
            [
                pltpu.VMEM((len(slots), 2, 3, chunks[c][1], rows, width), F32),
                pltpu.SemaphoreType.DMA((len(slots), 6)),
            ],
        )
        return list(outs)

    keys = keys_a
    arrived = []
    for c in range(len(chunks)):
        sent = pack(c, range(1, n), keys)
        keys, sent = lax.optimization_barrier((keys_a, sent))
        arrived.append([shift(v, s + 1) for s, v in enumerate(sent)])
    for c in range(len(chunks)):
        arrived[c] = pack(c, range(1), keys) + arrived[c]

    before = []
    early = None
    for c, (_, count) in enumerate(chunks):
        last = c + 1 == len(chunks)
        if last:
            outs = [shape(n, 2 * t, (per - plan.early) * width)] + [shape(plan.rest * own, width, width)] * 2
        else:
            held = max(1, count - plan.early)
            outs = [
                shape(n, 2 * t, plan.early * width),
                shape(n, 2 * t, held * width),
                shape(3 * count, width, width),
            ]
        scratch = [pltpu.VMEM((3 * count, width, width), F32)] * 4 + [
            pltpu.VMEM((count, 3, n * t, width), F32),
            pltpu.VMEM((count, 3, n * t, width), BF16),
        ]
        if last:
            scratch.append(pltpu.VMEM((n_dp * own, width, width), BF16))
        got = call(
            bind(chunk_kernel, chunk=c),
            outs,
            (ids, *arrived[c], *before),
            [SMEM] + [VMEM] * (n + len(before)),
            [VMEM] * len(outs),
            f"chunk{c}",
            scratch,
            flops=count * 640 * 10**6,
            size=count * 10**6,
            vmem=VMEM_LARGE,
        )
        if not last:
            early = got[0]
            before = [got[2], got[1]]
    late, c_keep, c_send = got
    early, c_send = lax.optimization_barrier((early, c_send))
    early = turn(early)

    halves = call(
        bind(pair_kernel),
        [shape(own, width, width)] * plan.rest,
        (ids, c_keep, swap(c_send, plan.pair - 1)),
        [SMEM] + [VMEM] * 2,
        [VMEM] * plan.rest,
        "state_pair",
        [pltpu.VMEM((plan.rest * own, width, width), F32)],
    )
    halves = [swap(halves[k], plan.pair * k) for k in range(plan.rest)]
    by_rows = call(
        bind(sum_kernel),
        [shape(own, rows, width)] * n,
        (ids, *halves),
        [SMEM] + [VMEM] * plan.rest,
        [VMEM] * n,
        "state_sum",
        [pltpu.VMEM((own, width, width), F32)],
    )
    by_rows = [shift(by_rows[s], s) for s in range(n)]
    by_rows[0], early = lax.optimization_barrier((by_rows[0], early))
    mine = call(
        bind(order_kernel, name="from"),
        shape(n, own, rows, width),
        (ids, *by_rows),
        [SMEM] + [VMEM] * n,
        VMEM,
        "state_rows",
    )
    mine, late = lax.optimization_barrier((mine, late))
    late = turn(late)
    rest = [swap(mine, plan.pair * k) for k in range(plan.rest)]
    half = call(
        bind(order_kernel, name="rest"),
        shape(plan.rest, n, own, rows, width),
        (ids, *rest),
        [SMEM] + [VMEM] * plan.rest,
        VMEM,
        "state_rest",
    )
    both = [swap(half, k) for k in range(plan.pair)]
    grad_state = call(
        bind(state_kernel),
        shape(*state_start.shape, dtype=F32),
        (ids, *both),
        [SMEM] + [VMEM] * plan.pair,
        VMEM,
        "state_out",
    )
    grad_keys, grad_values = call(
        bind(unpack_kernel),
        [shape(*keys_a.shape), shape(*values_a.shape)],
        (early, late),
        [VMEM] * 2,
        [ANY] * 2,
        "unpack",
        [pltpu.SemaphoreType.DMA((4 * n,))],
    )
    return grad_keys, grad_values, grad_state


def solution(mesh):
    placed = (
        P("dp", "ctx", None),
        P("dp", "ctx", None),
        P("dp", "ctx", None),
        P("dp", "ctx", None),
        P(None, None, "ctx", None),
        P("dp", None, None, "ctx", None),
    )
    return jax.shard_map(
        local,
        mesh=mesh,
        in_specs=placed,
        out_specs=(P("dp", "ctx", None), P("dp", "ctx", None), P(None, None, "ctx", None)),
        check_vma=False,
    )
```

```python
import functools

import jax
import jax.numpy as jnp
from jax import lax
from jax.experimental import pallas as pl
from jax.experimental.pallas import tpu as pltpu
from jax.sharding import PartitionSpec as P

RATE = 4.0
CA = 3.4445
CB = -4.775
CC = 2.0315
STEPS = 2
F32 = jnp.float32
BF16 = jnp.bfloat16
VMEM_SMALL = 8 * 1024 * 1024
VMEM_LARGE = 28 * 1024 * 1024
SMEM = pl.BlockSpec(memory_space=pltpu.SMEM)
VMEM = pl.BlockSpec(memory_space=pltpu.VMEM)
ANY = pl.BlockSpec(memory_space=pl.ANY)
HBM = pl.BlockSpec(memory_space=pltpu.HBM)


def dot_nn(a, b):
    return lax.dot_general(a, b, (((1,), (0,)), ((), ())), preferred_element_type=F32)


def dot_nt(a, b):
    return lax.dot_general(a, b, (((1,), (1,)), ((), ())), preferred_element_type=F32)


def dot_tn(a, b):
    return lax.dot_general(a, b, (((0,), (0,)), ((), ())), preferred_element_type=F32)


def call(
    kernel, out_shape, args, in_specs, out_specs, name, scratch=(), flops=10**6, size=10**6, vmem=VMEM_SMALL
):
    return pl.pallas_call(
        kernel,
        out_shape=out_shape,
        in_specs=in_specs,
        out_specs=out_specs,
        scratch_shapes=list(scratch),
        compiler_params=pltpu.CompilerParams(vmem_limit_bytes=vmem),
        cost_estimate=pl.CostEstimate(flops=flops, bytes_accessed=size, transcendentals=0),
        name=name,
    )(*args)


def swish_terms(g):
    s = 1.0 / (1.0 + jnp.exp(-g))
    sw = g * s
    slope = s * (1.0 + g * (1.0 - s))
    return s, sw, slope


def newton_pullback(grads, updates):
    each = range(len(grads))
    inv = [lax.rsqrt(jnp.sum(g * g, keepdims=True) + 1e-06) for g in grads]
    xs = [[(grads[m] * inv[m]).astype(BF16) for m in each]]
    grams = []
    polys = []
    for step in range(STEPS):
        x = xs[-1]
        gram = [dot_nt(x[m], x[m]).astype(BF16) for m in each]
        poly = [(CB * gram[m].astype(F32) + CC * dot_nn(gram[m], gram[m])).astype(BF16) for m in each]
        grams.append(gram)
        polys.append(poly)
        if step + 1 < STEPS:
            xs.append([(CA * x[m].astype(F32) + dot_nn(poly[m], x[m])).astype(BF16) for m in each])
    d = updates
    for step in reversed(range(STEPS)):
        x, gram, poly = xs[step], grams[step], polys[step]
        dp = [dot_nt(d[m], x[m]) for m in each]
        sym = [dp[m] + dp[m].T for m in each]
        turned = [dot_nn(sym[m].astype(BF16), gram[m]) for m in each]
        da = [(CB * sym[m] + CC * (turned[m] + turned[m].T)).astype(BF16) for m in each]
        d = [
            (CA * d[m].astype(F32) + dot_nn(poly[m], d[m]) + dot_nn(da[m], x[m])).astype(BF16)
            for m in each
        ]
    out = []
    for m in each:
        df = d[m].astype(F32)
        along = jnp.sum(df * grads[m], keepdims=True)
        out.append(df * inv[m] - grads[m] * (along * (inv[m] * inv[m] * inv[m])))
    return out


class Plan:
    def __init__(self, n, n_dp, tokens, heads, rows, width):
        self.n, self.n_dp = n, n_dp
        self.tokens, self.heads, self.rows, self.width = tokens, heads, rows, width
        self.per = -(-heads // n)
        self.mats = 3 * self.per
        most = max(1, self.per - 1)
        self.chunks = [(0, most), (most, self.per - most)]
        self.early = (most + 2) // 2
        self.pair = min(2, n_dp)
        self.rest = n_dp // self.pair
        self.own = -(-self.mats // n_dp)
        self.block = -(-rows // 16) * 16
        self.share = -(-3 * most // self.pair)
        self.share_blocks = -(-self.share // most)
        self.ids = {}
        at = 0
        for name, size in (("to", n), ("from", n), ("head", n), ("rest", self.rest), ("mine", 1), ("place", 1)):
            self.ids[name] = at
            at += size

    def packed_rows(self, chunk):
        return 4 * self.tokens + (3 + (self.share_blocks if chunk == 0 else 3)) * self.block

    def first_head(self, c):
        return min(c * self.per, self.heads - self.per)


def pack_kernel(ids, k_ref, v_ref, q_ref, o_ref, s_ref, t_ref, *refs, plan, slots, chunk):
    t, w = plan.tokens, plan.width
    first, count = plan.chunks[chunk]
    outs, (state, sems) = refs[:-2], refs[-2:]
    loads = []
    copies = []
    for k, slot in enumerate(slots):
        head = ids[plan.ids["head"] + slot] + first
        for i, src in enumerate((s_ref, t_ref.at[0])):
            loads.append(
                pltpu.make_async_copy(src.at[:, pl.ds(head, count)], state.at[k, i], sems.at[k, 4 + i])
            )
            loads[-1].start()
        cols = pl.ds(pl.multiple_of(head * w, w), count * w)
        for i, src in enumerate((k_ref, v_ref, q_ref, o_ref)):
            copies.append(
                pltpu.make_async_copy(src.at[0, :, cols], outs[k].at[pl.ds(i * t, t), :], sems.at[k, i])
            )
            copies[-1].start()
    for k in range(len(slots)):
        loads[2 * k].wait()
        loads[2 * k + 1].wait()
        for j in range(count):
            for m in range(3):
                top = 4 * t + m * plan.block
                outs[k][top : top + plan.rows, j * w : (j + 1) * w] = state[k, 1, m, j].astype(BF16)
                if chunk > 0:
                    top += 3 * plan.block
                    outs[k][top : top + plan.rows, j * w : (j + 1) * w] = state[k, 0, m, j].astype(BF16)
        for q in range(plan.share if chunk == 0 else 0):
            mat = jnp.minimum(ids[plan.ids["mine"]] * plan.share + q, 3 * count - 1)
            top = 4 * t + (3 + q // count) * plan.block
            left = (q % count) * w
            part = state[k, 0, lax.rem(mat, 3), lax.div(mat, 3)]
            outs[k][top : top + plan.rows, left : left + w] = part.astype(BF16)
    for copy in copies:
        copy.wait()


def start_kernel(ids, *refs, plan):
    in_refs, (out, whole) = refs[: plan.n], refs[plan.n :]
    count, w = plan.chunks[0][1], plan.width
    for slot in range(plan.n):
        at = pl.ds(pl.multiple_of(ids[plan.ids["from"] + slot] * plan.rows, plan.rows), plan.rows)
        for q in range(plan.share):
            top = 4 * plan.tokens + (3 + q // count) * plan.block
            left = (q % count) * w
            whole[q, at, :] = in_refs[slot][top : top + plan.rows, left : left + w].astype(F32)
    out[...] = whole[...].astype(BF16)


def tokens_of(refs, j, group, plan):
    t, w = plan.tokens, plan.width
    cols = slice(j * w, (j + 1) * w)
    top = 2 * group * t
    x = jnp.concatenate([r[top : top + t, cols] for r in refs], axis=0)
    y = jnp.concatenate([r[top + t : top + 2 * t, cols] for r in refs], axis=0)
    return x, y


def forward(x, y, wa, wb, wc):
    w = wa.shape[1]
    gu = dot_nn(x, jnp.concatenate([wa, wb], axis=1))
    g, u = gu[:, :w], gu[:, w:]
    p = dot_nn(y, wc)
    _, sw, slope = swish_terms(g)
    hidden = (sw * u).astype(BF16)
    dg = (p * u * slope).astype(BF16)
    du = (p * sw).astype(BF16)
    ab = dot_tn(x, jnp.concatenate([dg, du], axis=1))
    return (ab[:, :w], ab[:, w:], dot_tn(y, hidden)), (g, u, p), (dg, du, hidden)


def chunk_kernel(ids, *refs, plan, chunk):
    n, t, w = plan.n, plan.tokens, plan.width
    first, count = plan.chunks[chunk]
    last = chunk + 1 == len(plan.chunks)
    mats = 3 * count
    refs = list(refs)

    def take(k):
        got = refs[:k]
        del refs[:k]
        return got

    in_refs = take(n)
    before, held = take(2) if last else (None, None)
    shares = take(0 if last else plan.pair)
    d_refs = take(1 if last else 2)
    c_refs = take(2 if last else 1)
    w0, w1, gsum, ssum, acts, fields = take(6)
    total = take(1)[0] if last else c_refs[0]
    base = 3 * first if last else 0

    for slot in range(n):
        at = pl.ds(pl.multiple_of(ids[plan.ids["from"] + slot] * plan.rows, plan.rows), plan.rows)
        for j in range(count):
            for m in range(3):
                for i, dst in enumerate((w1, w0) if last else (w1,)):
                    top = 4 * t + (3 * i + m) * plan.block
                    part = in_refs[slot][top : top + plan.rows, j * w : (j + 1) * w]
                    dst[3 * j + m, at, :] = part.astype(F32)
    for k, part in enumerate(shares):
        at = jnp.bitwise_xor(ids[plan.ids["mine"]], k) * plan.share
        w0[pl.ds(at, plan.share)] = part[...].astype(F32)

    for j in range(count):
        x, y = tokens_of(in_refs, j, 0, plan)
        sums, act, field = forward(x, y, *[w0[3 * j + m].astype(BF16) for m in range(3)])
        for m in range(3):
            gsum[3 * j + m] = sums[m]
            acts[j, m] = act[m]
            fields[j, m] = field[m]
        x, y = tokens_of(in_refs, j, 1, plan)
        sums, _, _ = forward(x, y, *[w1[3 * j + m].astype(BF16) for m in range(3)])
        for m in range(3):
            ssum[3 * j + m] = sums[m]

    grads = [gsum[m] for m in range(mats)]
    updates = [(RATE * ssum[m]).astype(BF16) for m in range(mats)]
    for m, val in enumerate(newton_pullback(grads, updates)):
        gsum[m] = val

    for j in range(count):
        x, y = tokens_of(in_refs, j, 0, plan)
        fab = jnp.concatenate([gsum[3 * j], gsum[3 * j + 1]], axis=1).astype(BF16)
        fc = gsum[3 * j + 2].astype(BF16)
        wab = jnp.concatenate([w0[3 * j], w0[3 * j + 1]], axis=1).astype(BF16)
        wc = w0[3 * j + 2].astype(BF16)
        cdgu = dot_nn(x, fab)
        cdg, cdu = cdgu[:, :w], cdgu[:, w:]
        ch = dot_nn(y, fc)
        g, u, p = acts[j, 0], acts[j, 1], acts[j, 2]
        s, sw, slope = swish_terms(g)
        curve = s * (1.0 - s) * (2.0 + g * (1.0 - 2.0 * s))
        cg = ((ch * u + cdu * p) * slope + cdg * (p * u) * curve).astype(BF16)
        cu = (ch * sw + cdg * p * slope).astype(BF16)
        cp = (cdu * sw + cdg * u * slope).astype(BF16)
        dg, du, hidden = fields[j, 0], fields[j, 1], fields[j, 2]
        dx = dot_nt(jnp.concatenate([dg, du, cg, cu], axis=1), jnp.concatenate([fab, wab], axis=1))
        dy = dot_nt(jnp.concatenate([hidden, cp], axis=1), jnp.concatenate([fc, wc], axis=1))
        if last:
            d_ref, at = d_refs[0], first - plan.early + j
        elif j < plan.early:
            d_ref, at = d_refs[0], j
        else:
            d_ref, at = d_refs[1], j - plan.early
        cols = slice(at * w, (at + 1) * w)
        for slot in range(n):
            to = ids[plan.ids["from"] + slot]
            d_ref[to, 0:t, cols] = dx[slot * t : (slot + 1) * t].astype(BF16)
            d_ref[to, t : 2 * t, cols] = dy[slot * t : (slot + 1) * t].astype(BF16)
        ab = dot_tn(x, jnp.concatenate([cg, cu], axis=1))
        grown = (ab[:, :w], ab[:, w:], dot_tn(y, cp))
        for m in range(3):
            total[base + 3 * j + m] = (ssum[3 * j + m] + grown[m]).astype(BF16)

    if last:
        total[0 : before.shape[0]] = before[...]
        if first > plan.early:
            d_refs[0][:, :, 0 : held.shape[2]] = held[...]
        for m in range(plan.mats, plan.n_dp * plan.own):
            total[m] = jnp.zeros((w, w), BF16)
        mine = ids[plan.ids["mine"]]
        for r in range(plan.rest):
            to = slice(r * plan.own, (r + 1) * plan.own)
            for ref, which in zip(c_refs, (mine, plan.pair - 1 - mine)):
                ref[to] = total[pl.ds((plan.pair * r + which) * plan.own, plan.own)]


def pair_kernel(ids, keep_ref, got_ref, *refs, plan):
    outs, whole = refs[:-1], refs[-1]
    whole[...] = keep_ref[...].astype(F32) + got_ref[...].astype(F32)
    for k in range(plan.rest):
        outs[k][...] = whole[pl.ds(ids[plan.ids["rest"] + k] * plan.own, plan.own)].astype(BF16)


def sum_kernel(ids, *refs, plan):
    parts, outs, whole = refs[: plan.rest], refs[plan.rest : -1], refs[-1]
    added = parts[0][...].astype(F32)
    for part in parts[1:]:
        added = added + part[...].astype(F32)
    whole[...] = added / plan.n_dp
    for slot in range(plan.n):
        at = pl.ds(pl.multiple_of(ids[plan.ids["to"] + slot] * plan.rows, plan.rows), plan.rows)
        outs[slot][...] = whole[:, at, :].astype(BF16)


def order_kernel(ids, *refs, plan, name):
    parts, out = refs[:-1], refs[-1]
    for k, part in enumerate(parts):
        out[ids[plan.ids[name] + k]] = part[...]


def state_kernel(ids, *refs, plan):
    out = refs[-1]
    for k in range(plan.pair):
        for r in range(plan.rest):
            for i in range(plan.own):
                mat = (plan.pair * r + jnp.bitwise_xor(ids[plan.ids["mine"]], k)) * plan.own + i

                @pl.when(mat < plan.mats)
                def _(mat=mat, ref=refs[k], r=r, i=i):
                    for c in range(plan.n):
                        head = plan.first_head(c) + lax.div(mat, 3)
                        out[lax.rem(mat, 3), head] = ref[r, c, i].astype(F32)


def unpack_kernel(*refs, plan):
    t, w = plan.tokens, plan.width
    ins, (dk, dv, sems) = refs[:-3], refs[-3:]
    copies = []
    parts = [(0, plan.early), (plan.early, plan.per - plan.early)]
    for c, (first, count) in enumerate(parts):
        for owner in range(plan.n):
            cols = pl.ds((plan.first_head(owner) + first) * w, count * w)
            for part, dst in enumerate((dk, dv)):
                copy = pltpu.make_async_copy(
                    ins[c].at[owner, pl.ds(part * t, t), :],
                    dst.at[0, :, cols],
                    sems.at[(c * plan.n + owner) * 2 + part],
                )
                copy.start()
                copies.append(copy)
            if plan.n * plan.per != plan.heads:
                for copy in copies:
                    copy.wait()
                copies = []
    for copy in copies:
        copy.wait()


def local(keys_a, values_a, queries_b, grad_out, state_start, state_next):
    n, n_dp = lax.axis_size("ctx"), lax.axis_size("dp")
    _, heads, rows, width = state_start.shape
    t = keys_a.shape[1]
    plan = Plan(n, n_dp, t, heads, rows, width)
    per, own, chunks = plan.per, plan.own, plan.chunks
    bind = lambda kernel, **more: functools.partial(kernel, plan=plan, **more)

    me, dp = lax.axis_index("ctx"), lax.axis_index("dp")
    places = jnp.arange(n, dtype=jnp.int32)
    to_ids = lax.rem(me + places, n)
    place = lax.div(dp, plan.pair)
    ids = jnp.concatenate(
        [
            to_ids,
            lax.rem(me + n - places, n),
            jnp.minimum(to_ids * per, heads - per),
            jnp.bitwise_xor(place, jnp.arange(plan.rest, dtype=jnp.int32)),
            lax.rem(dp, plan.pair).reshape(1),
            place.reshape(1),
        ]
    )

    def swap(value, k):
        if k == 0:
            return value
        return lax.ppermute(value, "dp", [(i, i ^ k) for i in range(n_dp)])

    def shift(value, s):
        if s == 0:
            return value
        return lax.ppermute(value, "ctx", [(i, (i + s) % n) for i in range(n)])

    def turn(value):
        return lax.all_to_all(value, "ctx", split_axis=0, concat_axis=0, tiled=True)

    def shape(*dims, dtype=BF16):
        return jax.ShapeDtypeStruct(dims, dtype)

    def pack(c, slots, keys):
        args = (keys, values_a, queries_b, grad_out, state_start, state_next)
        outs = call(
            bind(pack_kernel, slots=slots, chunk=c),
            [shape(plan.packed_rows(c), chunks[c][1] * width)] * len(slots),
            (ids, *[pltpu.with_memory_space_constraint(arg, pltpu.HBM) for arg in args]),
            [SMEM] + [HBM] * 6,
            [VMEM] * len(slots),
            f"pack{c}_{slots[0]}",
            [
                pltpu.VMEM((len(slots), 2, 3, chunks[c][1], rows, width), F32),
                pltpu.SemaphoreType.DMA((len(slots), 6)),
            ],
        )
        return list(outs)

    sent = pack(0, range(1, n), keys_a)
    keys, sent = lax.optimization_barrier((keys_a, sent))
    arrived = [[shift(v, s + 1) for s, v in enumerate(sent)]]
    sent = pack(1, range(1, n), keys)
    sent, arrived[0][0] = lax.optimization_barrier((sent, arrived[0][0]))
    arrived.append([shift(v, s + 1) for s, v in enumerate(sent)])
    arrived = [pack(c, range(1), keys) + arrived[c] for c in range(2)]
    start_own = call(
        bind(start_kernel),
        shape(plan.share, width, width),
        (ids, *arrived[0]),
        [SMEM] + [VMEM] * n,
        VMEM,
        "start_share",
        [pltpu.VMEM((plan.share, width, width), F32)],
    )
    shares = [swap(start_own, k) for k in range(plan.pair)]

    before = shares
    for c, (_, count) in enumerate(chunks):
        last = c + 1 == len(chunks)
        if last:
            outs = [shape(n, 2 * t, (per - plan.early) * width)] + [shape(plan.rest * own, width, width)] * 2
        else:
            held = max(1, count - plan.early)
            outs = [
                shape(n, 2 * t, plan.early * width),
                shape(n, 2 * t, held * width),
                shape(3 * count, width, width),
            ]
        weights = 3 * count if last else plan.pair * plan.share
        scratch = [pltpu.VMEM((weights, width, width), F32)] + [pltpu.VMEM((3 * count, width, width), F32)] * 3 + [
            pltpu.VMEM((count, 3, n * t, width), F32),
            pltpu.VMEM((count, 3, n * t, width), BF16),
        ]
        if last:
            scratch.append(pltpu.VMEM((n_dp * own, width, width), BF16))
        got = call(
            bind(chunk_kernel, chunk=c),
            outs,
            (ids, *arrived[c], *before),
            [SMEM] + [VMEM] * (n + len(before)),
            [VMEM] * len(outs),
            f"chunk{c}",
            scratch,
            flops=count * 640 * 10**6,
            size=count * 10**6,
            vmem=VMEM_LARGE,
        )
        if not last:
            early = got[0]
            before = [got[2], got[1]]
    late, c_keep, c_send = got
    early, c_send = lax.optimization_barrier((early, c_send))
    early = turn(early)

    halves = call(
        bind(pair_kernel),
        [shape(own, width, width)] * plan.rest,
        (ids, c_keep, swap(c_send, plan.pair - 1)),
        [SMEM] + [VMEM] * 2,
        [VMEM] * plan.rest,
        "state_pair",
        [pltpu.VMEM((plan.rest * own, width, width), F32)],
    )
    halves = [swap(halves[k], plan.pair * k) for k in range(plan.rest)]
    by_rows = call(
        bind(sum_kernel),
        [shape(own, rows, width)] * n,
        (ids, *halves),
        [SMEM] + [VMEM] * plan.rest,
        [VMEM] * n,
        "state_sum",
        [pltpu.VMEM((own, width, width), F32)],
    )
    by_rows = [shift(by_rows[s], s) for s in range(n)]
    by_rows[0], early = lax.optimization_barrier((by_rows[0], early))
    mine = call(
        bind(order_kernel, name="from"),
        shape(n, own, rows, width),
        (ids, *by_rows),
        [SMEM] + [VMEM] * n,
        VMEM,
        "state_rows",
    )
    mine, late = lax.optimization_barrier((mine, late))
    late = turn(late)
    rest = [swap(mine, plan.pair * k) for k in range(plan.rest)]
    half = call(
        bind(order_kernel, name="rest"),
        shape(plan.rest, n, own, rows, width),
        (ids, *rest),
        [SMEM] + [VMEM] * plan.rest,
        VMEM,
        "state_rest",
    )
    both = [swap(half, k) for k in range(plan.pair)]
    grad_state = call(
        bind(state_kernel),
        shape(*state_start.shape, dtype=F32),
        (ids, *both),
        [SMEM] + [VMEM] * plan.pair,
        VMEM,
        "state_out",
    )
    grad_keys, grad_values = call(
        bind(unpack_kernel),
        [shape(*keys_a.shape), shape(*values_a.shape)],
        (early, late),
        [VMEM] * 2,
        [ANY] * 2,
        "unpack",
        [pltpu.SemaphoreType.DMA((4 * n,))],
    )
    return grad_keys, grad_values, grad_state


def solution(mesh):
    placed = (
        P("dp", "ctx", None),
        P("dp", "ctx", None),
        P("dp", "ctx", None),
        P("dp", "ctx", None),
        P(None, None, "ctx", None),
        P("dp", None, None, "ctx", None),
    )
    return jax.shard_map(
        local,
        mesh=mesh,
        in_specs=placed,
        out_specs=(P("dp", "ctx", None), P("dp", "ctx", None), P(None, None, "ctx", None)),
        check_vma=False,
    )
```

```python
import functools

import jax
import jax.numpy as jnp
from jax import lax
from jax.experimental import pallas as pl
from jax.experimental.pallas import tpu as pltpu
from jax.sharding import PartitionSpec as P

RATE = 4.0
CA = 3.4445
CB = -4.775
CC = 2.0315
STEPS = 2
F32 = jnp.float32
BF16 = jnp.bfloat16
VMEM_SMALL = 10 * 1024 * 1024
VMEM_LARGE = 28 * 1024 * 1024
SMEM = pl.BlockSpec(memory_space=pltpu.SMEM)
VMEM = pl.BlockSpec(memory_space=pltpu.VMEM)
ANY = pl.BlockSpec(memory_space=pl.ANY)
HBM = pl.BlockSpec(memory_space=pltpu.HBM)


def dot_nn(a, b):
    return lax.dot_general(a, b, (((1,), (0,)), ((), ())), preferred_element_type=F32)


def dot_nt(a, b):
    return lax.dot_general(a, b, (((1,), (1,)), ((), ())), preferred_element_type=F32)


def dot_tn(a, b):
    return lax.dot_general(a, b, (((0,), (0,)), ((), ())), preferred_element_type=F32)


def call(
    kernel, out_shape, args, in_specs, out_specs, name, scratch=(), flops=10**6, size=10**6, vmem=VMEM_SMALL
):
    return pl.pallas_call(
        kernel,
        out_shape=out_shape,
        in_specs=in_specs,
        out_specs=out_specs,
        scratch_shapes=list(scratch),
        compiler_params=pltpu.CompilerParams(vmem_limit_bytes=vmem),
        cost_estimate=pl.CostEstimate(flops=flops, bytes_accessed=size, transcendentals=0),
        name=name,
    )(*args)


def swish_terms(g):
    s = 1.0 / (1.0 + jnp.exp(-g))
    sw = g * s
    slope = s * (1.0 + g * (1.0 - s))
    return s, sw, slope


def newton_pullback(grads, updates):
    each = range(len(grads))
    inv = [lax.rsqrt(jnp.sum(g * g, keepdims=True) + 1e-06) for g in grads]
    xs = [[(grads[m] * inv[m]).astype(BF16) for m in each]]
    grams = []
    polys = []
    for step in range(STEPS):
        x = xs[-1]
        gram = [dot_nt(x[m], x[m]).astype(BF16) for m in each]
        poly = [(CB * gram[m].astype(F32) + CC * dot_nn(gram[m], gram[m])).astype(BF16) for m in each]
        grams.append(gram)
        polys.append(poly)
        if step + 1 < STEPS:
            xs.append([(CA * x[m].astype(F32) + dot_nn(poly[m], x[m])).astype(BF16) for m in each])
    d = updates
    for step in reversed(range(STEPS)):
        x, gram, poly = xs[step], grams[step], polys[step]
        dp = [dot_nt(d[m], x[m]) for m in each]
        sym = [dp[m] + dp[m].T for m in each]
        turned = [dot_nn(sym[m].astype(BF16), gram[m]) for m in each]
        da = [(CB * sym[m] + CC * (turned[m] + turned[m].T)).astype(BF16) for m in each]
        d = [
            (CA * d[m].astype(F32) + dot_nn(poly[m], d[m]) + dot_nn(da[m], x[m])).astype(BF16)
            for m in each
        ]
    out = []
    for m in each:
        df = d[m].astype(F32)
        along = jnp.sum(df * grads[m], keepdims=True)
        out.append(df * inv[m] - grads[m] * (along * (inv[m] * inv[m] * inv[m])))
    return out


class Plan:
    def __init__(self, n, n_dp, tokens, heads, rows, width):
        self.n, self.n_dp = n, n_dp
        self.tokens, self.heads, self.rows, self.width = tokens, heads, rows, width
        self.per = -(-heads // n)
        self.mats = 3 * self.per
        self.early = (self.per + 1) // 2
        self.pair = min(2, n_dp)
        self.rest = n_dp // self.pair
        self.own = -(-self.mats // n_dp)
        self.block = -(-rows // 16) * 16
        self.share = -(-self.mats // self.pair)
        self.packed_rows = 4 * tokens + (3 - (-self.share // self.per)) * self.block
        self.ids = {}
        at = 0
        for name, size in (("to", n), ("from", n), ("head", n), ("rest", self.rest), ("mine", 1), ("place", 1)):
            self.ids[name] = at
            at += size

    def first_head(self, c):
        return min(c * self.per, self.heads - self.per)


def pack_kernel(ids, k_ref, v_ref, q_ref, o_ref, s_ref, t_ref, *refs, plan, slots):
    t, w, per = plan.tokens, plan.width, plan.per
    outs, (state, sems) = refs[:-2], refs[-2:]
    loads = []
    copies = []
    for k, slot in enumerate(slots):
        head = ids[plan.ids["head"] + slot]
        for i, src in enumerate((s_ref, t_ref.at[0])):
            loads.append(
                pltpu.make_async_copy(src.at[:, pl.ds(head, per)], state.at[k, i], sems.at[k, 4 + i])
            )
            loads[-1].start()
        cols = pl.ds(pl.multiple_of(head * w, w), per * w)
        for i, src in enumerate((k_ref, v_ref, q_ref, o_ref)):
            copies.append(
                pltpu.make_async_copy(src.at[0, :, cols], outs[k].at[pl.ds(i * t, t), :], sems.at[k, i])
            )
            copies[-1].start()
    for k in range(len(slots)):
        loads[2 * k].wait()
        loads[2 * k + 1].wait()
        for j in range(per):
            for m in range(3):
                top = 4 * t + m * plan.block
                outs[k][top : top + plan.rows, j * w : (j + 1) * w] = state[k, 1, m, j].astype(BF16)
        for q in range(plan.share):
            mat = jnp.minimum(ids[plan.ids["mine"]] * plan.share + q, plan.mats - 1)
            top = 4 * t + (3 + q // per) * plan.block
            left = (q % per) * w
            part = state[k, 0, lax.rem(mat, 3), lax.div(mat, 3)]
            outs[k][top : top + plan.rows, left : left + w] = part.astype(BF16)
    for copy in copies:
        copy.wait()


def start_kernel(ids, *refs, plan):
    in_refs, (out, whole) = refs[: plan.n], refs[plan.n :]
    per, w = plan.per, plan.width
    for slot in range(plan.n):
        at = pl.ds(pl.multiple_of(ids[plan.ids["from"] + slot] * plan.rows, plan.rows), plan.rows)
        for q in range(plan.share):
            top = 4 * plan.tokens + (3 + q // per) * plan.block
            left = (q % per) * w
            whole[q, at, :] = in_refs[slot][top : top + plan.rows, left : left + w].astype(F32)
    out[...] = whole[...].astype(BF16)


def tokens_of(refs, j, group, plan):
    t, w = plan.tokens, plan.width
    cols = slice(j * w, (j + 1) * w)
    top = 2 * group * t
    x = jnp.concatenate([r[top : top + t, cols] for r in refs], axis=0)
    y = jnp.concatenate([r[top + t : top + 2 * t, cols] for r in refs], axis=0)
    return x, y


def forward(x, y, wa, wb, wc):
    w = wa.shape[1]
    gu = dot_nn(x, jnp.concatenate([wa, wb], axis=1))
    g, u = gu[:, :w], gu[:, w:]
    p = dot_nn(y, wc)
    _, sw, slope = swish_terms(g)
    hidden = (sw * u).astype(BF16)
    dg = (p * u * slope).astype(BF16)
    du = (p * sw).astype(BF16)
    ab = dot_tn(x, jnp.concatenate([dg, du], axis=1))
    return (ab[:, :w], ab[:, w:], dot_tn(y, hidden)), (g, u, p), (dg, du, hidden)


def main_kernel(ids, *refs, plan):
    n, t, w, count, mats = plan.n, plan.tokens, plan.width, plan.per, plan.mats
    in_refs, refs = refs[:n], refs[n:]
    shares, refs = refs[: plan.pair], refs[plan.pair :]
    early_ref, late_ref, keep_ref, send_ref, w0, w1, gsum, ssum, acts, fields, total = refs

    for slot in range(n):
        at = pl.ds(pl.multiple_of(ids[plan.ids["from"] + slot] * plan.rows, plan.rows), plan.rows)
        for j in range(count):
            for m in range(3):
                top = 4 * t + m * plan.block
                part = in_refs[slot][top : top + plan.rows, j * w : (j + 1) * w]
                w1[3 * j + m, at, :] = part.astype(F32)
    for k, part in enumerate(shares):
        at = jnp.bitwise_xor(ids[plan.ids["mine"]], k) * plan.share
        w0[pl.ds(at, plan.share)] = part[...]

    for j in range(count):
        x, y = tokens_of(in_refs, j, 0, plan)
        sums, act, field = forward(x, y, *[w0[3 * j + m] for m in range(3)])
        for m in range(3):
            gsum[3 * j + m] = sums[m]
            acts[j, m] = act[m]
            fields[j, m] = field[m]
        x, y = tokens_of(in_refs, j, 1, plan)
        sums, _, _ = forward(x, y, *[w1[3 * j + m].astype(BF16) for m in range(3)])
        for m in range(3):
            ssum[3 * j + m] = sums[m]

    grads = [gsum[m] for m in range(mats)]
    updates = [(RATE * ssum[m]).astype(BF16) for m in range(mats)]
    for m, val in enumerate(newton_pullback(grads, updates)):
        gsum[m] = val

    for j in range(count):
        x, y = tokens_of(in_refs, j, 0, plan)
        fab = jnp.concatenate([gsum[3 * j], gsum[3 * j + 1]], axis=1).astype(BF16)
        fc = gsum[3 * j + 2].astype(BF16)
        wab = jnp.concatenate([w0[3 * j], w0[3 * j + 1]], axis=1)
        wc = w0[3 * j + 2]
        cdgu = dot_nn(x, fab)
        cdg, cdu = cdgu[:, :w], cdgu[:, w:]
        ch = dot_nn(y, fc)
        g, u, p = acts[j, 0], acts[j, 1], acts[j, 2]
        s, sw, slope = swish_terms(g)
        curve = s * (1.0 - s) * (2.0 + g * (1.0 - 2.0 * s))
        cg = ((ch * u + cdu * p) * slope + cdg * (p * u) * curve).astype(BF16)
        cu = (ch * sw + cdg * p * slope).astype(BF16)
        cp = (cdu * sw + cdg * u * slope).astype(BF16)
        dg, du, hidden = fields[j, 0], fields[j, 1], fields[j, 2]
        dx = dot_nt(jnp.concatenate([dg, du, cg, cu], axis=1), jnp.concatenate([fab, wab], axis=1))
        dy = dot_nt(jnp.concatenate([hidden, cp], axis=1), jnp.concatenate([fc, wc], axis=1))
        d_ref, at = (early_ref, j) if j < plan.early else (late_ref, j - plan.early)
        cols = slice(at * w, (at + 1) * w)
        for slot in range(n):
            to = ids[plan.ids["from"] + slot]
            d_ref[to, 0:t, cols] = dx[slot * t : (slot + 1) * t].astype(BF16)
            d_ref[to, t : 2 * t, cols] = dy[slot * t : (slot + 1) * t].astype(BF16)
        ab = dot_tn(x, jnp.concatenate([cg, cu], axis=1))
        grown = (ab[:, :w], ab[:, w:], dot_tn(y, cp))
        for m in range(3):
            total[3 * j + m] = (ssum[3 * j + m] + grown[m]).astype(BF16)

    for m in range(plan.mats, plan.n_dp * plan.own):
        total[m] = jnp.zeros((w, w), BF16)
    mine = ids[plan.ids["mine"]]
    for r in range(plan.rest):
        to = slice(r * plan.own, (r + 1) * plan.own)
        for ref, which in ((keep_ref, mine), (send_ref, plan.pair - 1 - mine)):
            ref[to] = total[pl.ds((plan.pair * r + which) * plan.own, plan.own)]


def pair_kernel(ids, keep_ref, got_ref, *refs, plan):
    outs, whole = refs[:-1], refs[-1]
    whole[...] = keep_ref[...].astype(F32) + got_ref[...].astype(F32)
    for k in range(plan.rest):
        outs[k][...] = whole[pl.ds(ids[plan.ids["rest"] + k] * plan.own, plan.own)].astype(BF16)


def sum_kernel(ids, *refs, plan):
    parts, outs, whole = refs[: plan.rest], refs[plan.rest : -1], refs[-1]
    added = parts[0][...].astype(F32)
    for part in parts[1:]:
        added = added + part[...].astype(F32)
    whole[...] = added / plan.n_dp
    for slot in range(plan.n):
        at = pl.ds(pl.multiple_of(ids[plan.ids["to"] + slot] * plan.rows, plan.rows), plan.rows)
        outs[slot][...] = whole[:, at, :].astype(BF16)


def order_kernel(ids, *refs, plan, name):
    parts, out = refs[:-1], refs[-1]
    for k, part in enumerate(parts):
        out[ids[plan.ids[name] + k]] = part[...]


def state_kernel(ids, *refs, plan):
    out = refs[-1]
    for k in range(plan.pair):
        for r in range(plan.rest):
            for i in range(plan.own):
                mat = (plan.pair * r + jnp.bitwise_xor(ids[plan.ids["mine"]], k)) * plan.own + i

                @pl.when(mat < plan.mats)
                def _(mat=mat, ref=refs[k], r=r, i=i):
                    for c in range(plan.n):
                        head = plan.first_head(c) + lax.div(mat, 3)
                        out[lax.rem(mat, 3), head] = ref[r, c, i].astype(F32)


def unpack_kernel(*refs, plan):
    t, w = plan.tokens, plan.width
    ins, (dk, dv, sems) = refs[:-3], refs[-3:]
    copies = []
    parts = [(0, plan.early), (plan.early, plan.per - plan.early)]
    for c, (first, count) in enumerate(parts):
        for owner in range(plan.n):
            cols = pl.ds((plan.first_head(owner) + first) * w, count * w)
            for part, dst in enumerate((dk, dv)):
                copy = pltpu.make_async_copy(
                    ins[c].at[owner, pl.ds(part * t, t), :],
                    dst.at[0, :, cols],
                    sems.at[(c * plan.n + owner) * 2 + part],
                )
                copy.start()
                copies.append(copy)
            if plan.n * plan.per != plan.heads:
                for copy in copies:
                    copy.wait()
                copies = []
    for copy in copies:
        copy.wait()


def local(keys_a, values_a, queries_b, grad_out, state_start, state_next):
    n, n_dp = lax.axis_size("ctx"), lax.axis_size("dp")
    _, heads, rows, width = state_start.shape
    t = keys_a.shape[1]
    plan = Plan(n, n_dp, t, heads, rows, width)
    per, mats, own = plan.per, plan.mats, plan.own
    bind = lambda kernel, **more: functools.partial(kernel, plan=plan, **more)

    me, dp = lax.axis_index("ctx"), lax.axis_index("dp")
    places = jnp.arange(n, dtype=jnp.int32)
    to_ids = lax.rem(me + places, n)
    place = lax.div(dp, plan.pair)
    ids = jnp.concatenate(
        [
            to_ids,
            lax.rem(me + n - places, n),
            jnp.minimum(to_ids * per, heads - per),
            jnp.bitwise_xor(place, jnp.arange(plan.rest, dtype=jnp.int32)),
            lax.rem(dp, plan.pair).reshape(1),
            place.reshape(1),
        ]
    )

    def swap(value, k):
        if k == 0:
            return value
        return lax.ppermute(value, "dp", [(i, i ^ k) for i in range(n_dp)])

    def shift(value, s):
        if s == 0:
            return value
        return lax.ppermute(value, "ctx", [(i, (i + s) % n) for i in range(n)])

    def turn(value):
        return lax.all_to_all(value, "ctx", split_axis=0, concat_axis=0, tiled=True)

    def shape(*dims, dtype=BF16):
        return jax.ShapeDtypeStruct(dims, dtype)

    def pack(slots, keys):
        args = (keys, values_a, queries_b, grad_out, state_start, state_next)
        outs = call(
            bind(pack_kernel, slots=slots),
            [shape(plan.packed_rows, per * width)] * len(slots),
            (ids, *[pltpu.with_memory_space_constraint(arg, pltpu.HBM) for arg in args]),
            [SMEM] + [HBM] * 6,
            [VMEM] * len(slots),
            f"pack{slots[0]}",
            [
                pltpu.VMEM((len(slots), 2, 3, per, rows, width), F32),
                pltpu.SemaphoreType.DMA((len(slots), 6)),
            ],
        )
        return list(outs)

    sent = pack(range(1, n), keys_a)
    keys, sent = lax.optimization_barrier((keys_a, sent))
    arrived = pack(range(1), keys) + [shift(v, s + 1) for s, v in enumerate(sent)]
    start_own = call(
        bind(start_kernel),
        shape(plan.share, width, width),
        (ids, *arrived),
        [SMEM] + [VMEM] * n,
        VMEM,
        "start_share",
        [pltpu.VMEM((plan.share, width, width), F32)],
    )
    shares = [swap(start_own, k) for k in range(plan.pair)]
    early, late, c_keep, c_send = call(
        bind(main_kernel),
        [
            shape(n, 2 * t, plan.early * width),
            shape(n, 2 * t, (per - plan.early) * width),
            shape(plan.rest * own, width, width),
            shape(plan.rest * own, width, width),
        ],
        (ids, *arrived, *shares),
        [SMEM] + [VMEM] * (n + plan.pair),
        [VMEM] * 4,
        "main",
        [pltpu.VMEM((plan.pair * plan.share, width, width), BF16)]
        + [pltpu.VMEM((mats, width, width), F32)] * 3
        + [
            pltpu.VMEM((per, 3, n * t, width), F32),
            pltpu.VMEM((per, 3, n * t, width), BF16),
            pltpu.VMEM((n_dp * own, width, width), BF16),
        ],
        flops=per * 640 * 10**6,
        size=per * 10**6,
        vmem=VMEM_LARGE,
    )
    early, c_send = lax.optimization_barrier((early, c_send))
    early = turn(early)

    halves = call(
        bind(pair_kernel),
        [shape(own, width, width)] * plan.rest,
        (ids, c_keep, swap(c_send, plan.pair - 1)),
        [SMEM] + [VMEM] * 2,
        [VMEM] * plan.rest,
        "state_pair",
        [pltpu.VMEM((plan.rest * own, width, width), F32)],
    )
    halves = [swap(halves[k], plan.pair * k) for k in range(plan.rest)]
    by_rows = call(
        bind(sum_kernel),
        [shape(own, rows, width)] * n,
        (ids, *halves),
        [SMEM] + [VMEM] * plan.rest,
        [VMEM] * n,
        "state_sum",
        [pltpu.VMEM((own, width, width), F32)],
    )
    by_rows = [shift(by_rows[s], s) for s in range(n)]
    by_rows[0], early = lax.optimization_barrier((by_rows[0], early))
    mine = call(
        bind(order_kernel, name="from"),
        shape(n, own, rows, width),
        (ids, *by_rows),
        [SMEM] + [VMEM] * n,
        VMEM,
        "state_rows",
    )
    mine, late = lax.optimization_barrier((mine, late))
    late = turn(late)
    rest = [swap(mine, plan.pair * k) for k in range(plan.rest)]
    half = call(
        bind(order_kernel, name="rest"),
        shape(plan.rest, n, own, rows, width),
        (ids, *rest),
        [SMEM] + [VMEM] * plan.rest,
        VMEM,
        "state_rest",
    )
    both = [swap(half, k) for k in range(plan.pair)]
    grad_state = call(
        bind(state_kernel),
        shape(*state_start.shape, dtype=F32),
        (ids, *both),
        [SMEM] + [VMEM] * plan.pair,
        VMEM,
        "state_out",
    )
    grad_keys, grad_values = call(
        bind(unpack_kernel),
        [shape(*keys_a.shape), shape(*values_a.shape)],
        (early, late),
        [VMEM] * 2,
        [ANY] * 2,
        "unpack",
        [pltpu.SemaphoreType.DMA((4 * n,))],
    )
    return grad_keys, grad_values, grad_state


def solution(mesh):
    placed = (
        P("dp", "ctx", None),
        P("dp", "ctx", None),
        P("dp", "ctx", None),
        P("dp", "ctx", None),
        P(None, None, "ctx", None),
        P("dp", None, None, "ctx", None),
    )
    return jax.shard_map(
        local,
        mesh=mesh,
        in_specs=placed,
        out_specs=(P("dp", "ctx", None), P("dp", "ctx", None), P(None, None, "ctx", None)),
        check_vma=False,
    )
```

```python
import functools

import jax
import jax.numpy as jnp
from jax import lax
from jax.experimental import pallas as pl
from jax.experimental.pallas import tpu as pltpu
from jax.sharding import PartitionSpec as P

RATE = 4.0
CA = 3.4445
CB = -4.775
CC = 2.0315
STEPS = 2
F32 = jnp.float32
BF16 = jnp.bfloat16
VMEM_SMALL = 8 * 1024 * 1024
VMEM_LARGE = 28 * 1024 * 1024
SMEM = pl.BlockSpec(memory_space=pltpu.SMEM)
VMEM = pl.BlockSpec(memory_space=pltpu.VMEM)
ANY = pl.BlockSpec(memory_space=pl.ANY)
HBM = pl.BlockSpec(memory_space=pltpu.HBM)


def dot_nn(a, b):
    return lax.dot_general(a, b, (((1,), (0,)), ((), ())), preferred_element_type=F32)


def dot_nt(a, b):
    return lax.dot_general(a, b, (((1,), (1,)), ((), ())), preferred_element_type=F32)


def dot_tn(a, b):
    return lax.dot_general(a, b, (((0,), (0,)), ((), ())), preferred_element_type=F32)


def call(
    kernel, out_shape, args, in_specs, out_specs, name, scratch=(), flops=10**6, size=10**6, vmem=VMEM_SMALL
):
    return pl.pallas_call(
        kernel,
        out_shape=out_shape,
        in_specs=in_specs,
        out_specs=out_specs,
        scratch_shapes=list(scratch),
        compiler_params=pltpu.CompilerParams(vmem_limit_bytes=vmem),
        cost_estimate=pl.CostEstimate(flops=flops, bytes_accessed=size, transcendentals=0),
        name=name,
    )(*args)


def swish_terms(g, s):
    rest = 1.0 - s
    both = s * rest
    bent = g * both
    return g * s, s + bent, 2.0 * both + bent * (rest - s)


def newton_pullback(grads, updates):
    each = range(len(grads))
    inv = [lax.rsqrt(jnp.sum(g * g, keepdims=True) + 1e-06) for g in grads]
    xs = [[(grads[m] * inv[m]).astype(BF16) for m in each]]
    grams = []
    polys = []
    for step in range(STEPS):
        x = xs[-1]
        gram = [dot_nt(x[m], x[m]).astype(BF16) for m in each]
        poly = [(CB * gram[m].astype(F32) + CC * dot_nn(gram[m], gram[m])).astype(BF16) for m in each]
        grams.append(gram)
        polys.append(poly)
        if step + 1 < STEPS:
            xs.append([(CA * x[m].astype(F32) + dot_nn(poly[m], x[m])).astype(BF16) for m in each])
    d = updates
    for step in reversed(range(STEPS)):
        x, gram, poly = xs[step], grams[step], polys[step]
        dp = [dot_nt(d[m], x[m]) for m in each]
        sym = [dp[m] + dp[m].T for m in each]
        turned = [dot_nn(sym[m].astype(BF16), gram[m]) for m in each]
        da = [(CB * sym[m] + CC * (turned[m] + turned[m].T)).astype(BF16) for m in each]
        d = [
            (CA * d[m].astype(F32) + dot_nn(poly[m], d[m]) + dot_nn(da[m], x[m])).astype(BF16)
            for m in each
        ]
    out = []
    for m in each:
        df = d[m].astype(F32)
        along = jnp.sum(df * grads[m], keepdims=True)
        out.append(df * inv[m] - grads[m] * (along * (inv[m] * inv[m] * inv[m])))
    return out


class Plan:
    def __init__(self, n, n_dp, tokens, heads, rows, width):
        self.n, self.n_dp = n, n_dp
        self.tokens, self.heads, self.rows, self.width = tokens, heads, rows, width
        self.per = -(-heads // n)
        self.mats = 3 * self.per
        least = max(1, self.per // 2)
        self.chunks = [(0, least), (least, self.per - least)]
        self.early = (self.per + 1) // 2
        self.pair = min(2, n_dp)
        self.rest = n_dp // self.pair
        self.own = -(-self.mats // n_dp)
        self.block = -(-rows // 16) * 16
        self.share = -(-self.mats // self.pair)
        self.share_blocks = -(-self.share // least)
        self.ids = {}
        at = 0
        for name, size in (("to", n), ("from", n), ("head", n), ("rest", self.rest), ("mine", 1), ("place", 1)):
            self.ids[name] = at
            at += size

    def packed_rows(self, chunk):
        return 4 * self.tokens + (3 + (self.share_blocks if chunk == 0 else 0)) * self.block

    def first_head(self, c):
        return min(c * self.per, self.heads - self.per)


def pack_kernel(ids, k_ref, v_ref, q_ref, o_ref, s_ref, t_ref, *refs, plan, slots, chunk):
    t, w = plan.tokens, plan.width
    first, count = plan.chunks[chunk]
    outs, (state, sems) = refs[:-2], refs[-2:]
    per = plan.per
    loads = []
    copies = []
    for k, slot in enumerate(slots):
        head = ids[plan.ids["head"] + slot]
        wanted = [(t_ref.at[0, :, pl.ds(head + first, count)], state.at[k, :, pl.ds(0, count)])]
        if chunk == 0:
            wanted.append((s_ref.at[:, pl.ds(head, per)], state.at[k, :, pl.ds(count, per)]))
        for i, (src, dst) in enumerate(wanted):
            loads.append(pltpu.make_async_copy(src, dst, sems.at[k, 4 + i]))
            loads[-1].start()
        cols = pl.ds(pl.multiple_of((head + first) * w, w), count * w)
        for i, src in enumerate((k_ref, v_ref, q_ref, o_ref)):
            copies.append(
                pltpu.make_async_copy(src.at[0, :, cols], outs[k].at[pl.ds(i * t, t), :], sems.at[k, i])
            )
            copies[-1].start()
    for load in loads:
        load.wait()
    for k in range(len(slots)):
        for j in range(count):
            for m in range(3):
                top = 4 * t + m * plan.block
                outs[k][top : top + plan.rows, j * w : (j + 1) * w] = state[k, m, j].astype(BF16)
        for q in range(plan.share if chunk == 0 else 0):
            mat = jnp.minimum(ids[plan.ids["mine"]] * plan.share + q, plan.mats - 1)
            top = 4 * t + (3 + q // count) * plan.block
            left = (q % count) * w
            part = state[k, lax.rem(mat, 3), count + lax.div(mat, 3)]
            outs[k][top : top + plan.rows, left : left + w] = part.astype(BF16)
    for copy in copies:
        copy.wait()


def start_kernel(ids, *refs, plan):
    in_refs, (out, whole) = refs[: plan.n], refs[plan.n :]
    count, w = plan.chunks[0][1], plan.width
    for slot in range(plan.n):
        at = pl.ds(pl.multiple_of(ids[plan.ids["from"] + slot] * plan.rows, plan.rows), plan.rows)
        for q in range(plan.share):
            top = 4 * plan.tokens + (3 + q // count) * plan.block
            left = (q % count) * w
            whole[q, at, :] = in_refs[slot][top : top + plan.rows, left : left + w].astype(F32)
    out[...] = whole[...].astype(BF16)


def tokens_of(refs, j, group, plan):
    t, w = plan.tokens, plan.width
    cols = slice(j * w, (j + 1) * w)
    top = 2 * group * t
    x = jnp.concatenate([r[top : top + t, cols] for r in refs], axis=0)
    y = jnp.concatenate([r[top + t : top + 2 * t, cols] for r in refs], axis=0)
    return x, y


def forward(x, y, wa, wb, wc):
    w = wa.shape[1]
    gu = dot_nn(x, jnp.concatenate([wa, wb], axis=1))
    g, u = gu[:, :w], gu[:, w:]
    p = dot_nn(y, wc)
    s = 0.5 + 0.5 * jnp.tanh(0.5 * g)
    sw, slope, _ = swish_terms(g, s)
    hidden = (sw * u).astype(BF16)
    dg = (p * u * slope).astype(BF16)
    du = (p * sw).astype(BF16)
    ab = dot_tn(x, jnp.concatenate([dg, du], axis=1))
    return (ab[:, :w], ab[:, w:], dot_tn(y, hidden)), (g, u, p, s), (dg, du, hidden)


def chunk_kernel(ids, *refs, plan, chunk):
    n, t, w = plan.n, plan.tokens, plan.width
    first, count = plan.chunks[chunk]
    last = chunk + 1 == len(plan.chunks)
    mats = 3 * count
    refs = list(refs)

    def take(k):
        got = refs[:k]
        del refs[:k]
        return got

    in_refs = take(n)
    shares = take(plan.pair)
    before, held = take(2) if last else (None, None)
    d_refs = take(2 if last else 1)
    c_refs = take(2 if last else 1)
    w0, w1, gsum, ssum, acts, fields = take(6)
    total = take(1)[0] if last else c_refs[0]
    base = 3 * first if last else 0

    for slot in range(n):
        at = pl.ds(pl.multiple_of(ids[plan.ids["from"] + slot] * plan.rows, plan.rows), plan.rows)
        for j in range(count):
            for m in range(3):
                top = 4 * t + m * plan.block
                part = in_refs[slot][top : top + plan.rows, j * w : (j + 1) * w]
                w1[3 * j + m, at, :] = part.astype(F32)
    for k, part in enumerate(shares):
        at = jnp.bitwise_xor(ids[plan.ids["mine"]], k) * plan.share
        w0[pl.ds(at, plan.share)] = part[...]

    for j in range(count):
        x, y = tokens_of(in_refs, j, 0, plan)
        sums, act, field = forward(x, y, *[w0[3 * (first + j) + m] for m in range(3)])
        for m in range(3):
            gsum[3 * j + m] = sums[m]
            fields[j, m] = field[m]
        for i, val in enumerate(act):
            acts[j, i] = val
        x, y = tokens_of(in_refs, j, 1, plan)
        sums, _, _ = forward(x, y, *[w1[3 * j + m].astype(BF16) for m in range(3)])
        for m in range(3):
            ssum[3 * j + m] = sums[m]

    grads = [gsum[m] for m in range(mats)]
    updates = [(RATE * ssum[m]).astype(BF16) for m in range(mats)]
    for m, val in enumerate(newton_pullback(grads, updates)):
        gsum[m] = val

    for j in range(count):
        x, y = tokens_of(in_refs, j, 0, plan)
        fab = jnp.concatenate([gsum[3 * j], gsum[3 * j + 1]], axis=1).astype(BF16)
        fc = gsum[3 * j + 2].astype(BF16)
        at = 3 * (first + j)
        wab = jnp.concatenate([w0[at], w0[at + 1]], axis=1)
        wc = w0[at + 2]
        cdgu = dot_nn(x, fab)
        cdg, cdu = cdgu[:, :w], cdgu[:, w:]
        ch = dot_nn(y, fc)
        g, u, p, s = [acts[j, i] for i in range(4)]
        sw, slope, curve = swish_terms(g, s)
        cg = ((ch * u + cdu * p) * slope + cdg * (p * u) * curve).astype(BF16)
        cu = (ch * sw + cdg * p * slope).astype(BF16)
        cp = (cdu * sw + cdg * u * slope).astype(BF16)
        dg, du, hidden = fields[j, 0], fields[j, 1], fields[j, 2]
        dx = dot_nt(jnp.concatenate([dg, du, cg, cu], axis=1), jnp.concatenate([fab, wab], axis=1))
        dy = dot_nt(jnp.concatenate([hidden, cp], axis=1), jnp.concatenate([fc, wc], axis=1))
        d_ref, at = (d_refs[0], first + j) if first + j < plan.early else (d_refs[1], first + j - plan.early)
        cols = slice(at * w, (at + 1) * w)
        for slot in range(n):
            to = ids[plan.ids["from"] + slot]
            d_ref[to, 0:t, cols] = dx[slot * t : (slot + 1) * t].astype(BF16)
            d_ref[to, t : 2 * t, cols] = dy[slot * t : (slot + 1) * t].astype(BF16)
        ab = dot_tn(x, jnp.concatenate([cg, cu], axis=1))
        grown = (ab[:, :w], ab[:, w:], dot_tn(y, cp))
        for m in range(3):
            total[base + 3 * j + m] = (ssum[3 * j + m] + grown[m]).astype(BF16)

    if last:
        total[0 : before.shape[0]] = before[...]
        d_refs[0][:, :, 0 : held.shape[2]] = held[...]
        for m in range(plan.mats, plan.n_dp * plan.own):
            total[m] = jnp.zeros((w, w), BF16)
        mine = ids[plan.ids["mine"]]
        for r in range(plan.rest):
            to = slice(r * plan.own, (r + 1) * plan.own)
            for ref, which in zip(c_refs, (mine, plan.pair - 1 - mine)):
                ref[to] = total[pl.ds((plan.pair * r + which) * plan.own, plan.own)]


def pair_kernel(ids, keep_ref, got_ref, *refs, plan):
    outs, whole = refs[:-1], refs[-1]
    whole[...] = keep_ref[...].astype(F32) + got_ref[...].astype(F32)
    for k in range(plan.rest):
        outs[k][...] = whole[pl.ds(ids[plan.ids["rest"] + k] * plan.own, plan.own)].astype(BF16)


def sum_kernel(ids, *refs, plan):
    parts, outs, whole = refs[: plan.rest], refs[plan.rest : -1], refs[-1]
    added = parts[0][...].astype(F32)
    for part in parts[1:]:
        added = added + part[...].astype(F32)
    whole[...] = added / plan.n_dp
    for slot in range(plan.n):
        at = pl.ds(pl.multiple_of(ids[plan.ids["to"] + slot] * plan.rows, plan.rows), plan.rows)
        outs[slot][...] = whole[:, at, :].astype(BF16)


def order_kernel(ids, *refs, plan, name):
    parts, out = refs[:-1], refs[-1]
    for k, part in enumerate(parts):
        out[ids[plan.ids[name] + k]] = part[...]


def state_kernel(ids, *refs, plan):
    out = refs[-1]
    for k in range(plan.pair):
        for r in range(plan.rest):
            for i in range(plan.own):
                mat = (plan.pair * r + jnp.bitwise_xor(ids[plan.ids["mine"]], k)) * plan.own + i

                @pl.when(mat < plan.mats)
                def _(mat=mat, ref=refs[k], r=r, i=i):
                    for c in range(plan.n):
                        head = plan.first_head(c) + lax.div(mat, 3)
                        out[lax.rem(mat, 3), head] = ref[r, c, i].astype(F32)


def unpack_kernel(*refs, plan):
    t, w = plan.tokens, plan.width
    ins, (dk, dv, sems) = refs[:-3], refs[-3:]
    copies = []
    parts = [(0, plan.early), (plan.early, plan.per - plan.early)]
    for c, (first, count) in enumerate(parts):
        for owner in range(plan.n):
            cols = pl.ds((plan.first_head(owner) + first) * w, count * w)
            for part, dst in enumerate((dk, dv)):
                copy = pltpu.make_async_copy(
                    ins[c].at[owner, pl.ds(part * t, t), :],
                    dst.at[0, :, cols],
                    sems.at[(c * plan.n + owner) * 2 + part],
                )
                copy.start()
                copies.append(copy)
            if plan.n * plan.per != plan.heads:
                for copy in copies:
                    copy.wait()
                copies = []
    for copy in copies:
        copy.wait()


def local(keys_a, values_a, queries_b, grad_out, state_start, state_next):
    n, n_dp = lax.axis_size("ctx"), lax.axis_size("dp")
    _, heads, rows, width = state_start.shape
    t = keys_a.shape[1]
    plan = Plan(n, n_dp, t, heads, rows, width)
    per, own, chunks = plan.per, plan.own, plan.chunks
    bind = lambda kernel, **more: functools.partial(kernel, plan=plan, **more)

    me, dp = lax.axis_index("ctx"), lax.axis_index("dp")
    places = jnp.arange(n, dtype=jnp.int32)
    to_ids = lax.rem(me + places, n)
    place = lax.div(dp, plan.pair)
    ids = jnp.concatenate(
        [
            to_ids,
            lax.rem(me + n - places, n),
            jnp.minimum(to_ids * per, heads - per),
            jnp.bitwise_xor(place, jnp.arange(plan.rest, dtype=jnp.int32)),
            lax.rem(dp, plan.pair).reshape(1),
            place.reshape(1),
        ]
    )

    def swap(value, k):
        if k == 0:
            return value
        return lax.ppermute(value, "dp", [(i, i ^ k) for i in range(n_dp)])

    def shift(value, s):
        if s == 0:
            return value
        return lax.ppermute(value, "ctx", [(i, (i + s) % n) for i in range(n)])

    def turn(value):
        return lax.all_to_all(value, "ctx", split_axis=0, concat_axis=0, tiled=True)

    def shape(*dims, dtype=BF16):
        return jax.ShapeDtypeStruct(dims, dtype)

    def pack(c, slots, keys):
        args = (keys, values_a, queries_b, grad_out, state_start, state_next)
        outs = call(
            bind(pack_kernel, slots=slots, chunk=c),
            [shape(plan.packed_rows(c), chunks[c][1] * width)] * len(slots),
            (ids, *[pltpu.with_memory_space_constraint(arg, pltpu.HBM) for arg in args]),
            [SMEM] + [HBM] * 6,
            [VMEM] * len(slots),
            f"pack{c}_{slots[0]}",
            [
                pltpu.VMEM((len(slots), 3, chunks[c][1] + (0 if c else per), rows, width), F32),
                pltpu.SemaphoreType.DMA((len(slots), 6)),
            ],
        )
        return list(outs)

    sent = pack(0, range(1, n), keys_a)
    keys, sent = lax.optimization_barrier((keys_a, sent))
    arrived = [[shift(v, s + 1) for s, v in enumerate(sent)]]
    sent = pack(1, range(1, n), keys)
    keys, sent = lax.optimization_barrier((keys_a, sent))
    arrived.append([shift(v, s + 1) for s, v in enumerate(sent)])
    arrived = [pack(c, range(1), keys) + arrived[c] for c in range(2)]
    start_own = call(
        bind(start_kernel),
        shape(plan.share, width, width),
        (ids, *arrived[0]),
        [SMEM] + [VMEM] * n,
        VMEM,
        "start_share",
        [pltpu.VMEM((plan.share, width, width), F32)],
    )
    shares = [swap(start_own, k) for k in range(plan.pair)]

    before = []
    for c, (_, count) in enumerate(chunks):
        last = c + 1 == len(chunks)
        if last:
            outs = [shape(n, 2 * t, size * width) for size in (plan.early, per - plan.early)]
            outs += [shape(plan.rest * own, width, width)] * 2
        else:
            outs = [shape(n, 2 * t, count * width), shape(3 * count, width, width)]
        scratch = [pltpu.VMEM((plan.pair * plan.share, width, width), BF16)]
        scratch += [pltpu.VMEM((3 * count, width, width), F32)] * 3 + [
            pltpu.VMEM((count, 4, n * t, width), F32),
            pltpu.VMEM((count, 3, n * t, width), BF16),
        ]
        if last:
            scratch.append(pltpu.VMEM((n_dp * own, width, width), BF16))
        got = call(
            bind(chunk_kernel, chunk=c),
            outs,
            (ids, *arrived[c], *shares, *before),
            [SMEM] + [VMEM] * (n + plan.pair + len(before)),
            [VMEM] * len(outs),
            f"chunk{c}",
            scratch,
            flops=count * 640 * 10**6,
            size=count * 10**6,
            vmem=VMEM_LARGE,
        )
        before = [got[1], got[0]]
    early, late, c_keep, c_send = got
    early, c_send = lax.optimization_barrier((early, c_send))
    early = turn(early)

    halves = call(
        bind(pair_kernel),
        [shape(own, width, width)] * plan.rest,
        (ids, c_keep, swap(c_send, plan.pair - 1)),
        [SMEM] + [VMEM] * 2,
        [VMEM] * plan.rest,
        "state_pair",
        [pltpu.VMEM((plan.rest * own, width, width), F32)],
    )
    halves = [swap(halves[k], plan.pair * k) for k in range(plan.rest)]
    by_rows = call(
        bind(sum_kernel),
        [shape(own, rows, width)] * n,
        (ids, *halves),
        [SMEM] + [VMEM] * plan.rest,
        [VMEM] * n,
        "state_sum",
        [pltpu.VMEM((own, width, width), F32)],
    )
    by_rows = [shift(by_rows[s], s) for s in range(n)]
    by_rows[0], early = lax.optimization_barrier((by_rows[0], early))
    mine = call(
        bind(order_kernel, name="from"),
        shape(n, own, rows, width),
        (ids, *by_rows),
        [SMEM] + [VMEM] * n,
        VMEM,
        "state_rows",
    )
    mine, late = lax.optimization_barrier((mine, late))
    late = turn(late)
    rest = [swap(mine, plan.pair * k) for k in range(plan.rest)]
    half = call(
        bind(order_kernel, name="rest"),
        shape(plan.rest, n, own, rows, width),
        (ids, *rest),
        [SMEM] + [VMEM] * plan.rest,
        VMEM,
        "state_rest",
    )
    both = [swap(half, k) for k in range(plan.pair)]
    grad_state = call(
        bind(state_kernel),
        shape(*state_start.shape, dtype=F32),
        (ids, *both),
        [SMEM] + [VMEM] * plan.pair,
        VMEM,
        "state_out",
    )
    grad_keys, grad_values = call(
        bind(unpack_kernel),
        [shape(*keys_a.shape), shape(*values_a.shape)],
        (early, late),
        [VMEM] * 2,
        [ANY] * 2,
        "unpack",
        [pltpu.SemaphoreType.DMA((4 * n,))],
    )
    return grad_keys, grad_values, grad_state


def solution(mesh):
    placed = (
        P("dp", "ctx", None),
        P("dp", "ctx", None),
        P("dp", "ctx", None),
        P("dp", "ctx", None),
        P(None, None, "ctx", None),
        P("dp", None, None, "ctx", None),
    )
    return jax.shard_map(
        local,
        mesh=mesh,
        in_specs=placed,
        out_specs=(P("dp", "ctx", None), P("dp", "ctx", None), P(None, None, "ctx", None)),
        check_vma=False,
    )
```

```python
import functools

import jax
import jax.numpy as jnp
from jax import lax
from jax.experimental import pallas as pl
from jax.experimental.pallas import tpu as pltpu
from jax.sharding import PartitionSpec as P

RATE = 4.0
CA = 3.4445
CB = -4.775
CC = 2.0315
STEPS = 2
F32 = jnp.float32
BF16 = jnp.bfloat16
VMEM_SMALL = 8 * 1024 * 1024
VMEM_LARGE = 28 * 1024 * 1024
SMEM = pl.BlockSpec(memory_space=pltpu.SMEM)
VMEM = pl.BlockSpec(memory_space=pltpu.VMEM)
ANY = pl.BlockSpec(memory_space=pl.ANY)
HBM = pl.BlockSpec(memory_space=pltpu.HBM)


def dot_nn(a, b):
    return lax.dot_general(a, b, (((1,), (0,)), ((), ())), preferred_element_type=F32)


def dot_nt(a, b):
    return lax.dot_general(a, b, (((1,), (1,)), ((), ())), preferred_element_type=F32)


def dot_tn(a, b):
    return lax.dot_general(a, b, (((0,), (0,)), ((), ())), preferred_element_type=F32)


def call(
    kernel, out_shape, args, in_specs, out_specs, name, scratch=(), flops=10**6, size=10**6, vmem=VMEM_SMALL
):
    return pl.pallas_call(
        kernel,
        out_shape=out_shape,
        in_specs=in_specs,
        out_specs=out_specs,
        scratch_shapes=list(scratch),
        compiler_params=pltpu.CompilerParams(vmem_limit_bytes=vmem),
        cost_estimate=pl.CostEstimate(flops=flops, bytes_accessed=size, transcendentals=0),
        name=name,
    )(*args)


def swish_terms(g, s):
    rest = 1.0 - s
    both = s * rest
    bent = g * both
    return g * s, s + bent, 2.0 * both + bent * (rest - s)


def newton_pullback(grads, updates):
    each = range(len(grads))
    inv = [lax.rsqrt(jnp.sum(g * g, keepdims=True) + 1e-06) for g in grads]
    xs = [[(grads[m] * inv[m]).astype(BF16) for m in each]]
    grams = []
    polys = []
    for step in range(STEPS):
        x = xs[-1]
        gram = [dot_nt(x[m], x[m]).astype(BF16) for m in each]
        poly = [(CB * gram[m].astype(F32) + CC * dot_nn(gram[m], gram[m])).astype(BF16) for m in each]
        grams.append(gram)
        polys.append(poly)
        if step + 1 < STEPS:
            xs.append([(CA * x[m].astype(F32) + dot_nn(poly[m], x[m])).astype(BF16) for m in each])
    d = updates
    for step in reversed(range(STEPS)):
        x, gram, poly = xs[step], grams[step], polys[step]
        dp = [dot_nt(d[m], x[m]) for m in each]
        sym = [dp[m] + dp[m].T for m in each]
        turned = [dot_nn(sym[m].astype(BF16), gram[m]) for m in each]
        da = [(CB * sym[m] + CC * (turned[m] + turned[m].T)).astype(BF16) for m in each]
        d = [
            (CA * d[m].astype(F32) + dot_nn(poly[m], d[m]) + dot_nn(da[m], x[m])).astype(BF16)
            for m in each
        ]
    out = []
    for m in each:
        df = d[m].astype(F32)
        along = jnp.sum(df * grads[m], keepdims=True)
        out.append(df * inv[m] - grads[m] * (along * (inv[m] * inv[m] * inv[m])))
    return out


class Plan:
    def __init__(self, n, n_dp, tokens, heads, rows, width):
        self.n, self.n_dp = n, n_dp
        self.tokens, self.heads, self.rows, self.width = tokens, heads, rows, width
        self.per = -(-heads // n)
        self.mats = 3 * self.per
        least = max(1, self.per // 2)
        self.chunks = [(0, least), (least, self.per - least)]
        self.pair = min(2, n_dp)
        self.rest = n_dp // self.pair
        self.own = -(-self.mats // n_dp)
        self.block = -(-rows // 16) * 16
        self.share = -(-self.mats // self.pair)
        self.share_blocks = -(-self.share // least)

    def to(self, me, slot):
        return lax.rem(me[0] + slot, self.n)

    def source(self, me, slot):
        return lax.rem(me[0] + (self.n - slot), self.n)

    def head(self, me, slot):
        return jnp.minimum(self.to(me, slot) * self.per, self.heads - self.per)

    def mine(self, dp):
        return lax.rem(dp[0], self.pair)

    def other(self, dp, k):
        return jnp.bitwise_xor(lax.div(dp[0], self.pair), k)

    def packed_rows(self, chunk):
        return 4 * self.tokens + (3 + (self.share_blocks if chunk == 0 else 0)) * self.block

    def first_head(self, c):
        return min(c * self.per, self.heads - self.per)


def pack_kernel(me, dp, k_ref, v_ref, q_ref, o_ref, s_ref, t_ref, *refs, plan, slots, chunk):
    t, w = plan.tokens, plan.width
    first, count = plan.chunks[chunk]
    outs, (state, sems) = refs[:-2], refs[-2:]
    per = plan.per
    loads = []
    copies = []
    for k, slot in enumerate(slots):
        head = plan.head(me, slot)
        wanted = [(t_ref.at[0, :, pl.ds(head + first, count)], state.at[k, :, pl.ds(0, count)])]
        if chunk == 0:
            wanted.append((s_ref.at[:, pl.ds(head, per)], state.at[k, :, pl.ds(count, per)]))
        for i, (src, dst) in enumerate(wanted):
            loads.append(pltpu.make_async_copy(src, dst, sems.at[k, 4 + i]))
            loads[-1].start()
        cols = pl.ds(pl.multiple_of((head + first) * w, w), count * w)
        for i, src in enumerate((k_ref, v_ref, q_ref, o_ref)):
            copies.append(
                pltpu.make_async_copy(src.at[0, :, cols], outs[k].at[pl.ds(i * t, t), :], sems.at[k, i])
            )
            copies[-1].start()
    for load in loads:
        load.wait()
    for k in range(len(slots)):
        for j in range(count):
            for m in range(3):
                top = 4 * t + m * plan.block
                outs[k][top : top + plan.rows, j * w : (j + 1) * w] = state[k, m, j].astype(BF16)
        for q in range(plan.share if chunk == 0 else 0):
            mat = jnp.minimum(plan.mine(dp) * plan.share + q, plan.mats - 1)
            top = 4 * t + (3 + q // count) * plan.block
            left = (q % count) * w
            part = state[k, lax.rem(mat, 3), count + lax.div(mat, 3)]
            outs[k][top : top + plan.rows, left : left + w] = part.astype(BF16)
    for copy in copies:
        copy.wait()


def start_kernel(me, *refs, plan):
    in_refs, (out, whole) = refs[: plan.n], refs[plan.n :]
    count, w = plan.chunks[0][1], plan.width
    for slot in range(plan.n):
        at = pl.ds(pl.multiple_of(plan.source(me, slot) * plan.rows, plan.rows), plan.rows)
        for q in range(plan.share):
            top = 4 * plan.tokens + (3 + q // count) * plan.block
            left = (q % count) * w
            whole[q, at, :] = in_refs[slot][top : top + plan.rows, left : left + w].astype(F32)
    out[...] = whole[...].astype(BF16)


def tokens_of(refs, j, group, plan):
    t, w = plan.tokens, plan.width
    cols = slice(j * w, (j + 1) * w)
    top = 2 * group * t
    x = jnp.concatenate([r[top : top + t, cols] for r in refs], axis=0)
    y = jnp.concatenate([r[top + t : top + 2 * t, cols] for r in refs], axis=0)
    return x, y


def forward(x, y, wa, wb, wc):
    w = wa.shape[1]
    gu = dot_nn(x, jnp.concatenate([wa, wb], axis=1))
    g, u = gu[:, :w], gu[:, w:]
    p = dot_nn(y, wc)
    s = 0.5 + 0.5 * jnp.tanh(0.5 * g)
    sw, slope, _ = swish_terms(g, s)
    hidden = (sw * u).astype(BF16)
    dg = (p * u * slope).astype(BF16)
    du = (p * sw).astype(BF16)
    ab = dot_tn(x, jnp.concatenate([dg, du], axis=1))
    return (ab[:, :w], ab[:, w:], dot_tn(y, hidden)), (g, u, p, s), (dg, du, hidden)


def chunk_kernel(me, dp, *refs, plan, chunk):
    n, t, w = plan.n, plan.tokens, plan.width
    first, count = plan.chunks[chunk]
    last = chunk + 1 == len(plan.chunks)
    mats = 3 * count
    refs = list(refs)

    def take(k):
        got = refs[:k]
        del refs[:k]
        return got

    in_refs = take(n)
    shares = take(plan.pair)
    (before,) = take(1) if last else (None,)
    (d_ref,) = take(1)
    c_refs = take(2 if last else 1)
    w0, w1, gsum, ssum, acts, fields = take(6)
    total = take(1)[0] if last else c_refs[0]
    base = 3 * first if last else 0

    for slot in range(n):
        at = pl.ds(pl.multiple_of(plan.source(me, slot) * plan.rows, plan.rows), plan.rows)
        for j in range(count):
            for m in range(3):
                top = 4 * t + m * plan.block
                part = in_refs[slot][top : top + plan.rows, j * w : (j + 1) * w]
                w1[3 * j + m, at, :] = part.astype(F32)
    for k, part in enumerate(shares):
        at = jnp.bitwise_xor(plan.mine(dp), k) * plan.share
        w0[pl.ds(at, plan.share)] = part[...]

    for j in range(count):
        x, y = tokens_of(in_refs, j, 0, plan)
        sums, act, field = forward(x, y, *[w0[3 * (first + j) + m] for m in range(3)])
        for m in range(3):
            gsum[3 * j + m] = sums[m]
            fields[j, m] = field[m]
        for i, val in enumerate(act):
            acts[j, i] = val
        x, y = tokens_of(in_refs, j, 1, plan)
        sums, _, _ = forward(x, y, *[w1[3 * j + m].astype(BF16) for m in range(3)])
        for m in range(3):
            ssum[3 * j + m] = sums[m]

    grads = [gsum[m] for m in range(mats)]
    updates = [(RATE * ssum[m]).astype(BF16) for m in range(mats)]
    for m, val in enumerate(newton_pullback(grads, updates)):
        gsum[m] = val

    for j in range(count):
        x, y = tokens_of(in_refs, j, 0, plan)
        fab = jnp.concatenate([gsum[3 * j], gsum[3 * j + 1]], axis=1).astype(BF16)
        fc = gsum[3 * j + 2].astype(BF16)
        at = 3 * (first + j)
        wab = jnp.concatenate([w0[at], w0[at + 1]], axis=1)
        wc = w0[at + 2]
        cdgu = dot_nn(x, fab)
        cdg, cdu = cdgu[:, :w], cdgu[:, w:]
        ch = dot_nn(y, fc)
        g, u, p, s = [acts[j, i] for i in range(4)]
        sw, slope, curve = swish_terms(g, s)
        cg = ((ch * u + cdu * p) * slope + cdg * (p * u) * curve).astype(BF16)
        cu = (ch * sw + cdg * p * slope).astype(BF16)
        cp = (cdu * sw + cdg * u * slope).astype(BF16)
        dg, du, hidden = fields[j, 0], fields[j, 1], fields[j, 2]
        dx = dot_nt(jnp.concatenate([dg, du, cg, cu], axis=1), jnp.concatenate([fab, wab], axis=1))
        dy = dot_nt(jnp.concatenate([hidden, cp], axis=1), jnp.concatenate([fc, wc], axis=1))
        cols = slice(j * w, (j + 1) * w)
        for slot in range(n):
            to = plan.source(me, slot)
            d_ref[to, 0:t, cols] = dx[slot * t : (slot + 1) * t].astype(BF16)
            d_ref[to, t : 2 * t, cols] = dy[slot * t : (slot + 1) * t].astype(BF16)
        ab = dot_tn(x, jnp.concatenate([cg, cu], axis=1))
        grown = (ab[:, :w], ab[:, w:], dot_tn(y, cp))
        for m in range(3):
            total[base + 3 * j + m] = (ssum[3 * j + m] + grown[m]).astype(BF16)

    if last:
        total[0 : before.shape[0]] = before[...]
        for m in range(plan.mats, plan.n_dp * plan.own):
            total[m] = jnp.zeros((w, w), BF16)
        mine = plan.mine(dp)
        for r in range(plan.rest):
            to = slice(r * plan.own, (r + 1) * plan.own)
            for ref, which in zip(c_refs, (mine, plan.pair - 1 - mine)):
                ref[to] = total[pl.ds((plan.pair * r + which) * plan.own, plan.own)]


def pair_kernel(dp, keep_ref, got_ref, *refs, plan):
    outs, whole = refs[:-1], refs[-1]
    whole[...] = keep_ref[...].astype(F32) + got_ref[...].astype(F32)
    for k in range(plan.rest):
        outs[k][...] = whole[pl.ds(plan.other(dp, k) * plan.own, plan.own)].astype(BF16)


def sum_kernel(me, *refs, plan):
    parts, outs, whole = refs[: plan.rest], refs[plan.rest : -1], refs[-1]
    added = parts[0][...].astype(F32)
    for part in parts[1:]:
        added = added + part[...].astype(F32)
    whole[...] = added / plan.n_dp
    for slot in range(plan.n):
        at = pl.ds(pl.multiple_of(plan.to(me, slot) * plan.rows, plan.rows), plan.rows)
        outs[slot][...] = whole[:, at, :].astype(BF16)


def rows_kernel(me, *refs, plan):
    for slot, part in enumerate(refs[:-1]):
        refs[-1][plan.source(me, slot)] = part[...]


def rest_kernel(dp, *refs, plan):
    for k, part in enumerate(refs[:-1]):
        refs[-1][plan.other(dp, k)] = part[...]


def state_kernel(dp, *refs, plan):
    out = refs[-1]
    for k in range(plan.pair):
        for r in range(plan.rest):
            for i in range(plan.own):
                mat = (plan.pair * r + jnp.bitwise_xor(plan.mine(dp), k)) * plan.own + i

                @pl.when(mat < plan.mats)
                def _(mat=mat, ref=refs[k], r=r, i=i):
                    for c in range(plan.n):
                        head = plan.first_head(c) + lax.div(mat, 3)
                        out[lax.rem(mat, 3), head] = ref[r, c, i].astype(F32)


def unpack_kernel(*refs, plan):
    t, w = plan.tokens, plan.width
    ins, (dk, dv, sems) = refs[:-3], refs[-3:]
    copies = []
    for c, (first, count) in enumerate(plan.chunks):
        for owner in range(plan.n):
            cols = pl.ds((plan.first_head(owner) + first) * w, count * w)
            for part, dst in enumerate((dk, dv)):
                copy = pltpu.make_async_copy(
                    ins[c].at[owner, pl.ds(part * t, t), :],
                    dst.at[0, :, cols],
                    sems.at[(c * plan.n + owner) * 2 + part],
                )
                copy.start()
                copies.append(copy)
            if plan.n * plan.per != plan.heads:
                for copy in copies:
                    copy.wait()
                copies = []
    for copy in copies:
        copy.wait()


def local(keys_a, values_a, queries_b, grad_out, state_start, state_next):
    n, n_dp = lax.axis_size("ctx"), lax.axis_size("dp")
    _, heads, rows, width = state_start.shape
    t = keys_a.shape[1]
    plan = Plan(n, n_dp, t, heads, rows, width)
    per, own, chunks = plan.per, plan.own, plan.chunks
    bind = lambda kernel, **more: functools.partial(kernel, plan=plan, **more)

    me, dp = lax.axis_index("ctx").reshape(1), lax.axis_index("dp").reshape(1)

    def swap(value, k):
        if k == 0:
            return value
        return lax.ppermute(value, "dp", [(i, i ^ k) for i in range(n_dp)])

    def shift(value, s):
        if s == 0:
            return value
        return lax.ppermute(value, "ctx", [(i, (i + s) % n) for i in range(n)])

    def turn(value):
        return lax.all_to_all(value, "ctx", split_axis=0, concat_axis=0, tiled=True)

    def shape(*dims, dtype=BF16):
        return jax.ShapeDtypeStruct(dims, dtype)

    def pack(c, slots, keys):
        args = (keys, values_a, queries_b, grad_out, state_start, state_next)
        outs = call(
            bind(pack_kernel, slots=slots, chunk=c),
            [shape(plan.packed_rows(c), chunks[c][1] * width)] * len(slots),
            (me, dp, *[pltpu.with_memory_space_constraint(arg, pltpu.HBM) for arg in args]),
            [SMEM] * 2 + [HBM] * 6,
            [VMEM] * len(slots),
            f"pack{c}_{slots[0]}",
            [
                pltpu.VMEM((len(slots), 3, chunks[c][1] + (0 if c else per), rows, width), F32),
                pltpu.SemaphoreType.DMA((len(slots), 6)),
            ],
        )
        return list(outs)

    sent = pack(0, range(1, n), keys_a)
    keys, sent = lax.optimization_barrier((keys_a, sent))
    arrived = [[shift(v, s + 1) for s, v in enumerate(sent)]]
    sent = pack(1, range(1, n), keys)
    keys, sent = lax.optimization_barrier((keys_a, sent))
    arrived.append([shift(v, s + 1) for s, v in enumerate(sent)])
    arrived = [pack(c, range(1), keys) + arrived[c] for c in range(2)]
    start_own = call(
        bind(start_kernel),
        shape(plan.share, width, width),
        (me, *arrived[0]),
        [SMEM] + [VMEM] * n,
        VMEM,
        "start_share",
        [pltpu.VMEM((plan.share, width, width), F32)],
    )
    shares = [swap(start_own, k) for k in range(plan.pair)]

    before = []
    grads = []
    for c, (_, count) in enumerate(chunks):
        last = c + 1 == len(chunks)
        if last:
            outs = [shape(plan.rest * own, width, width)] * 2
        else:
            outs = [shape(3 * count, width, width)]
        outs = [shape(n, 2 * t, count * width)] + outs
        scratch = [pltpu.VMEM((plan.pair * plan.share, width, width), BF16)]
        scratch += [pltpu.VMEM((3 * count, width, width), F32)] * 3 + [
            pltpu.VMEM((count, 4, n * t, width), F32),
            pltpu.VMEM((count, 3, n * t, width), BF16),
        ]
        if last:
            scratch.append(pltpu.VMEM((n_dp * own, width, width), BF16))
        got = call(
            bind(chunk_kernel, chunk=c),
            outs,
            (me, dp, *arrived[c], *shares, *before),
            [SMEM] * 2 + [VMEM] * (n + plan.pair + len(before)),
            [VMEM] * len(outs),
            f"chunk{c}",
            scratch,
            flops=count * 640 * 10**6,
            size=count * 10**6,
            vmem=VMEM_LARGE,
        )
        grads.append(got[0])
        before = [got[1]]
    late, early = grads
    c_keep, c_send = got[1:]
    early, c_send = lax.optimization_barrier((early, c_send))
    early = turn(early)

    halves = call(
        bind(pair_kernel),
        [shape(own, width, width)] * plan.rest,
        (dp, c_keep, swap(c_send, plan.pair - 1)),
        [SMEM] + [VMEM] * 2,
        [VMEM] * plan.rest,
        "state_pair",
        [pltpu.VMEM((plan.rest * own, width, width), F32)],
    )
    halves = [swap(halves[k], plan.pair * k) for k in range(plan.rest)]
    by_rows = call(
        bind(sum_kernel),
        [shape(own, rows, width)] * n,
        (me, *halves),
        [SMEM] + [VMEM] * plan.rest,
        [VMEM] * n,
        "state_sum",
        [pltpu.VMEM((own, width, width), F32)],
    )
    by_rows = [shift(by_rows[s], s) for s in range(n)]
    by_rows[0], early = lax.optimization_barrier((by_rows[0], early))
    mine = call(
        bind(rows_kernel),
        shape(n, own, rows, width),
        (me, *by_rows),
        [SMEM] + [VMEM] * n,
        VMEM,
        "state_rows",
    )
    mine, late = lax.optimization_barrier((mine, late))
    late = turn(late)
    rest = [swap(mine, plan.pair * k) for k in range(plan.rest)]
    half = call(
        bind(rest_kernel),
        shape(plan.rest, n, own, rows, width),
        (dp, *rest),
        [SMEM] + [VMEM] * plan.rest,
        VMEM,
        "state_rest",
    )
    both = [swap(half, k) for k in range(plan.pair)]
    grad_state = call(
        bind(state_kernel),
        shape(*state_start.shape, dtype=F32),
        (dp, *both),
        [SMEM] + [VMEM] * plan.pair,
        VMEM,
        "state_out",
    )
    grad_keys, grad_values = call(
        bind(unpack_kernel),
        [shape(*keys_a.shape), shape(*values_a.shape)],
        (late, early),
        [VMEM] * 2,
        [ANY] * 2,
        "unpack",
        [pltpu.SemaphoreType.DMA((4 * n,))],
    )
    return grad_keys, grad_values, grad_state


def solution(mesh):
    placed = (
        P("dp", "ctx", None),
        P("dp", "ctx", None),
        P("dp", "ctx", None),
        P("dp", "ctx", None),
        P(None, None, "ctx", None),
        P("dp", None, None, "ctx", None),
    )
    return jax.shard_map(
        local,
        mesh=mesh,
        in_specs=placed,
        out_specs=(P("dp", "ctx", None), P("dp", "ctx", None), P(None, None, "ctx", None)),
        check_vma=False,
    )
```

```python
import functools

import jax
import jax.numpy as jnp
from jax import lax
from jax.experimental import pallas as pl
from jax.experimental.pallas import tpu as pltpu
from jax.sharding import PartitionSpec as P

RATE = 4.0
CA = 3.4445
CB = -4.775
CC = 2.0315
STEPS = 2
F32 = jnp.float32
BF16 = jnp.bfloat16
VMEM_SMALL = 8 * 1024 * 1024
VMEM_LARGE = 28 * 1024 * 1024
SMEM = pl.BlockSpec(memory_space=pltpu.SMEM)
VMEM = pl.BlockSpec(memory_space=pltpu.VMEM)
ANY = pl.BlockSpec(memory_space=pl.ANY)
HBM = pl.BlockSpec(memory_space=pltpu.HBM)


def dot_nn(a, b):
    return lax.dot_general(a, b, (((1,), (0,)), ((), ())), preferred_element_type=F32)


def dot_nt(a, b):
    return lax.dot_general(a, b, (((1,), (1,)), ((), ())), preferred_element_type=F32)


def dot_tn(a, b):
    return lax.dot_general(a, b, (((0,), (0,)), ((), ())), preferred_element_type=F32)


def call(
    kernel, out_shape, args, in_specs, out_specs, name, scratch=(), flops=10**6, size=10**6, vmem=VMEM_SMALL
):
    return pl.pallas_call(
        kernel,
        out_shape=out_shape,
        in_specs=in_specs,
        out_specs=out_specs,
        scratch_shapes=list(scratch),
        compiler_params=pltpu.CompilerParams(vmem_limit_bytes=vmem),
        cost_estimate=pl.CostEstimate(flops=flops, bytes_accessed=size, transcendentals=0),
        name=name,
    )(*args)


def swish_terms(g, s):
    rest = 1.0 - s
    both = s * rest
    bent = g * both
    return g * s, s + bent, 2.0 * both + bent * (rest - s)


def newton_pullback(grads, updates):
    each = range(len(grads))
    inv = [lax.rsqrt(jnp.sum(g * g, keepdims=True) + 1e-06) for g in grads]
    xs = [[(grads[m] * inv[m]).astype(BF16) for m in each]]
    grams = []
    polys = []
    for step in range(STEPS):
        x = xs[-1]
        gram = [dot_nt(x[m], x[m]).astype(BF16) for m in each]
        poly = [(CB * gram[m].astype(F32) + CC * dot_nn(gram[m], gram[m])).astype(BF16) for m in each]
        grams.append(gram)
        polys.append(poly)
        if step + 1 < STEPS:
            xs.append([(CA * x[m].astype(F32) + dot_nn(poly[m], x[m])).astype(BF16) for m in each])
    d = updates
    for step in reversed(range(STEPS)):
        x, gram, poly = xs[step], grams[step], polys[step]
        dp = [dot_nt(d[m], x[m]) for m in each]
        sym = [dp[m] + dp[m].T for m in each]
        turned = [dot_nn(sym[m].astype(BF16), gram[m]) for m in each]
        da = [(CB * sym[m] + CC * (turned[m] + turned[m].T)).astype(BF16) for m in each]
        d = [
            (CA * d[m].astype(F32) + dot_nn(poly[m], d[m]) + dot_nn(da[m], x[m])).astype(BF16)
            for m in each
        ]
    out = []
    for m in each:
        df = d[m].astype(F32)
        along = jnp.sum(df * grads[m], keepdims=True)
        out.append(df * inv[m] - grads[m] * (along * (inv[m] * inv[m] * inv[m])))
    return out


class Plan:
    def __init__(self, n, n_dp, tokens, heads, rows, width):
        self.n, self.n_dp = n, n_dp
        self.tokens, self.heads, self.rows, self.width = tokens, heads, rows, width
        self.per = -(-heads // n)
        self.mats = 3 * self.per
        least = max(1, self.per // 2)
        self.chunks = [(0, least), (least, self.per - least)]
        self.pair = min(2, n_dp)
        self.rest = n_dp // self.pair
        self.own = -(-self.mats // n_dp)
        self.block = -(-rows // 16) * 16
        self.group = min(4, n_dp)
        self.share = -(-self.mats // self.group)
        self.share_blocks = -(-self.share // least)

    def to(self, me, slot):
        return lax.rem(me[0] + slot, self.n)

    def source(self, me, slot):
        return lax.rem(me[0] + (self.n - slot), self.n)

    def head(self, me, slot):
        return jnp.minimum(self.to(me, slot) * self.per, self.heads - self.per)

    def mine(self, dp):
        return lax.rem(dp[0], self.pair)

    def member(self, dp):
        return lax.rem(dp[0], self.group)

    def other(self, dp, k):
        return jnp.bitwise_xor(lax.div(dp[0], self.pair), k)

    def packed_rows(self, chunk):
        return 4 * self.tokens + (3 + (self.share_blocks if chunk == 0 else 0)) * self.block

    def first_head(self, c):
        return min(c * self.per, self.heads - self.per)


def pack_kernel(me, dp, k_ref, v_ref, q_ref, o_ref, s_ref, t_ref, *refs, plan, slots, chunk):
    t, w = plan.tokens, plan.width
    first, count = plan.chunks[chunk]
    outs, (state, sems) = refs[:-2], refs[-2:]
    per = plan.per
    loads = []
    copies = []
    for k, slot in enumerate(slots):
        head = plan.head(me, slot)
        wanted = [(t_ref.at[0, :, pl.ds(head + first, count)], state.at[k, :, pl.ds(0, count)])]
        if chunk == 0:
            wanted.append((s_ref.at[:, pl.ds(head, per)], state.at[k, :, pl.ds(count, per)]))
        for i, (src, dst) in enumerate(wanted):
            loads.append(pltpu.make_async_copy(src, dst, sems.at[k, 4 + i]))
            loads[-1].start()
        cols = pl.ds(pl.multiple_of((head + first) * w, w), count * w)
        for i, src in enumerate((k_ref, v_ref, q_ref, o_ref)):
            copies.append(
                pltpu.make_async_copy(src.at[0, :, cols], outs[k].at[pl.ds(i * t, t), :], sems.at[k, i])
            )
            copies[-1].start()
    for load in loads:
        load.wait()
    for k in range(len(slots)):
        for j in range(count):
            for m in range(3):
                top = 4 * t + m * plan.block
                outs[k][top : top + plan.rows, j * w : (j + 1) * w] = state[k, m, j].astype(BF16)
        for q in range(plan.share if chunk == 0 else 0):
            mat = jnp.minimum(plan.member(dp) * plan.share + q, plan.mats - 1)
            top = 4 * t + (3 + q // count) * plan.block
            left = (q % count) * w
            part = state[k, lax.rem(mat, 3), count + lax.div(mat, 3)]
            outs[k][top : top + plan.rows, left : left + w] = part.astype(BF16)
    for copy in copies:
        copy.wait()


def start_kernel(me, *refs, plan):
    in_refs, (out, whole) = refs[: plan.n], refs[plan.n :]
    count, w = plan.chunks[0][1], plan.width
    for slot in range(plan.n):
        at = pl.ds(pl.multiple_of(plan.source(me, slot) * plan.rows, plan.rows), plan.rows)
        for q in range(plan.share):
            top = 4 * plan.tokens + (3 + q // count) * plan.block
            left = (q % count) * w
            whole[q, at, :] = in_refs[slot][top : top + plan.rows, left : left + w].astype(F32)
    out[...] = whole[...].astype(BF16)


def tokens_of(refs, j, group, plan):
    t, w = plan.tokens, plan.width
    cols = slice(j * w, (j + 1) * w)
    top = 2 * group * t
    x = jnp.concatenate([r[top : top + t, cols] for r in refs], axis=0)
    y = jnp.concatenate([r[top + t : top + 2 * t, cols] for r in refs], axis=0)
    return x, y


def forward(x, y, wa, wb, wc):
    w = wa.shape[1]
    gu = dot_nn(x, jnp.concatenate([wa, wb], axis=1))
    g, u = gu[:, :w], gu[:, w:]
    p = dot_nn(y, wc)
    s = 0.5 + 0.5 * jnp.tanh(0.5 * g)
    sw, slope, _ = swish_terms(g, s)
    hidden = (sw * u).astype(BF16)
    dg = (p * u * slope).astype(BF16)
    du = (p * sw).astype(BF16)
    ab = dot_tn(x, jnp.concatenate([dg, du], axis=1))
    return (ab[:, :w], ab[:, w:], dot_tn(y, hidden)), (g, u, p, s), (dg, du, hidden)


def chunk_kernel(me, dp, *refs, plan, chunk):
    n, t, w = plan.n, plan.tokens, plan.width
    first, count = plan.chunks[chunk]
    last = chunk + 1 == len(plan.chunks)
    mats = 3 * count
    refs = list(refs)

    def take(k):
        got = refs[:k]
        del refs[:k]
        return got

    in_refs = take(n)
    shares = take(plan.group)
    (before,) = take(1) if last else (None,)
    (d_ref,) = take(1)
    c_refs = take(2 if last else 1)
    w0, w1, gsum, ssum, acts, fields = take(6)
    total = take(1)[0] if last else c_refs[0]
    base = 3 * first if last else 0

    for slot in range(n):
        at = pl.ds(pl.multiple_of(plan.source(me, slot) * plan.rows, plan.rows), plan.rows)
        for j in range(count):
            for m in range(3):
                top = 4 * t + m * plan.block
                part = in_refs[slot][top : top + plan.rows, j * w : (j + 1) * w]
                w1[3 * j + m, at, :] = part.astype(F32)
    for k, part in enumerate(shares):
        at = jnp.bitwise_xor(plan.member(dp), k) * plan.share
        w0[pl.ds(at, plan.share)] = part[...]

    for j in range(count):
        x, y = tokens_of(in_refs, j, 0, plan)
        sums, act, field = forward(x, y, *[w0[3 * (first + j) + m] for m in range(3)])
        for m in range(3):
            gsum[3 * j + m] = sums[m]
            fields[j, m] = field[m]
        for i, val in enumerate(act):
            acts[j, i] = val
        x, y = tokens_of(in_refs, j, 1, plan)
        sums, _, _ = forward(x, y, *[w1[3 * j + m].astype(BF16) for m in range(3)])
        for m in range(3):
            ssum[3 * j + m] = sums[m]

    grads = [gsum[m] for m in range(mats)]
    updates = [(RATE * ssum[m]).astype(BF16) for m in range(mats)]
    for m, val in enumerate(newton_pullback(grads, updates)):
        gsum[m] = val

    for j in range(count):
        x, y = tokens_of(in_refs, j, 0, plan)
        fab = jnp.concatenate([gsum[3 * j], gsum[3 * j + 1]], axis=1).astype(BF16)
        fc = gsum[3 * j + 2].astype(BF16)
        at = 3 * (first + j)
        wab = jnp.concatenate([w0[at], w0[at + 1]], axis=1)
        wc = w0[at + 2]
        cdgu = dot_nn(x, fab)
        cdg, cdu = cdgu[:, :w], cdgu[:, w:]
        ch = dot_nn(y, fc)
        g, u, p, s = [acts[j, i] for i in range(4)]
        sw, slope, curve = swish_terms(g, s)
        cg = ((ch * u + cdu * p) * slope + cdg * (p * u) * curve).astype(BF16)
        cu = (ch * sw + cdg * p * slope).astype(BF16)
        cp = (cdu * sw + cdg * u * slope).astype(BF16)
        dg, du, hidden = fields[j, 0], fields[j, 1], fields[j, 2]
        dx = dot_nt(jnp.concatenate([dg, du, cg, cu], axis=1), jnp.concatenate([fab, wab], axis=1))
        dy = dot_nt(jnp.concatenate([hidden, cp], axis=1), jnp.concatenate([fc, wc], axis=1))
        cols = slice(j * w, (j + 1) * w)
        for slot in range(n):
            to = plan.source(me, slot)
            d_ref[to, 0:t, cols] = dx[slot * t : (slot + 1) * t].astype(BF16)
            d_ref[to, t : 2 * t, cols] = dy[slot * t : (slot + 1) * t].astype(BF16)
        ab = dot_tn(x, jnp.concatenate([cg, cu], axis=1))
        grown = (ab[:, :w], ab[:, w:], dot_tn(y, cp))
        for m in range(3):
            total[base + 3 * j + m] = (ssum[3 * j + m] + grown[m]).astype(BF16)

    if last:
        total[0 : before.shape[0]] = before[...]
        for m in range(plan.mats, plan.n_dp * plan.own):
            total[m] = jnp.zeros((w, w), BF16)
        mine = plan.mine(dp)
        for r in range(plan.rest):
            to = slice(r * plan.own, (r + 1) * plan.own)
            for ref, which in zip(c_refs, (mine, plan.pair - 1 - mine)):
                ref[to] = total[pl.ds((plan.pair * r + which) * plan.own, plan.own)]


def pair_kernel(dp, keep_ref, got_ref, *refs, plan):
    outs, whole = refs[:-1], refs[-1]
    whole[...] = keep_ref[...].astype(F32) + got_ref[...].astype(F32)
    for k in range(plan.rest):
        outs[k][...] = whole[pl.ds(plan.other(dp, k) * plan.own, plan.own)].astype(BF16)


def sum_kernel(me, *refs, plan):
    parts, outs, whole = refs[: plan.rest], refs[plan.rest : -1], refs[-1]
    added = parts[0][...].astype(F32)
    for part in parts[1:]:
        added = added + part[...].astype(F32)
    whole[...] = added / plan.n_dp
    for slot in range(plan.n):
        at = pl.ds(pl.multiple_of(plan.to(me, slot) * plan.rows, plan.rows), plan.rows)
        outs[slot][...] = whole[:, at, :].astype(BF16)


def rows_kernel(me, *refs, plan):
    for slot, part in enumerate(refs[:-1]):
        refs[-1][plan.source(me, slot)] = part[...]


def rest_kernel(dp, *refs, plan):
    for k, part in enumerate(refs[:-1]):
        refs[-1][plan.other(dp, k)] = part[...]


def state_kernel(dp, *refs, plan):
    out = refs[-1]
    for k in range(plan.pair):
        for r in range(plan.rest):
            for i in range(plan.own):
                mat = (plan.pair * r + jnp.bitwise_xor(plan.mine(dp), k)) * plan.own + i

                @pl.when(mat < plan.mats)
                def _(mat=mat, ref=refs[k], r=r, i=i):
                    for c in range(plan.n):
                        head = plan.first_head(c) + lax.div(mat, 3)
                        out[lax.rem(mat, 3), head] = ref[r, c, i].astype(F32)


def unpack_kernel(*refs, plan):
    t, w = plan.tokens, plan.width
    ins, (dk, dv, sems) = refs[:-3], refs[-3:]
    copies = []
    for c, (first, count) in enumerate(plan.chunks):
        for owner in range(plan.n):
            cols = pl.ds((plan.first_head(owner) + first) * w, count * w)
            for part, dst in enumerate((dk, dv)):
                copy = pltpu.make_async_copy(
                    ins[c].at[owner, pl.ds(part * t, t), :],
                    dst.at[0, :, cols],
                    sems.at[(c * plan.n + owner) * 2 + part],
                )
                copy.start()
                copies.append(copy)
            if plan.n * plan.per != plan.heads:
                for copy in copies:
                    copy.wait()
                copies = []
    for copy in copies:
        copy.wait()


def local(keys_a, values_a, queries_b, grad_out, state_start, state_next):
    n, n_dp = lax.axis_size("ctx"), lax.axis_size("dp")
    _, heads, rows, width = state_start.shape
    t = keys_a.shape[1]
    plan = Plan(n, n_dp, t, heads, rows, width)
    per, own, chunks = plan.per, plan.own, plan.chunks
    bind = lambda kernel, **more: functools.partial(kernel, plan=plan, **more)

    me, dp = lax.axis_index("ctx").reshape(1), lax.axis_index("dp").reshape(1)

    def swap(value, k):
        if k == 0:
            return value
        return lax.ppermute(value, "dp", [(i, i ^ k) for i in range(n_dp)])

    def shift(value, s):
        if s == 0:
            return value
        return lax.ppermute(value, "ctx", [(i, (i + s) % n) for i in range(n)])

    def turn(value):
        return lax.all_to_all(value, "ctx", split_axis=0, concat_axis=0, tiled=True)

    def shape(*dims, dtype=BF16):
        return jax.ShapeDtypeStruct(dims, dtype)

    def pack(c, slots, keys):
        args = (keys, values_a, queries_b, grad_out, state_start, state_next)
        outs = call(
            bind(pack_kernel, slots=slots, chunk=c),
            [shape(plan.packed_rows(c), chunks[c][1] * width)] * len(slots),
            (me, dp, *[pltpu.with_memory_space_constraint(arg, pltpu.HBM) for arg in args]),
            [SMEM] * 2 + [HBM] * 6,
            [VMEM] * len(slots),
            f"pack{c}_{slots[0]}",
            [
                pltpu.VMEM((len(slots), 3, chunks[c][1] + (0 if c else per), rows, width), F32),
                pltpu.SemaphoreType.DMA((len(slots), 6)),
            ],
        )
        return list(outs)

    sent = pack(0, range(1, n), keys_a)
    keys, sent = lax.optimization_barrier((keys_a, sent))
    arrived = [[shift(v, s + 1) for s, v in enumerate(sent)]]
    sent = pack(1, range(1, n), keys)
    keys, sent = lax.optimization_barrier((keys_a, sent))
    arrived.append([shift(v, s + 1) for s, v in enumerate(sent)])
    arrived = [pack(c, range(1), keys) + arrived[c] for c in range(2)]
    start_own = call(
        bind(start_kernel),
        shape(plan.share, width, width),
        (me, *arrived[0]),
        [SMEM] + [VMEM] * n,
        VMEM,
        "start_share",
        [pltpu.VMEM((plan.share, width, width), F32)],
    )
    shares = [swap(start_own, k) for k in range(plan.group)]

    before = []
    grads = []
    for c, (_, count) in enumerate(chunks):
        last = c + 1 == len(chunks)
        if last:
            outs = [shape(plan.rest * own, width, width)] * 2
        else:
            outs = [shape(3 * count, width, width)]
        outs = [shape(n, 2 * t, count * width)] + outs
        scratch = [pltpu.VMEM((plan.group * plan.share, width, width), BF16)]
        scratch += [pltpu.VMEM((3 * count, width, width), F32)] * 3 + [
            pltpu.VMEM((count, 4, n * t, width), F32),
            pltpu.VMEM((count, 3, n * t, width), BF16),
        ]
        if last:
            scratch.append(pltpu.VMEM((n_dp * own, width, width), BF16))
        got = call(
            bind(chunk_kernel, chunk=c),
            outs,
            (me, dp, *arrived[c], *shares, *before),
            [SMEM] * 2 + [VMEM] * (n + plan.group + len(before)),
            [VMEM] * len(outs),
            f"chunk{c}",
            scratch,
            flops=count * 640 * 10**6,
            size=count * 10**6,
            vmem=VMEM_LARGE,
        )
        grads.append(got[0])
        before = [got[1]]
    late, early = grads
    c_keep, c_send = got[1:]
    early, c_send = lax.optimization_barrier((early, c_send))
    early = turn(early)

    halves = call(
        bind(pair_kernel),
        [shape(own, width, width)] * plan.rest,
        (dp, c_keep, swap(c_send, plan.pair - 1)),
        [SMEM] + [VMEM] * 2,
        [VMEM] * plan.rest,
        "state_pair",
        [pltpu.VMEM((plan.rest * own, width, width), F32)],
    )
    halves = [swap(halves[k], plan.pair * k) for k in range(plan.rest)]
    by_rows = call(
        bind(sum_kernel),
        [shape(own, rows, width)] * n,
        (me, *halves),
        [SMEM] + [VMEM] * plan.rest,
        [VMEM] * n,
        "state_sum",
        [pltpu.VMEM((own, width, width), F32)],
    )
    by_rows = [shift(by_rows[s], s) for s in range(n)]
    by_rows[0], early = lax.optimization_barrier((by_rows[0], early))
    mine = call(
        bind(rows_kernel),
        shape(n, own, rows, width),
        (me, *by_rows),
        [SMEM] + [VMEM] * n,
        VMEM,
        "state_rows",
    )
    mine, late = lax.optimization_barrier((mine, late))
    late = turn(late)
    rest = [swap(mine, plan.pair * k) for k in range(plan.rest)]
    half = call(
        bind(rest_kernel),
        shape(plan.rest, n, own, rows, width),
        (dp, *rest),
        [SMEM] + [VMEM] * plan.rest,
        VMEM,
        "state_rest",
    )
    both = [swap(half, k) for k in range(plan.pair)]
    grad_state = call(
        bind(state_kernel),
        shape(*state_start.shape, dtype=F32),
        (dp, *both),
        [SMEM] + [VMEM] * plan.pair,
        VMEM,
        "state_out",
    )
    grad_keys, grad_values = call(
        bind(unpack_kernel),
        [shape(*keys_a.shape), shape(*values_a.shape)],
        (late, early),
        [VMEM] * 2,
        [ANY] * 2,
        "unpack",
        [pltpu.SemaphoreType.DMA((4 * n,))],
    )
    return grad_keys, grad_values, grad_state


def solution(mesh):
    placed = (
        P("dp", "ctx", None),
        P("dp", "ctx", None),
        P("dp", "ctx", None),
        P("dp", "ctx", None),
        P(None, None, "ctx", None),
        P("dp", None, None, "ctx", None),
    )
    return jax.shard_map(
        local,
        mesh=mesh,
        in_specs=placed,
        out_specs=(P("dp", "ctx", None), P("dp", "ctx", None), P(None, None, "ctx", None)),
        check_vma=False,
    )
```

```python
import functools

import jax
import jax.numpy as jnp
from jax import lax
from jax.experimental import pallas as pl
from jax.experimental.pallas import tpu as pltpu
from jax.sharding import PartitionSpec as P

RATE = 4.0
CA = 3.4445
CB = -4.775
CC = 2.0315
STEPS = 2
F32 = jnp.float32
BF16 = jnp.bfloat16
VMEM_SMALL = 8 * 1024 * 1024
VMEM_LARGE = 28 * 1024 * 1024
SMEM = pl.BlockSpec(memory_space=pltpu.SMEM)
VMEM = pl.BlockSpec(memory_space=pltpu.VMEM)
ANY = pl.BlockSpec(memory_space=pl.ANY)
HBM = pl.BlockSpec(memory_space=pltpu.HBM)


def dot_nn(a, b):
    return lax.dot_general(a, b, (((1,), (0,)), ((), ())), preferred_element_type=F32)


def dot_nt(a, b):
    return lax.dot_general(a, b, (((1,), (1,)), ((), ())), preferred_element_type=F32)


def call(
    kernel, out_shape, args, in_specs, out_specs, name, scratch=(), flops=10**6, size=10**6, vmem=VMEM_SMALL
):
    return pl.pallas_call(
        kernel,
        out_shape=out_shape,
        in_specs=in_specs,
        out_specs=out_specs,
        scratch_shapes=list(scratch),
        compiler_params=pltpu.CompilerParams(vmem_limit_bytes=vmem),
        cost_estimate=pl.CostEstimate(flops=flops, bytes_accessed=size, transcendentals=0),
        name=name,
    )(*args)


def swish_terms(g, s):
    rest = 1.0 - s
    both = s * rest
    bent = g * both
    return g * s, s + bent, 2.0 * both + bent * (rest - s)


def newton_pullback(grads, updates):
    each = range(len(grads))
    inv = [lax.rsqrt(jnp.sum(g * g, keepdims=True) + 1e-06) for g in grads]
    xs = [[(grads[m] * inv[m]).astype(BF16) for m in each]]
    grams = []
    polys = []
    for step in range(STEPS):
        x = xs[-1]
        gram = [dot_nt(x[m], x[m]).astype(BF16) for m in each]
        poly = [(CB * gram[m].astype(F32) + CC * dot_nn(gram[m], gram[m])).astype(BF16) for m in each]
        grams.append(gram)
        polys.append(poly)
        if step + 1 < STEPS:
            xs.append([(CA * x[m].astype(F32) + dot_nn(poly[m], x[m])).astype(BF16) for m in each])
    d = updates
    for step in reversed(range(STEPS)):
        x, gram, poly = xs[step], grams[step], polys[step]
        sym = [dot_nt(d[m], x[m]) + dot_nt(x[m], d[m]) for m in each]
        low = [sym[m].astype(BF16) for m in each]
        turned = [dot_nn(low[m], gram[m]) + dot_nn(gram[m], low[m]) for m in each]
        da = [(CB * sym[m] + CC * turned[m]).astype(BF16) for m in each]
        d = [
            (CA * d[m].astype(F32) + dot_nn(poly[m], d[m]) + dot_nn(da[m], x[m])).astype(BF16)
            for m in each
        ]
    out = []
    for m in each:
        df = d[m].astype(F32)
        along = jnp.sum(df * grads[m], keepdims=True)
        out.append(df * inv[m] - grads[m] * (along * (inv[m] * inv[m] * inv[m])))
    return out


class Plan:
    def __init__(self, n, n_dp, tokens, heads, rows, width):
        self.n, self.n_dp = n, n_dp
        self.tokens, self.heads, self.rows, self.width = tokens, heads, rows, width
        self.per = -(-heads // n)
        self.mats = 3 * self.per
        least = max(1, self.per // 2)
        self.chunks = [(0, least), (least, self.per - least)]
        self.pair = min(2, n_dp)
        self.rest = n_dp // self.pair
        self.own = -(-self.mats // n_dp)
        self.block = -(-rows // 16) * 16
        self.group = min(4, n_dp)
        self.share = -(-self.mats // self.group)
        self.share_blocks = -(-self.share // least)

    def to(self, me, slot):
        return lax.rem(me[0] + slot, self.n)

    def source(self, me, slot):
        return lax.rem(me[0] + (self.n - slot), self.n)

    def head(self, me, slot):
        return jnp.minimum(self.to(me, slot) * self.per, self.heads - self.per)

    def mine(self, dp):
        return lax.rem(dp[0], self.pair)

    def member(self, dp):
        return lax.rem(dp[0], self.group)

    def other(self, dp, k):
        return jnp.bitwise_xor(lax.div(dp[0], self.pair), k)

    def packed_rows(self, chunk):
        return 4 * self.tokens + (3 + (self.share_blocks if chunk == 0 else 0)) * self.block

    def first_head(self, c):
        return min(c * self.per, self.heads - self.per)


def pack_kernel(me, dp, k_ref, v_ref, q_ref, o_ref, s_ref, t_ref, *refs, plan, slots, chunk):
    t, w = plan.tokens, plan.width
    first, count = plan.chunks[chunk]
    outs, (state, sems) = refs[:-2], refs[-2:]
    per = plan.per
    loads = []
    copies = []
    for k, slot in enumerate(slots):
        head = plan.head(me, slot)
        wanted = [(t_ref.at[0, :, pl.ds(head + first, count)], state.at[k, :, pl.ds(0, count)])]
        if chunk == 0:
            wanted.append((s_ref.at[:, pl.ds(head, per)], state.at[k, :, pl.ds(count, per)]))
        for i, (src, dst) in enumerate(wanted):
            loads.append(pltpu.make_async_copy(src, dst, sems.at[k, 4 + i]))
            loads[-1].start()
        cols = pl.ds(pl.multiple_of((head + first) * w, w), count * w)
        for i, src in enumerate((k_ref, v_ref, q_ref, o_ref)):
            copies.append(
                pltpu.make_async_copy(src.at[0, :, cols], outs[k].at[pl.ds(i * t, t), :], sems.at[k, i])
            )
            copies[-1].start()
    for load in loads:
        load.wait()
    for k in range(len(slots)):
        for j in range(count):
            for m in range(3):
                top = 4 * t + m * plan.block
                outs[k][top : top + plan.rows, j * w : (j + 1) * w] = state[k, m, j].astype(BF16)
        for q in range(plan.share if chunk == 0 else 0):
            mat = jnp.minimum(plan.member(dp) * plan.share + q, plan.mats - 1)
            top = 4 * t + (3 + q // count) * plan.block
            left = (q % count) * w
            part = state[k, lax.rem(mat, 3), count + lax.div(mat, 3)]
            outs[k][top : top + plan.rows, left : left + w] = part.astype(BF16)
    for copy in copies:
        copy.wait()


def start_kernel(me, *refs, plan):
    in_refs, (out, whole) = refs[: plan.n], refs[plan.n :]
    count, w = plan.chunks[0][1], plan.width
    for slot in range(plan.n):
        at = pl.ds(pl.multiple_of(plan.source(me, slot) * plan.rows, plan.rows), plan.rows)
        for q in range(plan.share):
            top = 4 * plan.tokens + (3 + q // count) * plan.block
            left = (q % count) * w
            whole[q, at, :] = in_refs[slot][top : top + plan.rows, left : left + w].astype(F32)
    out[...] = whole[...].astype(BF16)


def tokens_of(refs, j, group, plan):
    t, w = plan.tokens, plan.width
    cols = slice(j * w, (j + 1) * w)
    top = 2 * group * t
    x = jnp.concatenate([r[top : top + t, cols] for r in refs], axis=0)
    y = jnp.concatenate([r[top + t : top + 2 * t, cols] for r in refs], axis=0)
    return x, y


def forward(x, y, x_turned, y_turned, wa, wb, wc):
    w = wa.shape[1]
    gu = dot_nn(x, jnp.concatenate([wa, wb], axis=1))
    g, u = gu[:, :w], gu[:, w:]
    p = dot_nn(y, wc)
    s = 0.5 + 0.5 * jnp.tanh(0.5 * g)
    sw, slope, _ = swish_terms(g, s)
    hidden = (sw * u).astype(BF16)
    dg = (p * u * slope).astype(BF16)
    du = (p * sw).astype(BF16)
    ab = dot_nn(x_turned, jnp.concatenate([dg, du], axis=1))
    return (ab[:, :w], ab[:, w:], dot_nn(y_turned, hidden)), (g, u, p, s), (dg, du, hidden)


def chunk_kernel(me, dp, *refs, plan, chunk):
    n, t, w = plan.n, plan.tokens, plan.width
    first, count = plan.chunks[chunk]
    last = chunk + 1 == len(plan.chunks)
    mats = 3 * count
    refs = list(refs)

    def take(k):
        got = refs[:k]
        del refs[:k]
        return got

    in_refs = take(n)
    shares = take(plan.group)
    (before,) = take(1) if last else (None,)
    (d_ref,) = take(1)
    c_refs = take(2 if last else 1)
    w0, w1, gsum, ssum, acts, fields, flips = take(7)
    total = take(1)[0] if last else c_refs[0]
    base = 3 * first if last else 0

    for slot in range(n):
        at = pl.ds(pl.multiple_of(plan.source(me, slot) * plan.rows, plan.rows), plan.rows)
        for j in range(count):
            for m in range(3):
                top = 4 * t + m * plan.block
                part = in_refs[slot][top : top + plan.rows, j * w : (j + 1) * w]
                w1[3 * j + m, at, :] = part.astype(F32)
    for k, part in enumerate(shares):
        at = jnp.bitwise_xor(plan.member(dp), k) * plan.share
        w0[pl.ds(at, plan.share)] = part[...]

    for j in range(count):
        x, y = tokens_of(in_refs, j, 0, plan)
        flips[j, 0], flips[j, 1] = x.T, y.T
        sums, act, field = forward(x, y, flips[j, 0], flips[j, 1], *[w0[3 * (first + j) + m] for m in range(3)])
        for m in range(3):
            gsum[3 * j + m] = sums[m]
            fields[j, m] = field[m]
        for i, val in enumerate(act):
            acts[j, i] = val
        x, y = tokens_of(in_refs, j, 1, plan)
        sums, _, _ = forward(x, y, x.T, y.T, *[w1[3 * j + m].astype(BF16) for m in range(3)])
        for m in range(3):
            ssum[3 * j + m] = sums[m]

    grads = [gsum[m] for m in range(mats)]
    updates = [(RATE * ssum[m]).astype(BF16) for m in range(mats)]
    for m, val in enumerate(newton_pullback(grads, updates)):
        gsum[m] = val

    for j in range(count):
        x, y = tokens_of(in_refs, j, 0, plan)
        fab = jnp.concatenate([gsum[3 * j], gsum[3 * j + 1]], axis=1).astype(BF16)
        fc = gsum[3 * j + 2].astype(BF16)
        at = 3 * (first + j)
        wab = jnp.concatenate([w0[at], w0[at + 1]], axis=1)
        wc = w0[at + 2]
        cdgu = dot_nn(x, fab)
        cdg, cdu = cdgu[:, :w], cdgu[:, w:]
        ch = dot_nn(y, fc)
        g, u, p, s = [acts[j, i] for i in range(4)]
        sw, slope, curve = swish_terms(g, s)
        cg = ((ch * u + cdu * p) * slope + cdg * (p * u) * curve).astype(BF16)
        cu = (ch * sw + cdg * p * slope).astype(BF16)
        cp = (cdu * sw + cdg * u * slope).astype(BF16)
        dg, du, hidden = fields[j, 0], fields[j, 1], fields[j, 2]
        dx = dot_nt(jnp.concatenate([dg, du, cg, cu], axis=1), jnp.concatenate([fab, wab], axis=1))
        dy = dot_nt(jnp.concatenate([hidden, cp], axis=1), jnp.concatenate([fc, wc], axis=1))
        cols = slice(j * w, (j + 1) * w)
        for slot in range(n):
            to = plan.source(me, slot)
            d_ref[to, 0:t, cols] = dx[slot * t : (slot + 1) * t].astype(BF16)
            d_ref[to, t : 2 * t, cols] = dy[slot * t : (slot + 1) * t].astype(BF16)
        ab = dot_nn(flips[j, 0], jnp.concatenate([cg, cu], axis=1))
        grown = (ab[:, :w], ab[:, w:], dot_nn(flips[j, 1], cp))
        for m in range(3):
            total[base + 3 * j + m] = (ssum[3 * j + m] + grown[m]).astype(BF16)

    if last:
        total[0 : before.shape[0]] = before[...]
        for m in range(plan.mats, plan.n_dp * plan.own):
            total[m] = jnp.zeros((w, w), BF16)
        mine = plan.mine(dp)
        for r in range(plan.rest):
            to = slice(r * plan.own, (r + 1) * plan.own)
            for ref, which in zip(c_refs, (mine, plan.pair - 1 - mine)):
                ref[to] = total[pl.ds((plan.pair * r + which) * plan.own, plan.own)]


def pair_kernel(dp, keep_ref, got_ref, *refs, plan):
    outs, whole = refs[:-1], refs[-1]
    whole[...] = keep_ref[...].astype(F32) + got_ref[...].astype(F32)
    for k in range(plan.rest):
        outs[k][...] = whole[pl.ds(plan.other(dp, k) * plan.own, plan.own)].astype(BF16)


def sum_kernel(me, *refs, plan):
    parts, outs, whole = refs[: plan.rest], refs[plan.rest : -1], refs[-1]
    added = parts[0][...].astype(F32)
    for part in parts[1:]:
        added = added + part[...].astype(F32)
    whole[...] = added / plan.n_dp
    for slot in range(plan.n):
        at = pl.ds(pl.multiple_of(plan.to(me, slot) * plan.rows, plan.rows), plan.rows)
        outs[slot][...] = whole[:, at, :].astype(BF16)


def rows_kernel(me, *refs, plan):
    for slot, part in enumerate(refs[:-1]):
        refs[-1][plan.source(me, slot)] = part[...]


def rest_kernel(dp, *refs, plan):
    for k, part in enumerate(refs[:-1]):
        refs[-1][plan.other(dp, k)] = part[...]


def state_kernel(dp, *refs, plan):
    out = refs[-1]
    for k in range(plan.pair):
        for r in range(plan.rest):
            for i in range(plan.own):
                mat = (plan.pair * r + jnp.bitwise_xor(plan.mine(dp), k)) * plan.own + i

                @pl.when(mat < plan.mats)
                def _(mat=mat, ref=refs[k], r=r, i=i):
                    for c in range(plan.n):
                        head = plan.first_head(c) + lax.div(mat, 3)
                        out[lax.rem(mat, 3), head] = ref[r, c, i].astype(F32)


def unpack_kernel(*refs, plan):
    t, w = plan.tokens, plan.width
    ins, (dk, dv, sems) = refs[:-3], refs[-3:]
    copies = []
    for c, (first, count) in enumerate(plan.chunks):
        for owner in range(plan.n):
            cols = pl.ds((plan.first_head(owner) + first) * w, count * w)
            for part, dst in enumerate((dk, dv)):
                copy = pltpu.make_async_copy(
                    ins[c].at[owner, pl.ds(part * t, t), :],
                    dst.at[0, :, cols],
                    sems.at[(c * plan.n + owner) * 2 + part],
                )
                copy.start()
                copies.append(copy)
            if plan.n * plan.per != plan.heads:
                for copy in copies:
                    copy.wait()
                copies = []
    for copy in copies:
        copy.wait()


def local(keys_a, values_a, queries_b, grad_out, state_start, state_next):
    n, n_dp = lax.axis_size("ctx"), lax.axis_size("dp")
    _, heads, rows, width = state_start.shape
    t = keys_a.shape[1]
    plan = Plan(n, n_dp, t, heads, rows, width)
    per, own, chunks = plan.per, plan.own, plan.chunks
    bind = lambda kernel, **more: functools.partial(kernel, plan=plan, **more)

    me, dp = lax.axis_index("ctx").reshape(1), lax.axis_index("dp").reshape(1)

    def swap(value, k):
        if k == 0:
            return value
        return lax.ppermute(value, "dp", [(i, i ^ k) for i in range(n_dp)])

    def shift(value, s):
        if s == 0:
            return value
        return lax.ppermute(value, "ctx", [(i, (i + s) % n) for i in range(n)])

    def turn(value):
        return lax.all_to_all(value, "ctx", split_axis=0, concat_axis=0, tiled=True)

    def shape(*dims, dtype=BF16):
        return jax.ShapeDtypeStruct(dims, dtype)

    def pack(c, slots, keys):
        args = (keys, values_a, queries_b, grad_out, state_start, state_next)
        outs = call(
            bind(pack_kernel, slots=slots, chunk=c),
            [shape(plan.packed_rows(c), chunks[c][1] * width)] * len(slots),
            (me, dp, *[pltpu.with_memory_space_constraint(arg, pltpu.HBM) for arg in args]),
            [SMEM] * 2 + [HBM] * 6,
            [VMEM] * len(slots),
            f"pack{c}_{slots[0]}",
            [
                pltpu.VMEM((len(slots), 3, chunks[c][1] + (0 if c else per), rows, width), F32),
                pltpu.SemaphoreType.DMA((len(slots), 6)),
            ],
        )
        return list(outs)

    sent = pack(0, range(1, n), keys_a)
    keys, sent = lax.optimization_barrier((keys_a, sent))
    arrived = [[shift(v, s + 1) for s, v in enumerate(sent)]]
    sent = pack(1, range(1, n), keys)
    keys, sent = lax.optimization_barrier((keys_a, sent))
    arrived.append([shift(v, s + 1) for s, v in enumerate(sent)])
    arrived = [pack(c, range(1), keys) + arrived[c] for c in range(2)]
    start_own = call(
        bind(start_kernel),
        shape(plan.share, width, width),
        (me, *arrived[0]),
        [SMEM] + [VMEM] * n,
        VMEM,
        "start_share",
        [pltpu.VMEM((plan.share, width, width), F32)],
    )
    shares = [swap(start_own, k) for k in range(plan.group)]

    before = []
    grads = []
    for c, (_, count) in enumerate(chunks):
        last = c + 1 == len(chunks)
        if last:
            outs = [shape(plan.rest * own, width, width)] * 2
        else:
            outs = [shape(3 * count, width, width)]
        outs = [shape(n, 2 * t, count * width)] + outs
        scratch = [pltpu.VMEM((plan.group * plan.share, width, width), BF16)]
        scratch += [pltpu.VMEM((3 * count, width, width), F32)] * 3 + [
            pltpu.VMEM((count, 4, n * t, width), F32),
            pltpu.VMEM((count, 3, n * t, width), BF16),
            pltpu.VMEM((count, 2, width, n * t), BF16),
        ]
        if last:
            scratch.append(pltpu.VMEM((n_dp * own, width, width), BF16))
        got = call(
            bind(chunk_kernel, chunk=c),
            outs,
            (me, dp, *arrived[c], *shares, *before),
            [SMEM] * 2 + [VMEM] * (n + plan.group + len(before)),
            [VMEM] * len(outs),
            f"chunk{c}",
            scratch,
            flops=count * 640 * 10**6,
            size=count * 10**6,
            vmem=VMEM_LARGE,
        )
        grads.append(got[0])
        before = [got[1]]
    late, early = grads
    c_keep, c_send = got[1:]
    early, c_send = lax.optimization_barrier((early, c_send))
    early = turn(early)

    halves = call(
        bind(pair_kernel),
        [shape(own, width, width)] * plan.rest,
        (dp, c_keep, swap(c_send, plan.pair - 1)),
        [SMEM] + [VMEM] * 2,
        [VMEM] * plan.rest,
        "state_pair",
        [pltpu.VMEM((plan.rest * own, width, width), F32)],
    )
    halves = [swap(halves[k], plan.pair * k) for k in range(plan.rest)]
    by_rows = call(
        bind(sum_kernel),
        [shape(own, rows, width)] * n,
        (me, *halves),
        [SMEM] + [VMEM] * plan.rest,
        [VMEM] * n,
        "state_sum",
        [pltpu.VMEM((own, width, width), F32)],
    )
    by_rows = [shift(by_rows[s], s) for s in range(n)]
    by_rows[0], early = lax.optimization_barrier((by_rows[0], early))
    mine = call(
        bind(rows_kernel),
        shape(n, own, rows, width),
        (me, *by_rows),
        [SMEM] + [VMEM] * n,
        VMEM,
        "state_rows",
    )
    mine, late = lax.optimization_barrier((mine, late))
    late = turn(late)
    rest = [swap(mine, plan.pair * k) for k in range(plan.rest)]
    half = call(
        bind(rest_kernel),
        shape(plan.rest, n, own, rows, width),
        (dp, *rest),
        [SMEM] + [VMEM] * plan.rest,
        VMEM,
        "state_rest",
    )
    both = [swap(half, k) for k in range(plan.pair)]
    grad_state = call(
        bind(state_kernel),
        shape(*state_start.shape, dtype=F32),
        (dp, *both),
        [SMEM] + [VMEM] * plan.pair,
        VMEM,
        "state_out",
    )
    grad_keys, grad_values = call(
        bind(unpack_kernel),
        [shape(*keys_a.shape), shape(*values_a.shape)],
        (late, early),
        [VMEM] * 2,
        [ANY] * 2,
        "unpack",
        [pltpu.SemaphoreType.DMA((4 * n,))],
    )
    return grad_keys, grad_values, grad_state


def solution(mesh):
    placed = (
        P("dp", "ctx", None),
        P("dp", "ctx", None),
        P("dp", "ctx", None),
        P("dp", "ctx", None),
        P(None, None, "ctx", None),
        P("dp", None, None, "ctx", None),
    )
    return jax.shard_map(
        local,
        mesh=mesh,
        in_specs=placed,
        out_specs=(P("dp", "ctx", None), P("dp", "ctx", None), P(None, None, "ctx", None)),
        check_vma=False,
    )
```

```python
import functools

import jax
import jax.numpy as jnp
from jax import lax
from jax.experimental import pallas as pl
from jax.experimental.pallas import tpu as pltpu
from jax.sharding import PartitionSpec as P

RATE = 4.0
CA = 3.4445
CB = -4.775
CC = 2.0315
STEPS = 2
F32 = jnp.float32
BF16 = jnp.bfloat16
VMEM_SMALL = 8 * 1024 * 1024
VMEM_LARGE = 28 * 1024 * 1024
SMEM = pl.BlockSpec(memory_space=pltpu.SMEM)
VMEM = pl.BlockSpec(memory_space=pltpu.VMEM)
ANY = pl.BlockSpec(memory_space=pl.ANY)
HBM = pl.BlockSpec(memory_space=pltpu.HBM)


def dot_nn(a, b):
    return lax.dot_general(a, b, (((1,), (0,)), ((), ())), preferred_element_type=F32)


def dot_nt(a, b):
    return lax.dot_general(a, b, (((1,), (1,)), ((), ())), preferred_element_type=F32)


def call(
    kernel, out_shape, args, in_specs, out_specs, name, scratch=(), flops=10**6, size=10**6, vmem=VMEM_SMALL
):
    return pl.pallas_call(
        kernel,
        out_shape=out_shape,
        in_specs=in_specs,
        out_specs=out_specs,
        scratch_shapes=list(scratch),
        compiler_params=pltpu.CompilerParams(vmem_limit_bytes=vmem),
        cost_estimate=pl.CostEstimate(flops=flops, bytes_accessed=size, transcendentals=0),
        name=name,
    )(*args)


def swish_terms(g, s):
    rest = 1.0 - s
    both = s * rest
    bent = g * both
    return g * s, s + bent, 2.0 * both + bent * (rest - s)


def newton_forward(grads, kept):
    each = range(len(grads))
    inv = [lax.rsqrt(jnp.sum(g * g, keepdims=True) + 1e-06) for g in grads]
    x = [(grads[m] * inv[m]).astype(BF16) for m in each]
    for step in range(STEPS):
        gram = [dot_nt(x[m], x[m]).astype(BF16) for m in each]
        yield
        poly = [(CB * gram[m].astype(F32) + CC * dot_nn(gram[m], gram[m])).astype(BF16) for m in each]
        kept.append((x, gram, poly))
        if step + 1 < STEPS:
            yield
            x = [(CA * x[m].astype(F32) + dot_nn(poly[m], x[m])).astype(BF16) for m in each]
            yield


def newton_pullback(grads, kept, updates):
    each = range(len(grads))
    inv = [lax.rsqrt(jnp.sum(g * g, keepdims=True) + 1e-06) for g in grads]
    d = updates
    for x, gram, poly in reversed(kept):
        sym = [dot_nt(d[m], x[m]) + dot_nt(x[m], d[m]) for m in each]
        low = [sym[m].astype(BF16) for m in each]
        turned = [dot_nn(low[m], gram[m]) + dot_nn(gram[m], low[m]) for m in each]
        da = [(CB * sym[m] + CC * turned[m]).astype(BF16) for m in each]
        d = [
            (CA * d[m].astype(F32) + dot_nn(poly[m], d[m]) + dot_nn(da[m], x[m])).astype(BF16)
            for m in each
        ]
    out = []
    for m in each:
        df = d[m].astype(F32)
        along = jnp.sum(df * grads[m], keepdims=True)
        out.append(df * inv[m] - grads[m] * (along * (inv[m] * inv[m] * inv[m])))
    return out


class Plan:
    def __init__(self, n, n_dp, tokens, heads, rows, width):
        self.n, self.n_dp = n, n_dp
        self.tokens, self.heads, self.rows, self.width = tokens, heads, rows, width
        self.per = -(-heads // n)
        self.mats = 3 * self.per
        least = max(1, self.per // 2)
        self.chunks = [(0, least), (least, self.per - least)]
        self.pair = min(2, n_dp)
        self.rest = n_dp // self.pair
        self.own = -(-self.mats // n_dp)
        self.block = -(-rows // 16) * 16
        self.group = min(4, n_dp)
        self.share = -(-self.mats // self.group)
        self.share_blocks = -(-self.share // least)

    def to(self, me, slot):
        return lax.rem(me[0] + slot, self.n)

    def source(self, me, slot):
        return lax.rem(me[0] + (self.n - slot), self.n)

    def head(self, me, slot):
        return jnp.minimum(self.to(me, slot) * self.per, self.heads - self.per)

    def mine(self, dp):
        return lax.rem(dp[0], self.pair)

    def member(self, dp):
        return lax.rem(dp[0], self.group)

    def other(self, dp, k):
        return jnp.bitwise_xor(lax.div(dp[0], self.pair), k)

    def packed_rows(self, chunk):
        return 4 * self.tokens + (3 + (self.share_blocks if chunk == 0 else 0)) * self.block

    def first_head(self, c):
        return min(c * self.per, self.heads - self.per)


def pack_kernel(me, dp, k_ref, v_ref, q_ref, o_ref, s_ref, t_ref, *refs, plan, slots, chunk):
    t, w = plan.tokens, plan.width
    first, count = plan.chunks[chunk]
    outs, (state, sems) = refs[:-2], refs[-2:]
    per = plan.per
    loads = []
    copies = []
    for k, slot in enumerate(slots):
        head = plan.head(me, slot)
        wanted = [(t_ref.at[0, :, pl.ds(head + first, count)], state.at[k, :, pl.ds(0, count)])]
        if chunk == 0:
            wanted.append((s_ref.at[:, pl.ds(head, per)], state.at[k, :, pl.ds(count, per)]))
        for i, (src, dst) in enumerate(wanted):
            loads.append(pltpu.make_async_copy(src, dst, sems.at[k, 4 + i]))
            loads[-1].start()
        cols = pl.ds(pl.multiple_of((head + first) * w, w), count * w)
        for i, src in enumerate((k_ref, v_ref, q_ref, o_ref)):
            copies.append(
                pltpu.make_async_copy(src.at[0, :, cols], outs[k].at[pl.ds(i * t, t), :], sems.at[k, i])
            )
            copies[-1].start()
    for load in loads:
        load.wait()
    for k in range(len(slots)):
        for j in range(count):
            for m in range(3):
                top = 4 * t + m * plan.block
                outs[k][top : top + plan.rows, j * w : (j + 1) * w] = state[k, m, j].astype(BF16)
        for q in range(plan.share if chunk == 0 else 0):
            mat = jnp.minimum(plan.member(dp) * plan.share + q, plan.mats - 1)
            top = 4 * t + (3 + q // count) * plan.block
            left = (q % count) * w
            part = state[k, lax.rem(mat, 3), count + lax.div(mat, 3)]
            outs[k][top : top + plan.rows, left : left + w] = part.astype(BF16)
    for copy in copies:
        copy.wait()


def start_kernel(me, *refs, plan):
    in_refs, (out, whole) = refs[: plan.n], refs[plan.n :]
    count, w = plan.chunks[0][1], plan.width
    for slot in range(plan.n):
        at = pl.ds(pl.multiple_of(plan.source(me, slot) * plan.rows, plan.rows), plan.rows)
        for q in range(plan.share):
            top = 4 * plan.tokens + (3 + q // count) * plan.block
            left = (q % count) * w
            whole[q, at, :] = in_refs[slot][top : top + plan.rows, left : left + w].astype(F32)
    out[...] = whole[...].astype(BF16)


def tokens_of(refs, j, group, plan):
    t, w = plan.tokens, plan.width
    cols = slice(j * w, (j + 1) * w)
    top = 2 * group * t
    x = jnp.concatenate([r[top : top + t, cols] for r in refs], axis=0)
    y = jnp.concatenate([r[top + t : top + 2 * t, cols] for r in refs], axis=0)
    return x, y


def forward(x, y, x_turned, y_turned, wa, wb, wc):
    w = wa.shape[1]
    gu = dot_nn(x, jnp.concatenate([wa, wb], axis=1))
    g, u = gu[:, :w], gu[:, w:]
    p = dot_nn(y, wc)
    s = 0.5 + 0.5 * jnp.tanh(0.5 * g)
    sw, slope, _ = swish_terms(g, s)
    hidden = (sw * u).astype(BF16)
    dg = (p * u * slope).astype(BF16)
    du = (p * sw).astype(BF16)
    ab = dot_nn(x_turned, jnp.concatenate([dg, du], axis=1))
    return (ab[:, :w], ab[:, w:], dot_nn(y_turned, hidden)), (g, u, p, s), (dg, du, hidden)


def chunk_kernel(me, dp, *refs, plan, chunk):
    n, t, w = plan.n, plan.tokens, plan.width
    first, count = plan.chunks[chunk]
    last = chunk + 1 == len(plan.chunks)
    mats = 3 * count
    refs = list(refs)

    def take(k):
        got = refs[:k]
        del refs[:k]
        return got

    in_refs = take(n)
    shares = take(plan.group)
    (before,) = take(1) if last else (None,)
    (d_ref,) = take(1)
    c_refs = take(2 if last else 1)
    w0, w1, gsum, ssum, acts, fields, flips = take(7)
    total = take(1)[0] if last else c_refs[0]
    base = 3 * first if last else 0

    for slot in range(n):
        at = pl.ds(pl.multiple_of(plan.source(me, slot) * plan.rows, plan.rows), plan.rows)
        for j in range(count):
            for m in range(3):
                top = 4 * t + m * plan.block
                part = in_refs[slot][top : top + plan.rows, j * w : (j + 1) * w]
                w1[3 * j + m, at, :] = part.astype(F32)
    for k, part in enumerate(shares):
        at = jnp.bitwise_xor(plan.member(dp), k) * plan.share
        w0[pl.ds(at, plan.share)] = part[...]

    for j in range(count):
        x, y = tokens_of(in_refs, j, 0, plan)
        flips[j, 0], flips[j, 1] = x.T, y.T
        sums, act, field = forward(x, y, flips[j, 0], flips[j, 1], *[w0[3 * (first + j) + m] for m in range(3)])
        for m in range(3):
            gsum[3 * j + m] = sums[m]
            fields[j, m] = field[m]
        for i, val in enumerate(act):
            acts[j, i] = val

    grads = [gsum[m] for m in range(mats)]
    kept = []
    steps = newton_forward(grads, kept)
    for j in range(count):
        next(steps, None)
        x, y = tokens_of(in_refs, j, 1, plan)
        sums, _, _ = forward(x, y, x.T, y.T, *[w1[3 * j + m].astype(BF16) for m in range(3)])
        next(steps, None)
        for m in range(3):
            ssum[3 * j + m] = sums[m]
    for _ in steps:
        pass

    updates = [(RATE * ssum[m]).astype(BF16) for m in range(mats)]
    for m, val in enumerate(newton_pullback(grads, kept, updates)):
        gsum[m] = val

    for j in range(count):
        x, y = tokens_of(in_refs, j, 0, plan)
        fab = jnp.concatenate([gsum[3 * j], gsum[3 * j + 1]], axis=1).astype(BF16)
        fc = gsum[3 * j + 2].astype(BF16)
        at = 3 * (first + j)
        wab = jnp.concatenate([w0[at], w0[at + 1]], axis=1)
        wc = w0[at + 2]
        cdgu = dot_nn(x, fab)
        cdg, cdu = cdgu[:, :w], cdgu[:, w:]
        ch = dot_nn(y, fc)
        g, u, p, s = [acts[j, i] for i in range(4)]
        sw, slope, curve = swish_terms(g, s)
        cg = ((ch * u + cdu * p) * slope + cdg * (p * u) * curve).astype(BF16)
        cu = (ch * sw + cdg * p * slope).astype(BF16)
        cp = (cdu * sw + cdg * u * slope).astype(BF16)
        dg, du, hidden = fields[j, 0], fields[j, 1], fields[j, 2]
        dx = dot_nt(jnp.concatenate([dg, du, cg, cu], axis=1), jnp.concatenate([fab, wab], axis=1))
        dy = dot_nt(jnp.concatenate([hidden, cp], axis=1), jnp.concatenate([fc, wc], axis=1))
        cols = slice(j * w, (j + 1) * w)
        for slot in range(n):
            to = plan.source(me, slot)
            d_ref[to, 0:t, cols] = dx[slot * t : (slot + 1) * t].astype(BF16)
            d_ref[to, t : 2 * t, cols] = dy[slot * t : (slot + 1) * t].astype(BF16)
        ab = dot_nn(flips[j, 0], jnp.concatenate([cg, cu], axis=1))
        grown = (ab[:, :w], ab[:, w:], dot_nn(flips[j, 1], cp))
        for m in range(3):
            total[base + 3 * j + m] = (ssum[3 * j + m] + grown[m]).astype(BF16)

    if last:
        total[0 : before.shape[0]] = before[...]
        for m in range(plan.mats, plan.n_dp * plan.own):
            total[m] = jnp.zeros((w, w), BF16)
        mine = plan.mine(dp)
        for r in range(plan.rest):
            to = slice(r * plan.own, (r + 1) * plan.own)
            for ref, which in zip(c_refs, (mine, plan.pair - 1 - mine)):
                ref[to] = total[pl.ds((plan.pair * r + which) * plan.own, plan.own)]


def pair_kernel(dp, keep_ref, got_ref, *refs, plan):
    outs, whole = refs[:-1], refs[-1]
    whole[...] = keep_ref[...].astype(F32) + got_ref[...].astype(F32)
    for k in range(plan.rest):
        outs[k][...] = whole[pl.ds(plan.other(dp, k) * plan.own, plan.own)].astype(BF16)


def sum_kernel(me, *refs, plan):
    parts, outs, whole = refs[: plan.rest], refs[plan.rest : -1], refs[-1]
    added = parts[0][...].astype(F32)
    for part in parts[1:]:
        added = added + part[...].astype(F32)
    whole[...] = added / plan.n_dp
    for slot in range(plan.n):
        at = pl.ds(pl.multiple_of(plan.to(me, slot) * plan.rows, plan.rows), plan.rows)
        outs[slot][...] = whole[:, at, :].astype(BF16)


def rows_kernel(me, *refs, plan):
    for slot, part in enumerate(refs[:-1]):
        refs[-1][plan.source(me, slot)] = part[...]


def rest_kernel(dp, *refs, plan):
    for k, part in enumerate(refs[:-1]):
        refs[-1][plan.other(dp, k)] = part[...]


def state_kernel(dp, *refs, plan):
    out = refs[-1]
    for k in range(plan.pair):
        for r in range(plan.rest):
            for i in range(plan.own):
                mat = (plan.pair * r + jnp.bitwise_xor(plan.mine(dp), k)) * plan.own + i

                @pl.when(mat < plan.mats)
                def _(mat=mat, ref=refs[k], r=r, i=i):
                    for c in range(plan.n):
                        head = plan.first_head(c) + lax.div(mat, 3)
                        out[lax.rem(mat, 3), head] = ref[r, c, i].astype(F32)


def unpack_kernel(*refs, plan):
    t, w = plan.tokens, plan.width
    ins, (dk, dv, sems) = refs[:-3], refs[-3:]
    copies = []
    for c, (first, count) in enumerate(plan.chunks):
        for owner in range(plan.n):
            cols = pl.ds((plan.first_head(owner) + first) * w, count * w)
            for part, dst in enumerate((dk, dv)):
                copy = pltpu.make_async_copy(
                    ins[c].at[owner, pl.ds(part * t, t), :],
                    dst.at[0, :, cols],
                    sems.at[(c * plan.n + owner) * 2 + part],
                )
                copy.start()
                copies.append(copy)
            if plan.n * plan.per != plan.heads:
                for copy in copies:
                    copy.wait()
                copies = []
    for copy in copies:
        copy.wait()


def local(keys_a, values_a, queries_b, grad_out, state_start, state_next):
    n, n_dp = lax.axis_size("ctx"), lax.axis_size("dp")
    _, heads, rows, width = state_start.shape
    t = keys_a.shape[1]
    plan = Plan(n, n_dp, t, heads, rows, width)
    per, own, chunks = plan.per, plan.own, plan.chunks
    bind = lambda kernel, **more: functools.partial(kernel, plan=plan, **more)

    me, dp = lax.axis_index("ctx").reshape(1), lax.axis_index("dp").reshape(1)

    def swap(value, k):
        if k == 0:
            return value
        return lax.ppermute(value, "dp", [(i, i ^ k) for i in range(n_dp)])

    def shift(value, s):
        if s == 0:
            return value
        return lax.ppermute(value, "ctx", [(i, (i + s) % n) for i in range(n)])

    def turn(value):
        return lax.all_to_all(value, "ctx", split_axis=0, concat_axis=0, tiled=True)

    def shape(*dims, dtype=BF16):
        return jax.ShapeDtypeStruct(dims, dtype)

    def pack(c, slots, keys):
        args = (keys, values_a, queries_b, grad_out, state_start, state_next)
        outs = call(
            bind(pack_kernel, slots=slots, chunk=c),
            [shape(plan.packed_rows(c), chunks[c][1] * width)] * len(slots),
            (me, dp, *[pltpu.with_memory_space_constraint(arg, pltpu.HBM) for arg in args]),
            [SMEM] * 2 + [HBM] * 6,
            [VMEM] * len(slots),
            f"pack{c}_{slots[0]}",
            [
                pltpu.VMEM((len(slots), 3, chunks[c][1] + (0 if c else per), rows, width), F32),
                pltpu.SemaphoreType.DMA((len(slots), 6)),
            ],
        )
        return list(outs)

    sent = pack(0, range(1, n), keys_a)
    keys, sent = lax.optimization_barrier((keys_a, sent))
    arrived = [[shift(v, s + 1) for s, v in enumerate(sent)]]
    sent = pack(1, range(1, n), keys)
    keys, sent = lax.optimization_barrier((keys_a, sent))
    arrived.append([shift(v, s + 1) for s, v in enumerate(sent)])
    arrived = [pack(c, range(1), keys) + arrived[c] for c in range(2)]
    start_own = call(
        bind(start_kernel),
        shape(plan.share, width, width),
        (me, *arrived[0]),
        [SMEM] + [VMEM] * n,
        VMEM,
        "start_share",
        [pltpu.VMEM((plan.share, width, width), F32)],
    )
    shares = [swap(start_own, k) for k in range(plan.group)]

    before = []
    grads = []
    for c, (_, count) in enumerate(chunks):
        last = c + 1 == len(chunks)
        if last:
            outs = [shape(plan.rest * own, width, width)] * 2
        else:
            outs = [shape(3 * count, width, width)]
        outs = [shape(n, 2 * t, count * width)] + outs
        scratch = [pltpu.VMEM((plan.group * plan.share, width, width), BF16)]
        scratch += [pltpu.VMEM((3 * count, width, width), F32)] * 3 + [
            pltpu.VMEM((count, 4, n * t, width), F32),
            pltpu.VMEM((count, 3, n * t, width), BF16),
            pltpu.VMEM((count, 2, width, n * t), BF16),
        ]
        if last:
            scratch.append(pltpu.VMEM((n_dp * own, width, width), BF16))
        got = call(
            bind(chunk_kernel, chunk=c),
            outs,
            (me, dp, *arrived[c], *shares, *before),
            [SMEM] * 2 + [VMEM] * (n + plan.group + len(before)),
            [VMEM] * len(outs),
            f"chunk{c}",
            scratch,
            flops=count * 640 * 10**6,
            size=count * 10**6,
            vmem=VMEM_LARGE,
        )
        grads.append(got[0])
        before = [got[1]]
    late, early = grads
    c_keep, c_send = got[1:]
    early, c_send = lax.optimization_barrier((early, c_send))
    early = turn(early)

    halves = call(
        bind(pair_kernel),
        [shape(own, width, width)] * plan.rest,
        (dp, c_keep, swap(c_send, plan.pair - 1)),
        [SMEM] + [VMEM] * 2,
        [VMEM] * plan.rest,
        "state_pair",
        [pltpu.VMEM((plan.rest * own, width, width), F32)],
    )
    halves = [swap(halves[k], plan.pair * k) for k in range(plan.rest)]
    by_rows = call(
        bind(sum_kernel),
        [shape(own, rows, width)] * n,
        (me, *halves),
        [SMEM] + [VMEM] * plan.rest,
        [VMEM] * n,
        "state_sum",
        [pltpu.VMEM((own, width, width), F32)],
    )
    by_rows = [shift(by_rows[s], s) for s in range(n)]
    by_rows[0], early = lax.optimization_barrier((by_rows[0], early))
    mine = call(
        bind(rows_kernel),
        shape(n, own, rows, width),
        (me, *by_rows),
        [SMEM] + [VMEM] * n,
        VMEM,
        "state_rows",
    )
    mine, late = lax.optimization_barrier((mine, late))
    late = turn(late)
    rest = [swap(mine, plan.pair * k) for k in range(plan.rest)]
    half = call(
        bind(rest_kernel),
        shape(plan.rest, n, own, rows, width),
        (dp, *rest),
        [SMEM] + [VMEM] * plan.rest,
        VMEM,
        "state_rest",
    )
    both = [swap(half, k) for k in range(plan.pair)]
    grad_state = call(
        bind(state_kernel),
        shape(*state_start.shape, dtype=F32),
        (dp, *both),
        [SMEM] + [VMEM] * plan.pair,
        VMEM,
        "state_out",
    )
    grad_keys, grad_values = call(
        bind(unpack_kernel),
        [shape(*keys_a.shape), shape(*values_a.shape)],
        (late, early),
        [VMEM] * 2,
        [ANY] * 2,
        "unpack",
        [pltpu.SemaphoreType.DMA((4 * n,))],
    )
    return grad_keys, grad_values, grad_state


def solution(mesh):
    placed = (
        P("dp", "ctx", None),
        P("dp", "ctx", None),
        P("dp", "ctx", None),
        P("dp", "ctx", None),
        P(None, None, "ctx", None),
        P("dp", None, None, "ctx", None),
    )
    return jax.shard_map(
        local,
        mesh=mesh,
        in_specs=placed,
        out_specs=(P("dp", "ctx", None), P("dp", "ctx", None), P(None, None, "ctx", None)),
        check_vma=False,
    )
```

```python
import functools

import jax
import jax.numpy as jnp
from jax import lax
from jax.experimental import pallas as pl
from jax.experimental.pallas import tpu as pltpu
from jax.sharding import PartitionSpec as P

RATE = 4.0
CA = 3.4445
CB = -4.775
CC = 2.0315
STEPS = 2
F32 = jnp.float32
BF16 = jnp.bfloat16
VMEM_SMALL = 8 * 1024 * 1024
VMEM_LARGE = 28 * 1024 * 1024
SMEM = pl.BlockSpec(memory_space=pltpu.SMEM)
VMEM = pl.BlockSpec(memory_space=pltpu.VMEM)
ANY = pl.BlockSpec(memory_space=pl.ANY)
HBM = pl.BlockSpec(memory_space=pltpu.HBM)


def dot_nn(a, b):
    return lax.dot_general(a, b, (((1,), (0,)), ((), ())), preferred_element_type=F32)


def dot_nt(a, b):
    return lax.dot_general(a, b, (((1,), (1,)), ((), ())), preferred_element_type=F32)


def dot_tn(a, b):
    return lax.dot_general(a, b, (((0,), (0,)), ((), ())), preferred_element_type=F32)


def call(
    kernel, out_shape, args, in_specs, out_specs, name, scratch=(), flops=10**6, size=10**6, vmem=VMEM_SMALL
):
    return pl.pallas_call(
        kernel,
        out_shape=out_shape,
        in_specs=in_specs,
        out_specs=out_specs,
        scratch_shapes=list(scratch),
        compiler_params=pltpu.CompilerParams(vmem_limit_bytes=vmem),
        cost_estimate=pl.CostEstimate(flops=flops, bytes_accessed=size, transcendentals=0),
        name=name,
    )(*args)


def swish_terms(g, s):
    rest = 1.0 - s
    both = s * rest
    bent = g * both
    return g * s, s + bent, 2.0 * both + bent * (rest - s)


def newton_pullback(grads, updates):
    each = range(len(grads))
    inv = [lax.rsqrt(jnp.sum(g * g, keepdims=True) + 1e-06) for g in grads]
    xs = [[(grads[m] * inv[m]).astype(BF16) for m in each]]
    grams = []
    polys = []
    for step in range(STEPS):
        x = xs[-1]
        gram = [dot_nt(x[m], x[m]).astype(BF16) for m in each]
        poly = [(CB * gram[m].astype(F32) + CC * dot_nn(gram[m], gram[m])).astype(BF16) for m in each]
        grams.append(gram)
        polys.append(poly)
        if step + 1 < STEPS:
            xs.append([(CA * x[m].astype(F32) + dot_nn(poly[m], x[m])).astype(BF16) for m in each])
    d = updates
    for step in reversed(range(STEPS)):
        x, gram, poly = xs[step], grams[step], polys[step]
        dp = [dot_nt(d[m], x[m]) for m in each]
        sym = [dp[m] + dp[m].T for m in each]
        turned = [dot_nn(sym[m].astype(BF16), gram[m]) for m in each]
        da = [(CB * sym[m] + CC * (turned[m] + turned[m].T)).astype(BF16) for m in each]
        d = [
            (CA * d[m].astype(F32) + dot_nn(poly[m], d[m]) + dot_nn(da[m], x[m])).astype(BF16)
            for m in each
        ]
    out = []
    for m in each:
        df = d[m].astype(F32)
        along = jnp.sum(df * grads[m], keepdims=True)
        out.append(df * inv[m] - grads[m] * (along * (inv[m] * inv[m] * inv[m])))
    return out


class Plan:
    def __init__(self, n, n_dp, tokens, heads, rows, width):
        self.n, self.n_dp = n, n_dp
        self.tokens, self.heads, self.rows, self.width = tokens, heads, rows, width
        self.per = -(-heads // n)
        self.mats = 3 * self.per
        least = max(1, self.per // 2)
        self.chunks = [(0, least), (least, self.per - least)]
        self.pair = min(2, n_dp)
        self.rest = n_dp // self.pair
        self.own = -(-self.mats // n_dp)
        self.block = -(-rows // 16) * 16
        self.group = min(8, n_dp)
        self.share = -(-self.mats // self.group)
        self.share_blocks = -(-self.share // least)

    def to(self, me, slot):
        return lax.rem(me[0] + slot, self.n)

    def source(self, me, slot):
        return lax.rem(me[0] + (self.n - slot), self.n)

    def head(self, me, slot):
        return jnp.minimum(self.to(me, slot) * self.per, self.heads - self.per)

    def mine(self, dp):
        return lax.rem(dp[0], self.pair)

    def member(self, dp):
        return lax.rem(dp[0], self.group)

    def other(self, dp, k):
        return jnp.bitwise_xor(lax.div(dp[0], self.pair), k)

    def packed_rows(self, chunk):
        return 4 * self.tokens + (3 + (self.share_blocks if chunk == 0 else 0)) * self.block

    def first_head(self, c):
        return min(c * self.per, self.heads - self.per)


def pack_kernel(me, dp, k_ref, v_ref, q_ref, o_ref, s_ref, t_ref, *refs, plan, slots, chunk):
    t, w = plan.tokens, plan.width
    first, count = plan.chunks[chunk]
    outs, (state, sems) = refs[:-2], refs[-2:]
    per = plan.per
    loads = []
    copies = []
    for k, slot in enumerate(slots):
        head = plan.head(me, slot)
        wanted = [(t_ref.at[0, :, pl.ds(head + first, count)], state.at[k, :, pl.ds(0, count)])]
        if chunk == 0:
            wanted.append((s_ref.at[:, pl.ds(head, per)], state.at[k, :, pl.ds(count, per)]))
        for i, (src, dst) in enumerate(wanted):
            loads.append(pltpu.make_async_copy(src, dst, sems.at[k, 4 + i]))
            loads[-1].start()
        cols = pl.ds(pl.multiple_of((head + first) * w, w), count * w)
        for i, src in enumerate((k_ref, v_ref, q_ref, o_ref)):
            copies.append(
                pltpu.make_async_copy(src.at[0, :, cols], outs[k].at[pl.ds(i * t, t), :], sems.at[k, i])
            )
            copies[-1].start()
    for load in loads:
        load.wait()
    for k in range(len(slots)):
        for j in range(count):
            for m in range(3):
                top = 4 * t + m * plan.block
                outs[k][top : top + plan.rows, j * w : (j + 1) * w] = state[k, m, j].astype(BF16)
        for q in range(plan.share if chunk == 0 else 0):
            mat = jnp.minimum(plan.member(dp) * plan.share + q, plan.mats - 1)
            top = 4 * t + (3 + q // count) * plan.block
            left = (q % count) * w
            part = state[k, lax.rem(mat, 3), count + lax.div(mat, 3)]
            outs[k][top : top + plan.rows, left : left + w] = part.astype(BF16)
    for copy in copies:
        copy.wait()


def start_kernel(me, *refs, plan):
    in_refs, (out, whole) = refs[: plan.n], refs[plan.n :]
    count, w = plan.chunks[0][1], plan.width
    for slot in range(plan.n):
        at = pl.ds(pl.multiple_of(plan.source(me, slot) * plan.rows, plan.rows), plan.rows)
        for q in range(plan.share):
            top = 4 * plan.tokens + (3 + q // count) * plan.block
            left = (q % count) * w
            whole[q, at, :] = in_refs[slot][top : top + plan.rows, left : left + w].astype(F32)
    out[...] = whole[...].astype(BF16)


def tokens_of(refs, j, group, plan):
    t, w = plan.tokens, plan.width
    cols = slice(j * w, (j + 1) * w)
    top = 2 * group * t
    x = jnp.concatenate([r[top : top + t, cols] for r in refs], axis=0)
    y = jnp.concatenate([r[top + t : top + 2 * t, cols] for r in refs], axis=0)
    return x, y


def forward(x, y, wa, wb, wc):
    w = wa.shape[1]
    gu = dot_nn(x, jnp.concatenate([wa, wb], axis=1))
    g, u = gu[:, :w], gu[:, w:]
    p = dot_nn(y, wc)
    s = 0.5 + 0.5 * jnp.tanh(0.5 * g)
    sw, slope, _ = swish_terms(g, s)
    hidden = (sw * u).astype(BF16)
    dg = (p * u * slope).astype(BF16)
    du = (p * sw).astype(BF16)
    ab = dot_tn(x, jnp.concatenate([dg, du], axis=1))
    return (ab[:, :w], ab[:, w:], dot_tn(y, hidden)), (g, u, p, s), (dg, du, hidden)


def chunk_kernel(me, dp, *refs, plan, chunk):
    n, t, w = plan.n, plan.tokens, plan.width
    first, count = plan.chunks[chunk]
    last = chunk + 1 == len(plan.chunks)
    mats = 3 * count
    refs = list(refs)

    def take(k):
        got = refs[:k]
        del refs[:k]
        return got

    in_refs = take(n)
    shares = take(plan.group)
    (before,) = take(1) if last else (None,)
    (d_ref,) = take(1)
    c_refs = take(2 if last else 1)
    w0, w1, gsum, ssum, acts, fields = take(6)
    total = take(1)[0] if last else c_refs[0]
    base = 3 * first if last else 0

    for slot in range(n):
        at = pl.ds(pl.multiple_of(plan.source(me, slot) * plan.rows, plan.rows), plan.rows)
        for j in range(count):
            for m in range(3):
                top = 4 * t + m * plan.block
                part = in_refs[slot][top : top + plan.rows, j * w : (j + 1) * w]
                w1[3 * j + m, at, :] = part.astype(F32)
    for k, part in enumerate(shares):
        at = jnp.bitwise_xor(plan.member(dp), k) * plan.share
        w0[pl.ds(at, plan.share)] = part[...]

    for j in range(count):
        x, y = tokens_of(in_refs, j, 0, plan)
        sums, act, field = forward(x, y, *[w0[3 * (first + j) + m] for m in range(3)])
        for m in range(3):
            gsum[3 * j + m] = sums[m]
            fields[j, m] = field[m]
        for i, val in enumerate(act):
            acts[j, i] = val
        x, y = tokens_of(in_refs, j, 1, plan)
        sums, _, _ = forward(x, y, *[w1[3 * j + m].astype(BF16) for m in range(3)])
        for m in range(3):
            ssum[3 * j + m] = sums[m]

    grads = [gsum[m] for m in range(mats)]
    updates = [(RATE * ssum[m]).astype(BF16) for m in range(mats)]
    for m, val in enumerate(newton_pullback(grads, updates)):
        gsum[m] = val

    for j in range(count):
        x, y = tokens_of(in_refs, j, 0, plan)
        fab = jnp.concatenate([gsum[3 * j], gsum[3 * j + 1]], axis=1).astype(BF16)
        fc = gsum[3 * j + 2].astype(BF16)
        at = 3 * (first + j)
        wab = jnp.concatenate([w0[at], w0[at + 1]], axis=1)
        wc = w0[at + 2]
        cdgu = dot_nn(x, fab)
        cdg, cdu = cdgu[:, :w], cdgu[:, w:]
        ch = dot_nn(y, fc)
        g, u, p, s = [acts[j, i] for i in range(4)]
        sw, slope, curve = swish_terms(g, s)
        cg = ((ch * u + cdu * p) * slope + cdg * (p * u) * curve).astype(BF16)
        cu = (ch * sw + cdg * p * slope).astype(BF16)
        cp = (cdu * sw + cdg * u * slope).astype(BF16)
        dg, du, hidden = fields[j, 0], fields[j, 1], fields[j, 2]
        dx = dot_nt(jnp.concatenate([dg, du, cg, cu], axis=1), jnp.concatenate([fab, wab], axis=1))
        dy = dot_nt(jnp.concatenate([hidden, cp], axis=1), jnp.concatenate([fc, wc], axis=1))
        cols = slice(j * w, (j + 1) * w)
        for slot in range(n):
            to = plan.source(me, slot)
            d_ref[to, 0:t, cols] = dx[slot * t : (slot + 1) * t].astype(BF16)
            d_ref[to, t : 2 * t, cols] = dy[slot * t : (slot + 1) * t].astype(BF16)
        ab = dot_tn(x, jnp.concatenate([cg, cu], axis=1))
        grown = (ab[:, :w], ab[:, w:], dot_tn(y, cp))
        for m in range(3):
            total[base + 3 * j + m] = (ssum[3 * j + m] + grown[m]).astype(BF16)

    if last:
        total[0 : before.shape[0]] = before[...]
        for m in range(plan.mats, plan.n_dp * plan.own):
            total[m] = jnp.zeros((w, w), BF16)
        mine = plan.mine(dp)
        for r in range(plan.rest):
            to = slice(r * plan.own, (r + 1) * plan.own)
            for ref, which in zip(c_refs, (mine, plan.pair - 1 - mine)):
                ref[to] = total[pl.ds((plan.pair * r + which) * plan.own, plan.own)]


def pair_kernel(dp, keep_ref, got_ref, *refs, plan):
    outs, whole = refs[:-1], refs[-1]
    whole[...] = keep_ref[...].astype(F32) + got_ref[...].astype(F32)
    for k in range(plan.rest):
        outs[k][...] = whole[pl.ds(plan.other(dp, k) * plan.own, plan.own)].astype(BF16)


def sum_kernel(me, *refs, plan):
    parts, outs, whole = refs[: plan.rest], refs[plan.rest : -1], refs[-1]
    added = parts[0][...].astype(F32)
    for part in parts[1:]:
        added = added + part[...].astype(F32)
    whole[...] = added / plan.n_dp
    for slot in range(plan.n):
        at = pl.ds(pl.multiple_of(plan.to(me, slot) * plan.rows, plan.rows), plan.rows)
        outs[slot][...] = whole[:, at, :].astype(BF16)


def rows_kernel(me, *refs, plan):
    for slot, part in enumerate(refs[:-1]):
        refs[-1][plan.source(me, slot)] = part[...]


def rest_kernel(dp, *refs, plan):
    for k, part in enumerate(refs[:-1]):
        refs[-1][plan.other(dp, k)] = part[...]


def state_kernel(dp, *refs, plan):
    out = refs[-1]
    for k in range(plan.pair):
        for r in range(plan.rest):
            for i in range(plan.own):
                mat = (plan.pair * r + jnp.bitwise_xor(plan.mine(dp), k)) * plan.own + i

                @pl.when(mat < plan.mats)
                def _(mat=mat, ref=refs[k], r=r, i=i):
                    for c in range(plan.n):
                        head = plan.first_head(c) + lax.div(mat, 3)
                        out[lax.rem(mat, 3), head] = ref[r, c, i].astype(F32)


def unpack_kernel(*refs, plan):
    t, w = plan.tokens, plan.width
    ins, (dk, dv, sems) = refs[:-3], refs[-3:]
    copies = []
    for c, (first, count) in enumerate(plan.chunks):
        for owner in range(plan.n):
            cols = pl.ds((plan.first_head(owner) + first) * w, count * w)
            for part, dst in enumerate((dk, dv)):
                copy = pltpu.make_async_copy(
                    ins[c].at[owner, pl.ds(part * t, t), :],
                    dst.at[0, :, cols],
                    sems.at[(c * plan.n + owner) * 2 + part],
                )
                copy.start()
                copies.append(copy)
            if plan.n * plan.per != plan.heads:
                for copy in copies:
                    copy.wait()
                copies = []
    for copy in copies:
        copy.wait()


def local(keys_a, values_a, queries_b, grad_out, state_start, state_next):
    n, n_dp = lax.axis_size("ctx"), lax.axis_size("dp")
    _, heads, rows, width = state_start.shape
    t = keys_a.shape[1]
    plan = Plan(n, n_dp, t, heads, rows, width)
    per, own, chunks = plan.per, plan.own, plan.chunks
    bind = lambda kernel, **more: functools.partial(kernel, plan=plan, **more)

    me, dp = lax.axis_index("ctx").reshape(1), lax.axis_index("dp").reshape(1)

    def swap(value, k):
        if k == 0:
            return value
        return lax.ppermute(value, "dp", [(i, i ^ k) for i in range(n_dp)])

    def shift(value, s):
        if s == 0:
            return value
        return lax.ppermute(value, "ctx", [(i, (i + s) % n) for i in range(n)])

    def turn(value):
        return lax.all_to_all(value, "ctx", split_axis=0, concat_axis=0, tiled=True)

    def shape(*dims, dtype=BF16):
        return jax.ShapeDtypeStruct(dims, dtype)

    def pack(c, slots, keys):
        args = (keys, values_a, queries_b, grad_out, state_start, state_next)
        outs = call(
            bind(pack_kernel, slots=slots, chunk=c),
            [shape(plan.packed_rows(c), chunks[c][1] * width)] * len(slots),
            (me, dp, *[pltpu.with_memory_space_constraint(arg, pltpu.HBM) for arg in args]),
            [SMEM] * 2 + [HBM] * 6,
            [VMEM] * len(slots),
            f"pack{c}_{slots[0]}",
            [
                pltpu.VMEM((len(slots), 3, chunks[c][1] + (0 if c else per), rows, width), F32),
                pltpu.SemaphoreType.DMA((len(slots), 6)),
            ],
        )
        return list(outs)

    sent = pack(0, range(1, n), keys_a)
    keys, sent = lax.optimization_barrier((keys_a, sent))
    arrived = [[shift(v, s + 1) for s, v in enumerate(sent)]]
    sent = pack(1, range(1, n), keys)
    keys, sent = lax.optimization_barrier((keys_a, sent))
    arrived.append([shift(v, s + 1) for s, v in enumerate(sent)])
    arrived = [pack(c, range(1), keys) + arrived[c] for c in range(2)]
    start_own = call(
        bind(start_kernel),
        shape(plan.share, width, width),
        (me, *arrived[0]),
        [SMEM] + [VMEM] * n,
        VMEM,
        "start_share",
        [pltpu.VMEM((plan.share, width, width), F32)],
    )
    shares = [swap(start_own, k) for k in range(plan.group)]

    before = []
    grads = []
    for c, (_, count) in enumerate(chunks):
        last = c + 1 == len(chunks)
        if last:
            outs = [shape(plan.rest * own, width, width)] * 2
        else:
            outs = [shape(3 * count, width, width)]
        outs = [shape(n, 2 * t, count * width)] + outs
        scratch = [pltpu.VMEM((plan.group * plan.share, width, width), BF16)]
        scratch += [pltpu.VMEM((3 * count, width, width), F32)] * 3 + [
            pltpu.VMEM((count, 4, n * t, width), F32),
            pltpu.VMEM((count, 3, n * t, width), BF16),
        ]
        if last:
            scratch.append(pltpu.VMEM((n_dp * own, width, width), BF16))
        got = call(
            bind(chunk_kernel, chunk=c),
            outs,
            (me, dp, *arrived[c], *shares, *before),
            [SMEM] * 2 + [VMEM] * (n + plan.group + len(before)),
            [VMEM] * len(outs),
            f"chunk{c}",
            scratch,
            flops=count * 640 * 10**6,
            size=count * 10**6,
            vmem=VMEM_LARGE,
        )
        grads.append(got[0])
        before = [got[1]]
    late, early = grads
    c_keep, c_send = got[1:]
    early, c_send = lax.optimization_barrier((early, c_send))
    early = turn(early)

    halves = call(
        bind(pair_kernel),
        [shape(own, width, width)] * plan.rest,
        (dp, c_keep, swap(c_send, plan.pair - 1)),
        [SMEM] + [VMEM] * 2,
        [VMEM] * plan.rest,
        "state_pair",
        [pltpu.VMEM((plan.rest * own, width, width), F32)],
    )
    halves = [swap(halves[k], plan.pair * k) for k in range(plan.rest)]
    by_rows = call(
        bind(sum_kernel),
        [shape(own, rows, width)] * n,
        (me, *halves),
        [SMEM] + [VMEM] * plan.rest,
        [VMEM] * n,
        "state_sum",
        [pltpu.VMEM((own, width, width), F32)],
    )
    by_rows = [shift(by_rows[s], s) for s in range(n)]
    by_rows[0], early = lax.optimization_barrier((by_rows[0], early))
    mine = call(
        bind(rows_kernel),
        shape(n, own, rows, width),
        (me, *by_rows),
        [SMEM] + [VMEM] * n,
        VMEM,
        "state_rows",
    )
    mine, late = lax.optimization_barrier((mine, late))
    late = turn(late)
    rest = [swap(mine, plan.pair * k) for k in range(plan.rest)]
    half = call(
        bind(rest_kernel),
        shape(plan.rest, n, own, rows, width),
        (dp, *rest),
        [SMEM] + [VMEM] * plan.rest,
        VMEM,
        "state_rest",
    )
    both = [swap(half, k) for k in range(plan.pair)]
    grad_state = call(
        bind(state_kernel),
        shape(*state_start.shape, dtype=F32),
        (dp, *both),
        [SMEM] + [VMEM] * plan.pair,
        VMEM,
        "state_out",
    )
    grad_keys, grad_values = call(
        bind(unpack_kernel),
        [shape(*keys_a.shape), shape(*values_a.shape)],
        (late, early),
        [VMEM] * 2,
        [ANY] * 2,
        "unpack",
        [pltpu.SemaphoreType.DMA((4 * n,))],
    )
    return grad_keys, grad_values, grad_state


def solution(mesh):
    placed = (
        P("dp", "ctx", None),
        P("dp", "ctx", None),
        P("dp", "ctx", None),
        P("dp", "ctx", None),
        P(None, None, "ctx", None),
        P("dp", None, None, "ctx", None),
    )
    return jax.shard_map(
        local,
        mesh=mesh,
        in_specs=placed,
        out_specs=(P("dp", "ctx", None), P("dp", "ctx", None), P(None, None, "ctx", None)),
        check_vma=False,
    )
```
